32 devices in a mesh: shell: 16 (over z, y, x), radial: 2 (over core).
Axes of the slice: x: 2, y: 2, z: 4, core: 2. Of those that a mesh axis runs over, the one named last changes fastest.
Arguments:
- state: float32 [8, 32, 128, 128], P(None, 'radial', 'shell')
- footpoints: int32 [32, 128, 128], P('radial', 'shell'), may hold values from 0 to 32767, as said below
- conductance: float32 [4, 128, 256], P(None, 'shell', 'radial'), may hold values from 0.1 to 0.45
- inverse_blocks: float32 [128, 2, 128, 128], P('shell', 'radial')
Outputs:
- state_next: float32 [8, 32, 128, 128], P(None, 'radial', 'shell')
- potential: float32 [128, 256], P('shell', 'radial')
- footpoint_potential: float32 [32, 128, 128], P('radial', 'shell')
The draws below stay inside these ranges and needn't reach their ends.
Inputs may be any that keep to these rules, and one draw needn't show every extreme that they name: `footpoints`: A cell whose longitude index lon lies in shell block s = lon // 8 maps to a node whose column (node % 256) lies in s * 16 to (s + 1) * 16 - 1.
All inputs are finite; a program needn't handle non-finite values.
Results may differ from the reference program's by a relative error of at most 0.0003.
Values sent between devices are 32-bit elements; how exact they have to be, the bound alone decides.
No kernel may reach another device: no remote copies, remote signals or barrier semaphores. Data moves between devices by JAX's collectives and lax.ppermute only.
A program may use at most 64 MiB of HBM per device.

```python
import math
import jax
import jax.numpy as jnp
from jax import lax

LON_DEV = 8
LAT_G = 128
NLAT_I = 128
NLON_I = 256
ITERS_I = 4
R_G = 32
LON_G = 128
LON_SECT = 16
HALVES = 2
HALF = 128


GAMMA = 5.0 / 3.0


def draw_state(key, part):
    subkeys = jax.random.split(jax.random.fold_in(key, 11), 4)
    grid_shape = (R_G, LON_G, LAT_G)
    density = jnp.exp(jax.random.uniform(subkeys[0], grid_shape, jnp.float32, 0.0, math.log(2.0)))
    velocity = jnp.clip(0.3 * jax.random.normal(subkeys[1], (3,) + grid_shape, jnp.float32), -1.0, 1.0)
    magnetic = jnp.clip(0.5 * jax.random.normal(subkeys[2], (3,) + grid_shape, jnp.float32), -2.0, 2.0)
    pressure = jnp.exp(jax.random.uniform(subkeys[3], grid_shape, jnp.float32, math.log(0.5), math.log(2.0)))
    kinetic = jnp.sum(velocity * velocity, axis=0)
    field_sq = jnp.sum(magnetic * magnetic, axis=0)
    energy = pressure / (GAMMA - 1.0) + 0.5 * density * kinetic + 0.5 * field_sq
    return jnp.concatenate([density[None], density[None] * velocity, magnetic, energy[None]], axis=0)


def draw_footpoints(key, part):
    key_lat = jax.random.fold_in(key, 21)
    key_lon = jax.random.fold_in(key, 22)
    grid_shape = (R_G, LON_G, LAT_G)
    radial_cells = lax.broadcasted_iota(jnp.int32, grid_shape, 0)
    lon_cells = lax.broadcasted_iota(jnp.int32, grid_shape, 1)
    lat_cells = lax.broadcasted_iota(jnp.int32, grid_shape, 2)
    column = lon_cells // LON_DEV * LON_SECT + jax.random.randint(key_lon, grid_shape, 0, LON_SECT)
    latitude = lat_cells * NLAT_I // LAT_G + radial_cells * 3 // R_G + jax.random.randint(key_lat, grid_shape, -4, 5)
    latitude = jnp.clip(latitude, 0, NLAT_I - 1)
    node_index = latitude * NLON_I + column
    node_index = node_index.at[0, 0, 0].set(0)
    node_index = node_index.at[R_G - 1, LON_G - 1, LAT_G - 1].set(NLAT_I * NLON_I - 1)
    return node_index.astype(jnp.int32)


def draw_inverse_blocks(key, part):
    key_diag = jax.random.fold_in(key, 31)
    key_off = jax.random.fold_in(key, 32)
    block_shape = (NLAT_I, HALVES, HALF, HALF)
    diagonal = jax.random.uniform(key_diag, (NLAT_I, HALVES, HALF), jnp.float32, 0.5, 1.0)
    spread = jax.random.normal(key_off, block_shape, jnp.float32) * (0.5 / math.sqrt(HALF))
    identity = (lax.broadcasted_iota(jnp.int32, block_shape, 2) == lax.broadcasted_iota(jnp.int32, block_shape, 3)).astype(jnp.float32)
    return spread + identity * diagonal[..., None]


def block_levels(key, shape, cuts, smallest, high):
    level, own = 1.0, jax.random.fold_in(key, 6)
    for dim, parts in cuts:
        heights = jnp.exp(jax.random.uniform(jax.random.fold_in(own, dim), (parts,), jnp.float32, smallest / len(cuts), high / len(cuts)))
        level = level * jnp.repeat(heights, shape[dim] // parts).reshape([-1 if axis == dim else 1 for axis in range(len(shape))])
    return level


def setup_inputs(seed: int = 0) -> dict:
    arg_keys = jax.random.split(jax.random.key(seed), 5)
    return {
        "state": draw_state(jax.random.fold_in(arg_keys[4], 71), 0),
        "footpoints": draw_footpoints(jax.random.fold_in(arg_keys[4], 71), 0),
        "conductance": jnp.clip(jnp.exp(math.log(0.45) - 1.50407736 * jax.random.uniform(arg_keys[2], (4, NLAT_I, NLON_I), jnp.float32) ** block_levels(arg_keys[2], (4, NLAT_I, NLON_I), ((1, 16), (2, 2)), -0.2, 0.2)), 0.1, 0.45),
        "inverse_blocks": draw_inverse_blocks(jax.random.fold_in(arg_keys[4], 71), 0),
    }


GAMMA = 5.0 / 3.0
TIME_STEP = 0.02
CELL_AREA = 0.125

def minmod(first_jump, second_jump):
    return 0.5 * (jnp.sign(first_jump) + jnp.sign(second_jump)) * jnp.minimum(jnp.abs(first_jump), jnp.abs(second_jump))

def physical_flux(conserved, direction):
    density = conserved[0]
    velocity = conserved[1:4] / density
    magnetic = conserved[4:7]
    energy = conserved[7]
    field_sq = lax.optimization_barrier(jnp.sum(magnetic * magnetic, axis=0))
    kinetic = lax.optimization_barrier(jnp.sum(velocity * velocity, axis=0))
    pressure = (GAMMA - 1.0) * (energy - 0.5 * density * kinetic - 0.5 * field_sq)
    total_pressure = pressure + 0.5 * field_sq
    normal_speed = velocity[direction]
    normal_field = magnetic[direction]
    selector = (jnp.arange(3) == direction).astype(jnp.float32).reshape((3,) + (1,) * density.ndim)
    momentum_flux = density * velocity * normal_speed - magnetic * normal_field + total_pressure * selector
    induction = normal_speed * magnetic - normal_field * velocity
    alignment = lax.optimization_barrier(jnp.sum(velocity * magnetic, axis=0))
    energy_flux = (energy + total_pressure) * normal_speed - normal_field * alignment
    fluxes = jnp.concatenate([(density * normal_speed)[None], momentum_flux, induction, energy_flux[None]], axis=0)
    signal = jnp.abs(normal_speed) + jnp.sqrt((GAMMA * jnp.abs(pressure) + field_sq) / density)
    return (fluxes, signal)

def face_divergence(padded, direction):
    dimension = direction + 1
    cell_count = padded.shape[dimension] - 4

    def window_slice(array, first_index, length):
        return lax.slice_in_dim(array, first_index, first_index + length, axis=dimension)
    jumps = window_slice(padded, 1, cell_count + 3) - window_slice(padded, 0, cell_count + 3)
    slopes = minmod(window_slice(jumps, 1, cell_count + 2), window_slice(jumps, 0, cell_count + 2))
    left_state = window_slice(padded, 1, cell_count + 1) + 0.5 * window_slice(slopes, 0, cell_count + 1)
    right_state = window_slice(padded, 2, cell_count + 1) - 0.5 * window_slice(slopes, 1, cell_count + 1)
    left_flux, left_signal = physical_flux(left_state, direction)
    right_flux, right_signal = physical_flux(right_state, direction)
    signal_max = jnp.maximum(left_signal, right_signal)
    face_flux = 0.5 * (left_flux + right_flux) - 0.5 * signal_max * (right_state - left_state)
    return window_slice(face_flux, 1, cell_count) - window_slice(face_flux, 0, cell_count)

def tendency(padded):
    total_div = face_divergence(padded[:, :, 2:-2, 2:-2], 0)
    total_div = total_div + face_divergence(padded[:, 2:-2, :, 2:-2], 1)
    total_div = total_div + face_divergence(padded[:, 2:-2, 2:-2, :], 2)
    return -total_div

def shifted(values, direction, offset):
    for dimension in range(3):
        first_index = offset if dimension == direction else 2
        length = values.shape[dimension] - 4
        values = lax.slice_in_dim(values, first_index, first_index + length, axis=dimension)
    return values

def field_current(padded):
    magnetic = padded[4:7]

    def derivative(component, direction):
        return 0.5 * (shifted(magnetic[component], direction, 3) - shifted(magnetic[component], direction, 1))
    curl_first = derivative(2, 1) - derivative(1, 2)
    curl_second = derivative(0, 2) - derivative(2, 0)
    curl_third = derivative(1, 0) - derivative(0, 1)
    centre = [shifted(magnetic[component], 0, 2) for component in range(3)]
    field_sq = centre[0] * centre[0] + centre[1] * centre[1] + centre[2] * centre[2]
    aligned = curl_first * centre[0] + curl_second * centre[1] + curl_third * centre[2]
    return CELL_AREA * aligned / jnp.sqrt(1.0 + field_sq)

def extend(field, margin):
    field = jnp.pad(field, ((0, 0), (margin, margin), (0, 0), (0, 0)), mode='edge')
    field = jnp.pad(field, ((0, 0), (0, 0), (margin, margin), (0, 0)), mode='wrap')
    return jnp.pad(field, ((0, 0), (0, 0), (0, 0), (margin, margin)), mode='edge')

def reference(state, footpoints, conductance, inverse_blocks):
    first_padded = extend(state, 2)
    section_one = state + TIME_STEP * tendency(first_padded)
    state_next = 0.5 * state + 0.5 * (section_one + TIME_STEP * tendency(extend(section_one, 2)))
    cell_current = field_current(first_padded)
    currents = jax.ops.segment_sum(cell_current.reshape(-1), footpoints.reshape(-1), num_segments=NLAT_I * NLON_I)
    currents = currents.reshape(NLAT_I, NLON_I)

    def apply_blocks(vector):
        blocked = vector.reshape(NLAT_I, HALVES, HALF)
        result = jnp.einsum('rhij,rhj->rhi', inverse_blocks, blocked, precision=lax.Precision.HIGHEST)
        return result.reshape(NLAT_I, NLON_I)
    potential = jnp.zeros((NLAT_I, NLON_I), jnp.float32)
    for sweep_index in range(ITERS_I):
        padded_panel = jnp.pad(potential, 1)
        coupled = currents + conductance[0] * padded_panel[:-2, 1:-1]
        coupled = coupled + conductance[1] * padded_panel[2:, 1:-1]
        coupled = coupled + conductance[2] * padded_panel[1:-1, :-2]
        coupled = coupled + conductance[3] * padded_panel[1:-1, 2:]
        potential = apply_blocks(coupled)
    footpoint_potential = potential.reshape(-1)[footpoints]
    return (state_next, potential, footpoint_potential)
```

```python
import functools
import jax
import jax.numpy as jnp
from jax import lax
from jax.experimental import pallas as pl
from jax.experimental.pallas import tpu as pltpu
from jax.sharding import PartitionSpec as P

ITERS_I = 4
HALO = ITERS_I - 1
GAMMA = 5.0 / 3.0
TIME_STEP = 0.02
CELL_AREA = 0.125
LANES = 128
SUB = 8
PARTS = 3
VMEM_LIMIT = 40 * 1024 * 1024


def call(kernel, out_shape, name, flops=1_000_000, nbytes=1_000_000, scratch=()):
    return pl.pallas_call(
        kernel,
        out_shape=out_shape,
        scratch_shapes=list(scratch),
        compiler_params=pltpu.CompilerParams(vmem_limit_bytes=VMEM_LIMIT),
        cost_estimate=pl.CostEstimate(flops=flops, bytes_accessed=nbytes, transcendentals=0),
        name=name,
    )


def shape_of(*dims):
    return jax.ShapeDtypeStruct(dims, jnp.float32)


def lane_index(rows, width=LANES):
    return lax.broadcasted_iota(jnp.int32, (rows, width), 1)


def row_index(rows, width=LANES):
    return lax.broadcasted_iota(jnp.int32, (rows, width), 0)


def minmod(a, b):
    return jnp.maximum(jnp.minimum(a, b), 0.0) + jnp.minimum(jnp.maximum(a, b), 0.0)


def reciprocal(value):
    guess = pl.reciprocal(value, approx=True)
    return guess * (2.0 - value * guess)


def flux_and_speed(u, d):
    density, m, b, energy = u[0], u[1:4], u[4:7], u[7]
    inverse = reciprocal(density)
    v = [component * inverse for component in m]
    field_sq = b[0] * b[0] + b[1] * b[1] + b[2] * b[2]
    twice_kinetic = m[0] * v[0] + m[1] * v[1] + m[2] * v[2]
    pressure = (GAMMA - 1.0) * (energy - 0.5 * (twice_kinetic + field_sq))
    total = pressure + 0.5 * field_sq
    alignment = v[0] * b[0] + v[1] * b[1] + v[2] * b[2]
    vn, bn = v[d], b[d]
    momentum = [m[j] * vn - b[j] * bn for j in range(3)]
    momentum[d] = momentum[d] + total
    induction = [None if j == d else vn * b[j] - bn * v[j] for j in range(3)]
    flux = [m[d]] + momentum + induction + [(energy + total) * vn - bn * alignment]
    speed = jnp.abs(vn) + jnp.sqrt((GAMMA * jnp.abs(pressure) + field_sq) * inverse)
    return flux, speed


def face_flux(left, right, d):
    left_flux, left_speed = flux_and_speed(left, d)
    right_flux, right_speed = flux_and_speed(right, d)
    speed = jnp.maximum(left_speed, right_speed)
    out = []
    for k in range(8):
        jump = speed * (right[k] - left[k])
        if left_flux[k] is None:
            out.append(-0.5 * jump)
        else:
            out.append(0.5 * (left_flux[k] + right_flux[k] - jump))
    return out, left_flux


def march(load, cells, d, emit):
    before, here, after = load(-2), load(-1), load(0)
    half = [0.5 * minmod(after[k] - here[k], here[k] - before[k]) for k in range(8)]
    left = [here[k] + half[k] for k in range(8)]
    jump = [after[k] - here[k] for k in range(8)]

    def face(f, here, left, jump):
        ahead = load(f + 1)
        next_jump = [ahead[k] - here[k] for k in range(8)]
        half = [0.5 * minmod(next_jump[k], jump[k]) for k in range(8)]
        right = [here[k] - half[k] for k in range(8)]
        flux, _ = face_flux(left, right, d)
        return ahead, [here[k] + half[k] for k in range(8)], next_jump, flux

    here, left, jump, flux = face(0, after, left, jump)

    def step(f, carry):
        here, left, jump, flux = carry
        here, left, jump, new = face(f, here, left, jump)
        emit(f - 1, [new[k] - flux[k] for k in range(8)])
        return here, left, jump, new

    lax.fori_loop(1, cells + 1, step, (here, left, jump, flux), unroll=2)


def pack_halos(source, low_ref, high_ref, edge_ref, layers, position):
    for k in range(8):
        for j in range(2):
            low_ref[k, j] = source[k, pl.ds(j, layers, stride=SUB), :]
            high_ref[k, j] = source[k, pl.ds(SUB - 2 + j, layers, stride=SUB), :]
    first = jnp.where(position == 0, (layers - 2) * SUB, 0)
    first = pl.multiple_of(first, SUB)
    for k in range(8):
        edge_ref[k] = source[k, pl.ds(first, 2 * SUB), :]


def tendency_into(x_ref, low_ref, high_ref, edge_ref, xr, xl, div, layers, position, last, finish):
    cells = layers * SUB
    for k in range(8):
        xr[k, 2 * SUB : 2 * SUB + cells] = x_ref[k]
        first, final = x_ref[k, 0:SUB], x_ref[k, cells - SUB : cells]
        for j in range(2):
            rows = slice(j * SUB, (j + 1) * SUB)
            xr[k, j * SUB : (j + 1) * SUB] = jnp.where(position == 0, first, edge_ref[k, rows])
            xr[k, cells + (2 + j) * SUB : cells + (3 + j) * SUB] = jnp.where(
                position == last, final, edge_ref[k, rows]
            )
            xl[k, j * layers : (j + 1) * layers] = low_ref[k, j]
            xl[k, (SUB + 2 + j) * layers : (SUB + 3 + j) * layers] = high_ref[k, j]
        for j in range(SUB):
            xl[k, (2 + j) * layers : (3 + j) * layers] = x_ref[k, pl.ds(j, layers, stride=SUB), :]

    def load_radial(c):
        start = (c + 2) * SUB
        if not isinstance(start, int):
            start = pl.multiple_of(start, SUB)
        return [xr[k, pl.ds(start, SUB), :] for k in range(8)]

    def emit_radial(c, values):
        start = pl.multiple_of(c * SUB, SUB)
        for k in range(8):
            div[k, pl.ds(start, SUB), :] = values[k]

    march(load_radial, layers, 0, emit_radial)

    def load_lon(c):
        start = (c + 2) * layers
        if not isinstance(start, int):
            start = pl.multiple_of(start, SUB)
        return [xl[k, pl.ds(start, layers), :] for k in range(8)]

    def emit_lon(c, values):
        for k in range(8):
            rows = pl.ds(c, layers, stride=SUB)
            div[k, rows, :] = div[k, rows, :] + values[k]

    march(load_lon, SUB, 1, emit_lon)

    lane = lane_index(SUB)
    at_first, at_last = lane == 0, lane == LANES - 1

    def layer(r, carry):
        rows = pl.ds(pl.multiple_of(r * SUB, SUB), SUB)
        x = [x_ref[k, rows, :] for k in range(8)]
        left, right = [], []
        for k in range(8):
            jump = jnp.where(at_last, 0.0, pltpu.roll(x[k], LANES - 1, 1) - x[k])
            half = 0.5 * minmod(jump, pltpu.roll(jump, 1, 1))
            left.append(x[k] + half)
            down = x[k] - half
            right.append(jnp.where(at_last, down, pltpu.roll(down, LANES - 1, 1)))
        flux, left_flux = face_flux(left, right, 2)
        total = []
        for k in range(8):
            edge = 0.0 if left_flux[k] is None else left_flux[k]
            total.append(
                div[k, rows, :] + flux[k] - jnp.where(at_first, edge, pltpu.roll(flux[k], 1, 1))
            )
        finish(rows, x, total)
        return carry

    lax.fori_loop(0, layers, layer, 0, unroll=2)


def pack_kernel(layers, x_ref, low_ref, high_ref, edge_ref):
    pack_halos(x_ref, low_ref, high_ref, edge_ref, layers, lax.axis_index("radial"))


def first_stage_kernel(
    layers, x_ref, low, high, edge, out_ref, low_ref, high_ref, edge_ref, xr, xl, div
):
    position, last = lax.axis_index("radial"), lax.axis_size("radial") - 1

    def finish(rows, x, total):
        for k in range(8):
            out_ref[k, rows, :] = x[k] - TIME_STEP * total[k]

    tendency_into(x_ref, low, high, edge, xr, xl, div, layers, position, last, finish)
    pack_halos(out_ref, low_ref, high_ref, edge_ref, layers, position)


def second_stage_kernel(layers, x_ref, low, high, edge, state_ref, out_ref, xr, xl, div):
    position, last = lax.axis_index("radial"), lax.axis_size("radial") - 1

    def finish(rows, x, total):
        for k in range(8):
            out_ref[k, rows, :] = 0.5 * state_ref[k, rows, :] + 0.5 * (x[k] - TIME_STEP * total[k])

    tendency_into(x_ref, low, high, edge, xr, xl, div, layers, position, last, finish)


def log2_of(value):
    assert value & (value - 1) == 0
    return value.bit_length() - 1


def node_row_column(nodes, columns):
    return lax.shift_right_logical(nodes, log2_of(columns)), nodes & (columns - 1)


def three_parts(value):
    parts = []
    for _ in range(PARTS):
        part = value.astype(jnp.bfloat16).astype(jnp.float32)
        parts.append(part)
        value = value - part
    return parts


def current_kernel(layers, width, columns, window, x_ref, low, high, edge, nodes_ref, out_ref, held):
    position, last = lax.axis_index("radial"), lax.axis_size("radial") - 1
    first_column = lax.axis_index("shell") * width
    lane, sub = lane_index(SUB), row_index(SUB)
    groups = max(16, width)
    group_rows = row_index(groups)
    slot_rows = row_index(LANES)

    def radial_pair(k, r):
        rows = lambda c: slice(c * SUB, (c + 1) * SUB)
        if r == 0:
            below = jnp.where(position == 0, x_ref[4 + k, rows(0)], edge[4 + k, rows(1)])
        else:
            below = x_ref[4 + k, rows(r - 1)]
        if r == layers - 1:
            above = jnp.where(position == last, x_ref[4 + k, rows(r)], edge[4 + k, rows(0)])
        else:
            above = x_ref[4 + k, rows(r + 1)]
        return 0.5 * (above - below)

    def lat_pair(value):
        above = jnp.where(lane == LANES - 1, value, pltpu.roll(value, LANES - 1, 1))
        below = jnp.where(lane == 0, value, pltpu.roll(value, 1, 1))
        return 0.5 * (above - below)

    def lon_pair(k, r, value):
        above = jnp.where(sub == SUB - 1, high[4 + k, 0, r : r + 1, :], pltpu.roll(value, SUB - 1, 0))
        below = jnp.where(sub == 0, low[4 + k, 1, r : r + 1, :], pltpu.roll(value, 1, 0))
        return 0.5 * (above - below)

    total = jnp.zeros((PARTS * groups, LANES), jnp.float32)
    for r in range(layers):
        b = [x_ref[4 + k, r * SUB : (r + 1) * SUB] for k in range(3)]
        first = lon_pair(2, r, b[2]) - lat_pair(b[1])
        second = lat_pair(b[0]) - radial_pair(2, r)
        third = radial_pair(1, r) - lon_pair(0, r, b[0])
        aligned = first * b[0] + second * b[1] + third * b[2]
        field_sq = b[0] * b[0] + b[1] * b[1] + b[2] * b[2]
        current = CELL_AREA * aligned * lax.rsqrt(1.0 + field_sq)
        row, column = node_row_column(nodes_ref[r * SUB : (r + 1) * SUB], columns)
        slot = row * width + (column - first_column)
        group, place = lax.shift_right_logical(slot, 7), slot & (LANES - 1)
        parts = three_parts(current)
        lefts, rights = [], []
        for l in range(SUB):
            here = group_rows == group[l : l + 1, :]
            lefts.append(
                jnp.concatenate([jnp.where(here, part[l : l + 1, :], 0.0) for part in parts], axis=0)
            )
            rights.append(jnp.where(slot_rows == place[l : l + 1, :], 1.0, 0.0))
        left = jnp.concatenate(lefts, axis=1).astype(jnp.bfloat16)
        right = jnp.concatenate(rights, axis=1).astype(jnp.bfloat16)
        total = total + lax.dot_general(
            left, right, (((1,), (1,)), ((), ())), preferred_element_type=jnp.float32
        )
    sums = total[:groups]
    for part in range(1, PARTS):
        sums = sums + total[part * groups : (part + 1) * groups]
    if not window:
        out_ref[...] = sums[: out_ref.shape[0]]
        return
    held[...] = jnp.zeros_like(held)
    held[SUB : SUB + groups] = sums
    out_ref[...] = jnp.zeros_like(out_ref)
    for twin in range(2):
        for j in range(3):
            out_ref[pl.ds(twin * 4 + j, groups, stride=8), :] = held[SUB - 1 + j : SUB - 1 + j + groups]


def rim_kernel(blocks_ref, conductance_ref, low_ref, high_ref):
    rows = blocks_ref.shape[0]
    size = blocks_ref.shape[1]
    for ref, first in ((low_ref, 0), (high_ref, rows - HALO)):
        ref[...] = jnp.zeros_like(ref)
        for e in range(HALO):
            ref[e, :size] = blocks_ref[first + e]
            for way in range(4):
                ref[e, size + way : size + way + 1] = conductance_ref[way, first + e : first + e + 1]


def swap_blocks(tile, piece):
    sub = row_index(SUB)
    block = lax.shift_right_logical(lane_index(SUB), log2_of(piece))
    for bit in (1, 2, 4):
        up, across = (sub & bit) != 0, (block & bit) != 0
        from_below = pltpu.roll(pltpu.roll(tile, SUB - bit, 0), bit * piece, 1)
        from_above = pltpu.roll(pltpu.roll(tile, bit, 0), LANES - bit * piece, 1)
        tile = jnp.where(up == across, tile, jnp.where(up, from_above, from_below))
    return tile


def sweep_kernel(
    width,
    arrived,
    own_blocks,
    own_conductance,
    own_low,
    own_high,
    twin_blocks,
    twin_conductance,
    twin_low,
    twin_high,
    out_ref,
    send_ref,
    pot,
    rhs_ref,
    cond,
):
    position = lax.axis_index("radial")
    size = LANES
    rows = SUB
    span = 3 * SUB
    base = SUB
    halves = []
    for h in range(2):
        tiles = []
        for g in range(3):
            both = [arrived[pl.ds(h * 64 + r * 4 + g, SUB, stride=8), :] for r in range(2)]
            tiles.append(swap_blocks(both[0] + both[1], width))
        halves.append(jnp.concatenate(tiles, axis=0))
    own_currents = jnp.where(position == 0, halves[0], halves[1])
    twin_currents = jnp.where(position == 0, halves[1], halves[0])
    currents = [own_currents, twin_currents]

    cond[...] = jnp.zeros_like(cond)
    sources = ((own_conductance, own_low, own_high), (twin_conductance, twin_low, twin_high))
    for side, (mid, low, high) in enumerate(sources):
        for way in range(4):
            cond[side, way, SUB : 2 * SUB] = mid[way]
            for e in range(HALO):
                row = size + way
                cond[side, way, SUB - HALO + e : SUB - HALO + e + 1] = low[e, row : row + 1]
                cond[side, way, 2 * SUB + e : 2 * SUB + e + 1] = high[e, row : row + 1]
    pot[...] = jnp.zeros_like(pot)
    eye = row_index(size, size) == lane_index(size, size)
    blocks = ((own_blocks, own_low, own_high), (twin_blocks, twin_low, twin_high))

    def matrix(side, e):
        mid, low, high = blocks[side]
        if e < SUB:
            return low[e - (SUB - HALO), :size]
        if e < 2 * SUB:
            return mid[e - SUB]
        return high[e - 2 * SUB, :size]

    lane = lane_index(span)
    for sweep in range(ITERS_I):
        reach = ITERS_I - 1 - sweep
        sides = (0, 1) if reach else (0,)
        if sweep == 0:
            rhs = currents
        else:
            mid = [pot[side, base : base + span] for side in range(2)]
            west = [pltpu.roll(mid[side], 1, 1) for side in range(2)]
            east = [pltpu.roll(mid[side], LANES - 1, 1) for side in range(2)]
            rhs = []
            for side in sides:
                is_right = position == (1 - side)
                west_edge = jnp.where(is_right, west[1 - side], 0.0)
                east_edge = jnp.where(is_right, 0.0, east[1 - side])
                coupled = currents[side] + cond[side, 0] * pot[side, base - 1 : base - 1 + span]
                coupled = coupled + cond[side, 1] * pot[side, base + 1 : base + 1 + span]
                coupled = coupled + cond[side, 2] * jnp.where(lane == 0, west_edge, west[side])
                coupled = coupled + cond[side, 3] * jnp.where(lane == LANES - 1, east_edge, east[side])
                rhs.append(coupled)
        for side in sides:
            rhs_ref[side] = rhs[side]
        for side in sides:
            for e in range(SUB - reach, 2 * SUB + reach):
                product = matrix(side, e) * rhs_ref[side, e : e + 1]
                column = jnp.sum(product, axis=1, keepdims=True)
                line = jnp.sum(jnp.where(eye, column, 0.0), axis=0, keepdims=True)
                pot[side, base + e : base + e + 1] = line
    result = pot[0, base + SUB : base + 2 * SUB]
    out_ref[...] = result
    for d in range(send_ref.shape[0] // rows):
        send_ref[d * rows : (d + 1) * rows] = result


def gather_kernel(width, columns, direct, table_ref, nodes_ref, out_ref):
    first_column = lax.axis_index("shell") * width
    if direct:
        table = table_ref[...]
    else:
        half = lax.shift_right_logical(first_column, 7)
        strip = table_ref[:, pl.ds(half, 1), :, :]
        strip = strip.reshape(strip.shape[0] * SUB, LANES)
        pick = lane_index(width) == row_index(width) + (first_column & (LANES - 1))
        table = lax.dot_general(
            jnp.where(pick, 1.0, 0.0),
            strip,
            (((1,), (1,)), ((), ())),
            precision=lax.Precision.HIGHEST,
            preferred_element_type=jnp.float32,
        )
    lines = [jnp.broadcast_to(table[c : c + 1, :], (SUB, LANES)) for c in range(width)]
    for r in range(nodes_ref.shape[0] // SUB):
        rows = slice(r * SUB, (r + 1) * SUB)
        row, column = node_row_column(nodes_ref[rows], columns)
        column = column - first_column
        value = jnp.zeros((SUB, LANES), jnp.float32)
        for c in range(width):
            value = jnp.where(column == c, jnp.take_along_axis(lines[c], row, axis=1), value)
        out_ref[rows] = value


def ring(axis, step, periodic):
    count = lax.axis_size(axis)
    pairs = [(i, i + step) for i in range(count)]
    if periodic:
        return [(i, j % count) for i, j in pairs]
    return [(i, j) for i, j in pairs if 0 <= j < count]


def exchange_halos(low, high, edge):
    from_below = lax.ppermute(high, "shell", ring("shell", 1, True))
    from_above = lax.ppermute(low, "shell", ring("shell", -1, True))
    other = lax.ppermute(edge, "radial", [(0, 1), (1, 0)])
    return from_below, from_above, other


def padded_2(block, sides, width):
    for axis, dim in sides:
        low = lax.ppermute(
            lax.slice_in_dim(block, block.shape[dim] - width, None, axis=dim), axis, ring(axis, 1, False)
        )
        high = lax.ppermute(lax.slice_in_dim(block, 0, width, axis=dim), axis, ring(axis, -1, False))
        block = jnp.concatenate([low, block, high], axis=dim)
    return block


def general_solve(partial, conductance, blocks, rows_total, width):
    row_partials = lax.all_to_all(
        partial.reshape(rows_total, width), "shell", split_axis=0, concat_axis=1, tiled=True
    )
    currents = lax.psum_scatter(row_partials, "radial", scatter_dimension=1, tiled=True)

    def apply_blocks(vector):
        return jnp.einsum("rij,rj->ri", blocks, vector, precision=lax.Precision.HIGHEST)

    potential = apply_blocks(currents)
    for _ in range(ITERS_I - 1):
        panel = padded_2(potential, (("shell", 0), ("radial", 1)), 1)
        coupled = currents + conductance[0] * panel[:-2, 1:-1]
        coupled = coupled + conductance[1] * panel[2:, 1:-1]
        coupled = coupled + conductance[2] * panel[1:-1, :-2]
        coupled = coupled + conductance[3] * panel[1:-1, 2:]
        potential = apply_blocks(coupled)
    full_rows = lax.all_gather(potential, "radial", axis=1, tiled=True)
    strip = lax.all_to_all(full_rows, "shell", split_axis=1, concat_axis=0, tiled=True)
    return potential, strip.T


def body(state, footpoints, conductance, inverse_blocks):
    fields, layers, lons, lats = state.shape
    shells, radials = lax.axis_size("shell"), lax.axis_size("radial")
    assert (fields, lons, lats, radials) == (8, SUB, LANES, 2)
    cells = layers * SUB
    own_rows, half = conductance.shape[1:]
    assert half == LANES
    rows_total, columns = own_rows * shells, half * radials
    width = columns // shells
    x = state.reshape(fields, cells, lats)
    nodes = footpoints.reshape(cells, lats)
    blocks = inverse_blocks[:, 0]
    fast = own_rows == SUB and width * SUB == LANES

    halo_shapes = [shape_of(8, 2, layers, lats), shape_of(8, 2, layers, lats), shape_of(8, 2 * SUB, lats)]
    stage_scratch = [
        pltpu.VMEM((8, cells + 4 * SUB, lats), jnp.float32),
        pltpu.VMEM((8, (SUB + 4) * layers, lats), jnp.float32),
        pltpu.VMEM((8, cells, lats), jnp.float32),
    ]
    packed = call(functools.partial(pack_kernel, layers), halo_shapes, "pack")(x)
    below, above, other = exchange_halos(*packed)

    if fast:
        rim_shape = shape_of(HALO, half + SUB, half)
        rim_low, rim_high = call(rim_kernel, [rim_shape, rim_shape], "rim")(blocks, conductance)
        own_low = lax.ppermute(rim_high, "shell", ring("shell", 1, False))
        own_high = lax.ppermute(rim_low, "shell", ring("shell", -1, False))
        twin = [(0, 1), (1, 0)]
        twin_parts = [lax.ppermute(v, "radial", twin) for v in (blocks, conductance, own_low, own_high)]

    send_shape = shape_of(shells * radials * 4, LANES) if fast else shape_of(width, LANES)
    sums = call(
        functools.partial(current_kernel, layers, width, columns, fast),
        send_shape,
        "currents",
        flops=10_000_000,
        scratch=[pltpu.VMEM((max(16, width) + 2 * SUB, LANES), jnp.float32)],
    )(x, below, above, other, nodes)

    stage = call(
        functools.partial(first_stage_kernel, layers),
        [shape_of(fields, cells, lats)] + halo_shapes,
        "first_stage",
        flops=20_000_000,
        scratch=stage_scratch,
    )(x, below, above, other)
    section_one = stage[0]
    second_halos = exchange_halos(*stage[1:])

    if fast:
        arrived = lax.all_to_all(sums, ("shell", "radial"), split_axis=0, concat_axis=0, tiled=True)
        potential, spread = call(
            functools.partial(sweep_kernel, width),
            [shape_of(own_rows, half), shape_of(shells * radials * own_rows, half)],
            "sweeps",
            scratch=[
                pltpu.VMEM((2, 5 * SUB, half), jnp.float32),
                pltpu.VMEM((2, 3 * SUB, half), jnp.float32),
                pltpu.VMEM((2, 4, 3 * SUB, half), jnp.float32),
            ],
        )(arrived, blocks, conductance, own_low, own_high, *twin_parts)
        table = lax.all_to_all(spread, ("shell", "radial"), split_axis=0, concat_axis=0, tiled=True)
        table = table.reshape(shells, radials, own_rows, half)
    else:
        potential, table = general_solve(sums, conductance, blocks, rows_total, width)

    state_next = call(
        functools.partial(second_stage_kernel, layers),
        shape_of(fields, cells, lats),
        "second_stage",
        flops=20_000_000,
        scratch=stage_scratch,
    )(section_one, *second_halos, x)

    footpoint_potential = call(
        functools.partial(gather_kernel, width, columns, not fast), shape_of(cells, lats), "gather"
    )(table, nodes)
    return (
        state_next.reshape(state.shape),
        potential,
        footpoint_potential.reshape(footpoints.shape),
    )


def solution(mesh):
    return jax.shard_map(
        body,
        mesh=mesh,
        in_specs=(
            P(None, "radial", "shell", None),
            P("radial", "shell", None),
            P(None, "shell", "radial"),
            P("shell", "radial", None, None),
        ),
        out_specs=(
            P(None, "radial", "shell", None),
            P("shell", "radial"),
            P("radial", "shell", None),
        ),
        check_vma=False,
    )
```

```python
import functools
import jax
import jax.numpy as jnp
from jax import lax
from jax.experimental import pallas as pl
from jax.experimental.pallas import tpu as pltpu
from jax.sharding import PartitionSpec as P

ITERS_I = 4
HALO = ITERS_I - 1
GAMMA = 5.0 / 3.0
TIME_STEP = 0.02
CELL_AREA = 0.125
LANES = 128
SUB = 8
PARTS = 3
VMEM_LIMIT = 40 * 1024 * 1024
CHEAP, CURRENTS, RELAY, DEAR = 1_000, 2_000_000_000, 1_000, 10_000_000_000
IN_VMEM = pl.BlockSpec(memory_space=pltpu.VMEM)
UNREAD = pl.BlockSpec(memory_space=pl.ANY)


def call(kernel, out_shape, name, flops=CHEAP, nbytes=1_000, scratch=(), **specs):
    return pl.pallas_call(
        kernel,
        out_shape=out_shape,
        **specs,
        scratch_shapes=list(scratch),
        compiler_params=pltpu.CompilerParams(vmem_limit_bytes=VMEM_LIMIT),
        cost_estimate=pl.CostEstimate(flops=flops, bytes_accessed=nbytes, transcendentals=0),
        name=name,
    )


def shape_of(*dims):
    return jax.ShapeDtypeStruct(dims, jnp.float32)


def lane_index(rows, width=LANES):
    return lax.broadcasted_iota(jnp.int32, (rows, width), 1)


def row_index(rows, width=LANES):
    return lax.broadcasted_iota(jnp.int32, (rows, width), 0)


def minmod(a, b):
    return jnp.maximum(jnp.minimum(a, b), 0.0) + jnp.minimum(jnp.maximum(a, b), 0.0)


def reciprocal(value):
    guess = pl.reciprocal(value, approx=True)
    return guess * (2.0 - value * guess)


def flux_and_speed(u, d):
    density, m, b, energy = u[0], u[1:4], u[4:7], u[7]
    inverse = reciprocal(density)
    v = [component * inverse for component in m]
    field_sq = b[0] * b[0] + b[1] * b[1] + b[2] * b[2]
    twice_kinetic = m[0] * v[0] + m[1] * v[1] + m[2] * v[2]
    pressure = (GAMMA - 1.0) * (energy - 0.5 * (twice_kinetic + field_sq))
    total = pressure + 0.5 * field_sq
    alignment = v[0] * b[0] + v[1] * b[1] + v[2] * b[2]
    vn, bn = v[d], b[d]
    momentum = [m[j] * vn - b[j] * bn for j in range(3)]
    momentum[d] = momentum[d] + total
    induction = [None if j == d else vn * b[j] - bn * v[j] for j in range(3)]
    flux = [m[d]] + momentum + induction + [(energy + total) * vn - bn * alignment]
    speed = jnp.abs(vn) + jnp.sqrt((GAMMA * jnp.abs(pressure) + field_sq) * inverse)
    return flux, speed


def face_flux(left, right, d):
    left_flux, left_speed = flux_and_speed(left, d)
    right_flux, right_speed = flux_and_speed(right, d)
    speed = jnp.maximum(left_speed, right_speed)
    out = []
    for k in range(8):
        jump = speed * (right[k] - left[k])
        if left_flux[k] is None:
            out.append(-0.5 * jump)
        else:
            out.append(0.5 * (left_flux[k] + right_flux[k] - jump))
    return out, left_flux


def march(load, cells, d, emit):
    before, here, after = load(-2), load(-1), load(0)
    half = [0.5 * minmod(after[k] - here[k], here[k] - before[k]) for k in range(8)]
    left = [here[k] + half[k] for k in range(8)]
    jump = [after[k] - here[k] for k in range(8)]

    def face(f, here, left, jump):
        ahead = load(f + 1)
        next_jump = [ahead[k] - here[k] for k in range(8)]
        half = [0.5 * minmod(next_jump[k], jump[k]) for k in range(8)]
        right = [here[k] - half[k] for k in range(8)]
        flux, _ = face_flux(left, right, d)
        return ahead, [here[k] + half[k] for k in range(8)], next_jump, flux

    here, left, jump, flux = face(0, after, left, jump)

    def step(f, carry):
        here, left, jump, flux = carry
        here, left, jump, new = face(f, here, left, jump)
        emit(f - 1, [new[k] - flux[k] for k in range(8)])
        return here, left, jump, new

    lax.fori_loop(1, cells + 1, step, (here, left, jump, flux), unroll=2)


def parity():
    return lax.axis_index("shell") & 1


def pack_halos(source, pair_ref, next_ref, edge_ref, layers, position):
    odd = parity()
    to_pair, to_next = jnp.where(odd == 1, 0, SUB - 2), jnp.where(odd == 1, SUB - 2, 0)
    for k in range(8):
        for j in range(2):
            pair_ref[k, j] = source[k, pl.ds(to_pair + j, layers, stride=SUB), :]
            next_ref[k, j] = source[k, pl.ds(to_next + j, layers, stride=SUB), :]
    first = jnp.where(position == 0, (layers - 2) * SUB, 0)
    first = pl.multiple_of(first, SUB)
    for k in range(8):
        edge_ref[k] = source[k, pl.ds(first, 2 * SUB), :]


def tendency_into(x_ref, pair_ref, next_ref, edge_ref, xr, xl, div, layers, position, last, finish):
    cells = layers * SUB
    from_below = parity() == 1
    for k in range(8):
        xr[k, 2 * SUB : 2 * SUB + cells] = x_ref[k]
        first, final = x_ref[k, 0:SUB], x_ref[k, cells - SUB : cells]
        for j in range(2):
            rows = slice(j * SUB, (j + 1) * SUB)
            xr[k, j * SUB : (j + 1) * SUB] = jnp.where(position == 0, first, edge_ref[k, rows])
            xr[k, cells + (2 + j) * SUB : cells + (3 + j) * SUB] = jnp.where(
                position == last, final, edge_ref[k, rows]
            )
            pair, after = pair_ref[k, j], next_ref[k, j]
            xl[k, j * layers : (j + 1) * layers] = jnp.where(from_below, pair, after)
            xl[k, (SUB + 2 + j) * layers : (SUB + 3 + j) * layers] = jnp.where(from_below, after, pair)
        for j in range(SUB):
            xl[k, (2 + j) * layers : (3 + j) * layers] = x_ref[k, pl.ds(j, layers, stride=SUB), :]

    def load_radial(c):
        start = (c + 2) * SUB
        if not isinstance(start, int):
            start = pl.multiple_of(start, SUB)
        return [xr[k, pl.ds(start, SUB), :] for k in range(8)]

    def emit_radial(c, values):
        start = pl.multiple_of(c * SUB, SUB)
        for k in range(8):
            div[k, pl.ds(start, SUB), :] = values[k]

    march(load_radial, layers, 0, emit_radial)

    def load_lon(c):
        start = (c + 2) * layers
        if not isinstance(start, int):
            start = pl.multiple_of(start, SUB)
        return [xl[k, pl.ds(start, layers), :] for k in range(8)]

    def emit_lon(c, values):
        for k in range(8):
            rows = pl.ds(c, layers, stride=SUB)
            div[k, rows, :] = div[k, rows, :] + values[k]

    march(load_lon, SUB, 1, emit_lon)

    lane = lane_index(SUB)
    at_first, at_last = lane == 0, lane == LANES - 1

    def layer(r, carry):
        rows = pl.ds(pl.multiple_of(r * SUB, SUB), SUB)
        x = [x_ref[k, rows, :] for k in range(8)]
        left, right = [], []
        for k in range(8):
            jump = jnp.where(at_last, 0.0, pltpu.roll(x[k], LANES - 1, 1) - x[k])
            half = 0.5 * minmod(jump, pltpu.roll(jump, 1, 1))
            left.append(x[k] + half)
            down = x[k] - half
            right.append(jnp.where(at_last, down, pltpu.roll(down, LANES - 1, 1)))
        flux, left_flux = face_flux(left, right, 2)
        total = []
        for k in range(8):
            edge = 0.0 if left_flux[k] is None else left_flux[k]
            total.append(
                div[k, rows, :] + flux[k] - jnp.where(at_first, edge, pltpu.roll(flux[k], 1, 1))
            )
        finish(rows, x, total)
        return carry

    lax.fori_loop(0, layers, layer, 0, unroll=2)


def pack_kernel(layers, x_ref, low_ref, high_ref, edge_ref):
    pack_halos(x_ref, low_ref, high_ref, edge_ref, layers, lax.axis_index("radial"))


def relay_kernel(*refs):
    pass


def first_stage_kernel(
    layers, x_ref, low, high, edge, _, out_ref, low_ref, high_ref, edge_ref, xr, xl, div
):
    position, last = lax.axis_index("radial"), lax.axis_size("radial") - 1

    def finish(rows, x, total):
        for k in range(8):
            out_ref[k, rows, :] = x[k] - TIME_STEP * total[k]

    tendency_into(x_ref, low, high, edge, xr, xl, div, layers, position, last, finish)
    pack_halos(out_ref, low_ref, high_ref, edge_ref, layers, position)


def second_stage_kernel(layers, x_ref, low, high, edge, state_ref, _, out_ref, xr, xl, div):
    position, last = lax.axis_index("radial"), lax.axis_size("radial") - 1

    def finish(rows, x, total):
        for k in range(8):
            out_ref[k, rows, :] = 0.5 * state_ref[k, rows, :] + 0.5 * (x[k] - TIME_STEP * total[k])

    tendency_into(x_ref, low, high, edge, xr, xl, div, layers, position, last, finish)


def log2_of(value):
    assert value & (value - 1) == 0
    return value.bit_length() - 1


def node_row_column(nodes, columns):
    return lax.shift_right_logical(nodes, log2_of(columns)), nodes & (columns - 1)


def three_parts(value):
    parts = []
    for _ in range(PARTS):
        part = value.astype(jnp.bfloat16).astype(jnp.float32)
        parts.append(part)
        value = value - part
    return parts


def current_kernel(layers, width, columns, window, x_ref, pair, after, edge, nodes_ref, out_ref, held):
    from_below = parity() == 1
    below_all = [None if k == 1 else jnp.where(from_below, pair[4 + k, 1], after[4 + k, 1]) for k in range(3)]
    above_all = [None if k == 1 else jnp.where(from_below, after[4 + k, 0], pair[4 + k, 0]) for k in range(3)]
    position, last = lax.axis_index("radial"), lax.axis_size("radial") - 1
    first_column = lax.axis_index("shell") * width
    lane, sub = lane_index(SUB), row_index(SUB)
    groups = max(16, width)
    group_rows = row_index(groups)
    slot_rows = row_index(LANES)

    def radial_pair(k, r):
        rows = lambda c: slice(c * SUB, (c + 1) * SUB)
        if r == 0:
            below = jnp.where(position == 0, x_ref[4 + k, rows(0)], edge[4 + k, rows(1)])
        else:
            below = x_ref[4 + k, rows(r - 1)]
        if r == layers - 1:
            above = jnp.where(position == last, x_ref[4 + k, rows(r)], edge[4 + k, rows(0)])
        else:
            above = x_ref[4 + k, rows(r + 1)]
        return 0.5 * (above - below)

    def lat_pair(value):
        above = jnp.where(lane == LANES - 1, value, pltpu.roll(value, LANES - 1, 1))
        below = jnp.where(lane == 0, value, pltpu.roll(value, 1, 1))
        return 0.5 * (above - below)

    def lon_pair(k, r, value):
        above = jnp.where(sub == SUB - 1, above_all[k][r : r + 1, :], pltpu.roll(value, SUB - 1, 0))
        below = jnp.where(sub == 0, below_all[k][r : r + 1, :], pltpu.roll(value, 1, 0))
        return 0.5 * (above - below)

    total = jnp.zeros((PARTS * groups, LANES), jnp.float32)
    for r in range(layers):
        b = [x_ref[4 + k, r * SUB : (r + 1) * SUB] for k in range(3)]
        first = lon_pair(2, r, b[2]) - lat_pair(b[1])
        second = lat_pair(b[0]) - radial_pair(2, r)
        third = radial_pair(1, r) - lon_pair(0, r, b[0])
        aligned = first * b[0] + second * b[1] + third * b[2]
        field_sq = b[0] * b[0] + b[1] * b[1] + b[2] * b[2]
        current = CELL_AREA * aligned * lax.rsqrt(1.0 + field_sq)
        row, column = node_row_column(nodes_ref[r * SUB : (r + 1) * SUB], columns)
        slot = row * width + (column - first_column)
        group, place = lax.shift_right_logical(slot, 7), slot & (LANES - 1)
        parts = three_parts(current)
        lefts, rights = [], []
        for l in range(SUB):
            here = group_rows == group[l : l + 1, :]
            lefts.append(
                jnp.concatenate([jnp.where(here, part[l : l + 1, :], 0.0) for part in parts], axis=0)
            )
            rights.append(jnp.where(slot_rows == place[l : l + 1, :], 1.0, 0.0))
        left = jnp.concatenate(lefts, axis=1).astype(jnp.bfloat16)
        right = jnp.concatenate(rights, axis=1).astype(jnp.bfloat16)
        total = total + lax.dot_general(
            left, right, (((1,), (1,)), ((), ())), preferred_element_type=jnp.float32
        )
    sums = total[:groups]
    for part in range(1, PARTS):
        sums = sums + total[part * groups : (part + 1) * groups]
    if not window:
        out_ref[...] = sums[: out_ref.shape[0]]
        return
    held[...] = jnp.zeros_like(held)
    held[SUB : SUB + groups] = sums
    out_ref[...] = jnp.zeros_like(out_ref)
    for twin in range(2):
        for j in range(3):
            out_ref[pl.ds(twin * 4 + j, groups, stride=8), :] = held[SUB - 1 + j : SUB - 1 + j + groups]


def rim_kernel(blocks_ref, conductance_ref, _, pair_ref, next_ref):
    size = blocks_ref.shape[1]
    high = blocks_ref.shape[0] - HALO
    odd = parity()
    for ref, first in ((pair_ref, jnp.where(odd == 1, 0, high)), (next_ref, jnp.where(odd == 1, high, 0))):
        ref[...] = jnp.zeros_like(ref)
        for e in range(HALO):
            ref[e, :size] = blocks_ref[first + e]
            for way in range(4):
                ref[e, size + way : size + way + 1] = conductance_ref[way, pl.ds(first + e, 1)]


def swap_blocks(tile, piece):
    sub = row_index(SUB)
    block = lax.shift_right_logical(lane_index(SUB), log2_of(piece))
    for bit in (1, 2, 4):
        up, across = (sub & bit) != 0, (block & bit) != 0
        from_below = pltpu.roll(pltpu.roll(tile, SUB - bit, 0), bit * piece, 1)
        from_above = pltpu.roll(pltpu.roll(tile, bit, 0), LANES - bit * piece, 1)
        tile = jnp.where(up == across, tile, jnp.where(up, from_above, from_below))
    return tile


def sweep_kernel(
    width,
    arrived,
    own_blocks,
    own_conductance,
    own_pair,
    own_next,
    twin_blocks,
    twin_conductance,
    twin_pair,
    twin_next,
    _,
    out_ref,
    send_ref,
    pot,
    rhs_ref,
    cond,
):
    position = lax.axis_index("radial")
    size = LANES
    rows = SUB
    span = 3 * SUB
    base = SUB
    halves = []
    for h in range(2):
        tiles = []
        for g in range(3):
            both = [arrived[pl.ds(h * 64 + r * 4 + g, SUB, stride=8), :] for r in range(2)]
            tiles.append(swap_blocks(both[0] + both[1], width))
        halves.append(jnp.concatenate(tiles, axis=0))
    own_currents = jnp.where(position == 0, halves[0], halves[1])
    twin_currents = jnp.where(position == 0, halves[1], halves[0])
    currents = [own_currents, twin_currents]

    cond[...] = jnp.zeros_like(cond)
    odd = parity()
    rims = ((own_pair, twin_pair, odd == 1), (own_next, twin_next, odd == 0))

    def rim_rows(reach):
        for own, twin, is_low in rims:
            for i in range(reach):
                row = jnp.where(is_low, HALO - reach + i, i)
                yield own, twin, row, jnp.where(is_low, SUB - reach + i, 2 * SUB + i)

    for side, mid in enumerate((own_conductance, twin_conductance)):
        for way in range(4):
            cond[side, way, SUB : 2 * SUB] = mid[way]
    for own, twin, row, place in rim_rows(HALO):
        for side, rim in enumerate((own, twin)):
            for way in range(4):
                cond[side, way, pl.ds(place, 1)] = rim[row, size + way : size + way + 1]
    pot[...] = jnp.zeros_like(pot)
    eye = row_index(size, size) == lane_index(size, size)

    def solve_row(side, matrix, row):
        product = matrix * rhs_ref[side, pl.ds(row, 1)]
        column = jnp.sum(product, axis=1, keepdims=True)
        line = jnp.sum(jnp.where(eye, column, 0.0), axis=0, keepdims=True)
        pot[side, pl.ds(base + row, 1)] = line

    lane = lane_index(span)
    for sweep in range(ITERS_I):
        reach = ITERS_I - 1 - sweep
        sides = (0, 1) if reach else (0,)
        if sweep == 0:
            rhs = currents
        else:
            mid = [pot[side, base : base + span] for side in range(2)]
            west = [pltpu.roll(mid[side], 1, 1) for side in range(2)]
            east = [pltpu.roll(mid[side], LANES - 1, 1) for side in range(2)]
            rhs = []
            for side in sides:
                is_right = position == (1 - side)
                west_edge = jnp.where(is_right, west[1 - side], 0.0)
                east_edge = jnp.where(is_right, 0.0, east[1 - side])
                coupled = currents[side] + cond[side, 0] * pot[side, base - 1 : base - 1 + span]
                coupled = coupled + cond[side, 1] * pot[side, base + 1 : base + 1 + span]
                coupled = coupled + cond[side, 2] * jnp.where(lane == 0, west_edge, west[side])
                coupled = coupled + cond[side, 3] * jnp.where(lane == LANES - 1, east_edge, east[side])
                rhs.append(coupled)
        for side in sides:
            rhs_ref[side] = rhs[side]
        for own, twin, row, place in rim_rows(reach):
            for side, rim in enumerate((own, twin)):
                solve_row(side, rim[row, :size], place)
        for side in sides:
            for e in range(SUB):
                solve_row(side, (own_blocks, twin_blocks)[side][e], SUB + e)
    result = pot[0, base + SUB : base + 2 * SUB]
    out_ref[...] = result
    for d in range(send_ref.shape[0] // rows):
        send_ref[d * rows : (d + 1) * rows] = result


def gather_kernel(width, columns, direct, table_ref, nodes_ref, out_ref):
    first_column = lax.axis_index("shell") * width
    if direct:
        table = table_ref[...]
    else:
        half = lax.shift_right_logical(first_column, 7)
        strip = table_ref[:, pl.ds(half, 1), :, :]
        strip = strip.reshape(strip.shape[0] * SUB, LANES)
        pick = lane_index(width) == row_index(width) + (first_column & (LANES - 1))
        table = lax.dot_general(
            jnp.where(pick, 1.0, 0.0),
            strip,
            (((1,), (1,)), ((), ())),
            precision=lax.Precision.HIGHEST,
            preferred_element_type=jnp.float32,
        )
    lines = [jnp.broadcast_to(table[c : c + 1, :], (SUB, LANES)) for c in range(width)]
    for r in range(nodes_ref.shape[0] // SUB):
        rows = slice(r * SUB, (r + 1) * SUB)
        row, column = node_row_column(nodes_ref[rows], columns)
        column = column - first_column
        value = jnp.zeros((SUB, LANES), jnp.float32)
        for c in range(width):
            value = jnp.where(column == c, jnp.take_along_axis(lines[c], row, axis=1), value)
        out_ref[rows] = value


def ring(axis, step, periodic):
    count = lax.axis_size(axis)
    pairs = [(i, i + step) for i in range(count)]
    if periodic:
        return [(i, j % count) for i, j in pairs]
    return [(i, j) for i, j in pairs if 0 <= j < count]


def pairs(first, periodic):
    count = lax.axis_size("shell")
    assert count % 2 == 0
    out = []
    for i in range(first, count, 2):
        if i + 1 < count or periodic:
            j = (i + 1) % count
            out += [(i, j), (j, i)]
    return out


def exchange_halos(pair, after, edge):
    return (
        lax.ppermute(pair, "shell", pairs(0, True)),
        lax.ppermute(after, "shell", pairs(1, True)),
        lax.ppermute(edge, "radial", [(0, 1), (1, 0)]),
    )


def padded_2(block, sides, width):
    for axis, dim in sides:
        low = lax.ppermute(
            lax.slice_in_dim(block, block.shape[dim] - width, None, axis=dim), axis, ring(axis, 1, False)
        )
        high = lax.ppermute(lax.slice_in_dim(block, 0, width, axis=dim), axis, ring(axis, -1, False))
        block = jnp.concatenate([low, block, high], axis=dim)
    return block


def general_solve(partial, conductance, blocks, rows_total, width):
    row_partials = lax.all_to_all(
        partial.reshape(rows_total, width), "shell", split_axis=0, concat_axis=1, tiled=True
    )
    currents = lax.psum_scatter(row_partials, "radial", scatter_dimension=1, tiled=True)

    def apply_blocks(vector):
        return jnp.einsum("rij,rj->ri", blocks, vector, precision=lax.Precision.HIGHEST)

    potential = apply_blocks(currents)
    for _ in range(ITERS_I - 1):
        panel = padded_2(potential, (("shell", 0), ("radial", 1)), 1)
        coupled = currents + conductance[0] * panel[:-2, 1:-1]
        coupled = coupled + conductance[1] * panel[2:, 1:-1]
        coupled = coupled + conductance[2] * panel[1:-1, :-2]
        coupled = coupled + conductance[3] * panel[1:-1, 2:]
        potential = apply_blocks(coupled)
    full_rows = lax.all_gather(potential, "radial", axis=1, tiled=True)
    strip = lax.all_to_all(full_rows, "shell", split_axis=1, concat_axis=0, tiled=True)
    return potential, strip.T


def body(state, footpoints, conductance, inverse_blocks):
    fields, layers, lons, lats = state.shape
    shells, radials = lax.axis_size("shell"), lax.axis_size("radial")
    assert (fields, lons, lats, radials) == (8, SUB, LANES, 2)
    cells = layers * SUB
    own_rows, half = conductance.shape[1:]
    assert half == LANES
    rows_total, columns = own_rows * shells, half * radials
    width = columns // shells
    x = state.reshape(fields, cells, lats)
    nodes = footpoints.reshape(cells, lats)
    blocks = inverse_blocks[:, 0]
    fast = own_rows == SUB and width * SUB == LANES

    halo_shapes = [shape_of(8, 2, layers, lats), shape_of(8, 2, layers, lats), shape_of(8, 2 * SUB, lats)]
    stage_scratch = [
        pltpu.VMEM((8, cells + 4 * SUB, lats), jnp.float32),
        pltpu.VMEM((8, (SUB + 4) * layers, lats), jnp.float32),
        pltpu.VMEM((8, cells, lats), jnp.float32),
    ]
    packed = call(functools.partial(pack_kernel, layers), halo_shapes, "pack")(x)
    below, above, other = exchange_halos(*packed)

    if fast:
        rim_shape = shape_of(HALO, half + SUB, half)
        rim_pair, rim_next = call(
            rim_kernel, [rim_shape, rim_shape], "rim", in_specs=[IN_VMEM, IN_VMEM, UNREAD]
        )(blocks, conductance, packed[2])
        rims = [
            lax.ppermute(rim_pair, "shell", pairs(0, False)),
            lax.ppermute(rim_next, "shell", pairs(1, False)),
        ]

    send_shape = shape_of(shells * radials * 4, LANES) if fast else shape_of(width, LANES)
    sums = call(
        functools.partial(current_kernel, layers, width, columns, fast),
        send_shape,
        "currents",
        flops=CURRENTS,
        scratch=[pltpu.VMEM((max(16, width) + 2 * SUB, LANES), jnp.float32)],
    )(x, below, above, other, nodes)

    section_one, *packed = call(
        functools.partial(first_stage_kernel, layers),
        [shape_of(fields, cells, lats)] + halo_shapes,
        "first_stage",
        flops=DEAR,
        scratch=stage_scratch,
        in_specs=[IN_VMEM] * 4 + [UNREAD],
    )(x, below, above, other, sums)
    second_halos = exchange_halos(*packed)
    after = sums

    if fast:
        rims = call(
            relay_kernel,
            [rim_shape] * 2,
            "relay",
            flops=RELAY,
            in_specs=[UNREAD] * 3,
            out_specs=[UNREAD] * 2,
            input_output_aliases={0: 0, 1: 1},
        )(*rims, sums)
        twin = [(0, 1), (1, 0)]
        twin_parts = [lax.ppermute(v, "radial", twin) for v in (blocks, conductance, *rims)]
        arrived = lax.all_to_all(sums, ("shell", "radial"), split_axis=0, concat_axis=0, tiled=True)
        potential, spread = call(
            functools.partial(sweep_kernel, width),
            [shape_of(own_rows, half), shape_of(shells * radials * own_rows, half)],
            "sweeps",
            scratch=[
                pltpu.VMEM((2, 5 * SUB, half), jnp.float32),
                pltpu.VMEM((2, 3 * SUB, half), jnp.float32),
                pltpu.VMEM((2, 4, 3 * SUB, half), jnp.float32),
            ],
            flops=DEAR,
            in_specs=[IN_VMEM] * 9 + [UNREAD],
        )(arrived, blocks, conductance, *rims, *twin_parts, section_one)
        after = spread
        table = lax.all_to_all(spread, ("shell", "radial"), split_axis=0, concat_axis=0, tiled=True)
        table = table.reshape(shells, radials, own_rows, half)
    else:
        potential, table = general_solve(sums, conductance, blocks, rows_total, width)

    state_next = call(
        functools.partial(second_stage_kernel, layers),
        shape_of(fields, cells, lats),
        "second_stage",
        flops=DEAR,
        scratch=stage_scratch,
        in_specs=[IN_VMEM] * 5 + [UNREAD],
    )(section_one, *second_halos, x, after)

    footpoint_potential = call(
        functools.partial(gather_kernel, width, columns, not fast), shape_of(cells, lats), "gather"
    )(table, nodes)
    return (
        state_next.reshape(state.shape),
        potential,
        footpoint_potential.reshape(footpoints.shape),
    )


def solution(mesh):
    return jax.shard_map(
        body,
        mesh=mesh,
        in_specs=(
            P(None, "radial", "shell", None),
            P("radial", "shell", None),
            P(None, "shell", "radial"),
            P("shell", "radial", None, None),
        ),
        out_specs=(
            P(None, "radial", "shell", None),
            P("shell", "radial"),
            P("radial", "shell", None),
        ),
        check_vma=False,
    )
```

```python
import functools
import jax
import jax.numpy as jnp
from jax import lax
from jax.experimental import pallas as pl
from jax.experimental.pallas import tpu as pltpu
from jax.sharding import PartitionSpec as P

ITERS_I = 4
HALO = ITERS_I - 1
GAMMA = 5.0 / 3.0
TIME_STEP = 0.02
CELL_AREA = 0.125
TINY = 1e-37
LANES = 128
UNROLL = (4, 4, 8)
SUB = 8
PARTS = 3
VMEM_LIMIT = 6 * 1024 * 1024
CHEAP, CURRENTS, RELAY, DEAR = 1_000, 2_000_000_000, 1_000, 10_000_000_000
IN_VMEM = pl.BlockSpec(memory_space=pltpu.VMEM)
UNREAD = pl.BlockSpec(memory_space=pl.ANY)


def call(kernel, out_shape, name, flops=CHEAP, nbytes=1_000, scratch=(), **specs):
    return pl.pallas_call(
        kernel,
        out_shape=out_shape,
        **specs,
        scratch_shapes=list(scratch),
        compiler_params=pltpu.CompilerParams(vmem_limit_bytes=VMEM_LIMIT),
        cost_estimate=pl.CostEstimate(flops=flops, bytes_accessed=nbytes, transcendentals=0),
        name=name,
    )


def shape_of(*dims):
    return jax.ShapeDtypeStruct(dims, jnp.float32)


def lane_index(rows, width=LANES):
    return lax.broadcasted_iota(jnp.int32, (rows, width), 1)


def row_index(rows, width=LANES):
    return lax.broadcasted_iota(jnp.int32, (rows, width), 0)


def minmod(a, b):
    return jnp.maximum(jnp.minimum(a, jnp.maximum(b, 0.0)), jnp.minimum(b, 0.0))


def reciprocal(value):
    guess = pl.reciprocal(value, approx=True)
    return guess * (2.0 - value * guess)


def flux_and_speed(u, d):
    density, m, b, energy = u[0], u[1:4], u[4:7], u[7]
    inverse = reciprocal(density)
    v = [component * inverse for component in m]
    field_sq = b[0] * b[0] + b[1] * b[1] + b[2] * b[2]
    twice_kinetic = m[0] * v[0] + m[1] * v[1] + m[2] * v[2]
    pressure = (GAMMA - 1.0) * (energy - 0.5 * (twice_kinetic + field_sq))
    total = pressure + 0.5 * field_sq
    alignment = v[0] * b[0] + v[1] * b[1] + v[2] * b[2]
    vn, bn = v[d], b[d]
    momentum = [m[j] * vn - b[j] * bn for j in range(3)]
    momentum[d] = momentum[d] + total
    induction = [None if j == d else vn * b[j] - bn * v[j] for j in range(3)]
    flux = [m[d]] + momentum + induction + [(energy + total) * vn - bn * alignment]
    squared = (GAMMA * jnp.abs(pressure) + field_sq) * inverse
    speed = jnp.abs(vn) + squared * lax.rsqrt(jnp.maximum(squared, TINY))
    return flux, speed


def face_flux(left, right, d):
    left_flux, left_speed = flux_and_speed(left, d)
    right_flux, right_speed = flux_and_speed(right, d)
    speed = jnp.maximum(left_speed, right_speed)
    out = []
    for k in range(8):
        jump = speed * (right[k] - left[k])
        if left_flux[k] is None:
            out.append(-jump)
        else:
            out.append(left_flux[k] + right_flux[k] - jump)
    return out, left_flux


def march(load, cells, d, emit, unroll):
    before, here, after = load(-2), load(-1), load(0)
    half = [0.5 * minmod(after[k] - here[k], here[k] - before[k]) for k in range(8)]
    left = [here[k] + half[k] for k in range(8)]
    jump = [after[k] - here[k] for k in range(8)]

    def face(f, here, left, jump):
        ahead = load(f + 1)
        next_jump = [ahead[k] - here[k] for k in range(8)]
        half = [0.5 * minmod(next_jump[k], jump[k]) for k in range(8)]
        right = [here[k] - half[k] for k in range(8)]
        flux, _ = face_flux(left, right, d)
        return ahead, [here[k] + half[k] for k in range(8)], next_jump, flux

    here, left, jump, flux = face(0, after, left, jump)

    def step(f, carry):
        here, left, jump, flux = carry
        here, left, jump, new = face(f, here, left, jump)
        emit(f - 1, [new[k] - flux[k] for k in range(8)])
        return here, left, jump, new

    lax.fori_loop(1, cells + 1, step, (here, left, jump, flux), unroll=unroll)


def parity():
    return lax.axis_index("shell") & 1


def pack_halos(source, next_ref, pair_ref, edge_ref, layers, position):
    odd = parity()
    to_pair, to_next = jnp.where(odd == 1, 0, SUB - 2), jnp.where(odd == 1, SUB - 2, 0)
    for k in range(8):
        for j in range(2):
            pair_ref[k, j] = source[k, pl.ds(to_pair + j, layers, stride=SUB), :]
            next_ref[k, j] = source[k, pl.ds(to_next + j, layers, stride=SUB), :]
    first = jnp.where(position == 0, (layers - 2) * SUB, 0)
    first = pl.multiple_of(first, SUB)
    for k in range(8):
        edge_ref[k] = source[k, pl.ds(first, 2 * SUB), :]


def tendency_into(x_ref, next_ref, pair_ref, edge_ref, xr, xl, div, layers, position, last, finish):
    cells = layers * SUB
    from_below = parity() == 1
    for k in range(8):
        xr[k, 2 * SUB : 2 * SUB + cells] = x_ref[k]
        first, final = x_ref[k, 0:SUB], x_ref[k, cells - SUB : cells]
        for j in range(2):
            rows = slice(j * SUB, (j + 1) * SUB)
            xr[k, j * SUB : (j + 1) * SUB] = jnp.where(position == 0, first, edge_ref[k, rows])
            xr[k, cells + (2 + j) * SUB : cells + (3 + j) * SUB] = jnp.where(
                position == last, final, edge_ref[k, rows]
            )
            pair, after = pair_ref[k, j], next_ref[k, j]
            xl[k, j * layers : (j + 1) * layers] = jnp.where(from_below, pair, after)
            xl[k, (SUB + 2 + j) * layers : (SUB + 3 + j) * layers] = jnp.where(from_below, after, pair)
        for j in range(SUB):
            xl[k, (2 + j) * layers : (3 + j) * layers] = x_ref[k, pl.ds(j, layers, stride=SUB), :]

    def load_radial(c):
        start = (c + 2) * SUB
        if not isinstance(start, int):
            start = pl.multiple_of(start, SUB)
        return [xr[k, pl.ds(start, SUB), :] for k in range(8)]

    def emit_radial(c, values):
        start = pl.multiple_of(c * SUB, SUB)
        for k in range(8):
            div[k, pl.ds(start, SUB), :] = values[k]

    march(load_radial, layers, 0, emit_radial, UNROLL[0])

    def load_lon(c):
        start = (c + 2) * layers
        if not isinstance(start, int):
            start = pl.multiple_of(start, SUB)
        return [xl[k, pl.ds(start, layers), :] for k in range(8)]

    def emit_lon(c, values):
        for k in range(8):
            rows = pl.ds(c, layers, stride=SUB)
            div[k, rows, :] = div[k, rows, :] + values[k]

    march(load_lon, SUB, 1, emit_lon, UNROLL[1])

    lane = lane_index(SUB)
    at_first, at_last = lane == 0, lane == LANES - 1

    def layer(r, carry):
        rows = pl.ds(pl.multiple_of(r * SUB, SUB), SUB)
        x = [x_ref[k, rows, :] for k in range(8)]
        left, right = [], []
        for k in range(8):
            jump = jnp.where(at_last, 0.0, pltpu.roll(x[k], LANES - 1, 1) - x[k])
            half = 0.5 * minmod(jump, pltpu.roll(jump, 1, 1))
            left.append(x[k] + half)
            down = x[k] - half
            right.append(jnp.where(at_last, down, pltpu.roll(down, LANES - 1, 1)))
        flux, left_flux = face_flux(left, right, 2)
        total = []
        for k in range(8):
            edge = 0.0 if left_flux[k] is None else 2.0 * left_flux[k]
            total.append(
                div[k, rows, :] + flux[k] - jnp.where(at_first, edge, pltpu.roll(flux[k], 1, 1))
            )
        finish(rows, x, total)
        return carry

    lax.fori_loop(0, layers, layer, 0, unroll=UNROLL[2])


def pack_kernel(layers, x_ref, next_ref, pair_ref, edge_ref):
    pack_halos(x_ref, next_ref, pair_ref, edge_ref, layers, lax.axis_index("radial"))


def relay_kernel(*refs):
    pass


def first_stage_kernel(
    layers, x_ref, after, pair, edge, _, out_ref, next_ref, pair_ref, edge_ref, xr, xl, div
):
    position, last = lax.axis_index("radial"), lax.axis_size("radial") - 1

    def finish(rows, x, total):
        for k in range(8):
            out_ref[k, rows, :] = x[k] - 0.5 * TIME_STEP * total[k]

    tendency_into(x_ref, after, pair, edge, xr, xl, div, layers, position, last, finish)
    pack_halos(out_ref, next_ref, pair_ref, edge_ref, layers, position)


def second_stage_kernel(layers, x_ref, after, pair, edge, state_ref, _, out_ref, xr, xl, div):
    position, last = lax.axis_index("radial"), lax.axis_size("radial") - 1

    def finish(rows, x, total):
        for k in range(8):
            out_ref[k, rows, :] = 0.5 * state_ref[k, rows, :] + 0.5 * (x[k] - 0.5 * TIME_STEP * total[k])

    tendency_into(x_ref, after, pair, edge, xr, xl, div, layers, position, last, finish)


def log2_of(value):
    assert value & (value - 1) == 0
    return value.bit_length() - 1


def node_row_column(nodes, columns):
    return lax.shift_right_logical(nodes, log2_of(columns)), nodes & (columns - 1)


def three_parts(value):
    parts = []
    for _ in range(PARTS):
        part = value.astype(jnp.bfloat16).astype(jnp.float32)
        parts.append(part)
        value = value - part
    return parts


def current_kernel(layers, width, columns, window, x_ref, after, pair, edge, nodes_ref, out_ref, held):
    from_below = parity() == 1
    below_all = [None if k == 1 else jnp.where(from_below, pair[4 + k, 1], after[4 + k, 1]) for k in range(3)]
    above_all = [None if k == 1 else jnp.where(from_below, after[4 + k, 0], pair[4 + k, 0]) for k in range(3)]
    position, last = lax.axis_index("radial"), lax.axis_size("radial") - 1
    first_column = lax.axis_index("shell") * width
    lane, sub = lane_index(SUB), row_index(SUB)
    groups = max(16, width)
    group_rows = row_index(groups)
    slot_rows = row_index(LANES)

    def radial_pair(k, r):
        rows = lambda c: slice(c * SUB, (c + 1) * SUB)
        if r == 0:
            below = jnp.where(position == 0, x_ref[4 + k, rows(0)], edge[4 + k, rows(1)])
        else:
            below = x_ref[4 + k, rows(r - 1)]
        if r == layers - 1:
            above = jnp.where(position == last, x_ref[4 + k, rows(r)], edge[4 + k, rows(0)])
        else:
            above = x_ref[4 + k, rows(r + 1)]
        return 0.5 * (above - below)

    def lat_pair(value):
        above = jnp.where(lane == LANES - 1, value, pltpu.roll(value, LANES - 1, 1))
        below = jnp.where(lane == 0, value, pltpu.roll(value, 1, 1))
        return 0.5 * (above - below)

    def lon_pair(k, r, value):
        above = jnp.where(sub == SUB - 1, above_all[k][r : r + 1, :], pltpu.roll(value, SUB - 1, 0))
        below = jnp.where(sub == 0, below_all[k][r : r + 1, :], pltpu.roll(value, 1, 0))
        return 0.5 * (above - below)

    total = jnp.zeros((PARTS * groups, LANES), jnp.float32)
    for r in range(layers):
        b = [x_ref[4 + k, r * SUB : (r + 1) * SUB] for k in range(3)]
        first = lon_pair(2, r, b[2]) - lat_pair(b[1])
        second = lat_pair(b[0]) - radial_pair(2, r)
        third = radial_pair(1, r) - lon_pair(0, r, b[0])
        aligned = first * b[0] + second * b[1] + third * b[2]
        field_sq = b[0] * b[0] + b[1] * b[1] + b[2] * b[2]
        current = CELL_AREA * aligned * lax.rsqrt(1.0 + field_sq)
        row, column = node_row_column(nodes_ref[r * SUB : (r + 1) * SUB], columns)
        slot = row * width + (column - first_column)
        group, place = lax.shift_right_logical(slot, 7), slot & (LANES - 1)
        parts = three_parts(current)
        lefts, rights = [], []
        for l in range(SUB):
            here = group_rows == group[l : l + 1, :]
            lefts.append(
                jnp.concatenate([jnp.where(here, part[l : l + 1, :], 0.0) for part in parts], axis=0)
            )
            rights.append(jnp.where(slot_rows == place[l : l + 1, :], 1.0, 0.0))
        left = jnp.concatenate(lefts, axis=1).astype(jnp.bfloat16)
        right = jnp.concatenate(rights, axis=1).astype(jnp.bfloat16)
        total = total + lax.dot_general(
            left, right, (((1,), (1,)), ((), ())), preferred_element_type=jnp.float32
        )
    sums = total[:groups]
    for part in range(1, PARTS):
        sums = sums + total[part * groups : (part + 1) * groups]
    if not window:
        out_ref[...] = sums[: out_ref.shape[0]]
        return
    held[...] = jnp.zeros_like(held)
    held[SUB : SUB + groups] = sums
    out_ref[...] = jnp.zeros_like(out_ref)
    for twin in range(2):
        for j in range(3):
            out_ref[pl.ds(twin * 4 + j, groups, stride=8), :] = held[SUB - 1 + j : SUB - 1 + j + groups]


def rim_kernel(blocks_ref, conductance_ref, _, pair_ref, next_ref):
    size = blocks_ref.shape[1]
    high = blocks_ref.shape[0] - HALO
    odd = parity()
    for ref, first in ((pair_ref, jnp.where(odd == 1, 0, high)), (next_ref, jnp.where(odd == 1, high, 0))):
        ref[...] = jnp.zeros_like(ref)
        for e in range(HALO):
            ref[e, :size] = blocks_ref[first + e]
            for way in range(4):
                ref[e, size + way : size + way + 1] = conductance_ref[way, pl.ds(first + e, 1)]


def swap_blocks(tile, piece):
    sub = row_index(SUB)
    block = lax.shift_right_logical(lane_index(SUB), log2_of(piece))
    for bit in (1, 2, 4):
        up, across = (sub & bit) != 0, (block & bit) != 0
        from_below = pltpu.roll(pltpu.roll(tile, SUB - bit, 0), bit * piece, 1)
        from_above = pltpu.roll(pltpu.roll(tile, bit, 0), LANES - bit * piece, 1)
        tile = jnp.where(up == across, tile, jnp.where(up, from_above, from_below))
    return tile


def sweep_kernel(
    width,
    arrived,
    own_blocks,
    own_conductance,
    own_pair,
    own_next,
    twin_blocks,
    twin_conductance,
    twin_pair,
    twin_next,
    _,
    out_ref,
    send_ref,
    pot,
    rhs_ref,
    cond,
):
    position = lax.axis_index("radial")
    size = LANES
    rows = SUB
    span = 3 * SUB
    base = SUB
    halves = []
    for h in range(2):
        tiles = []
        for g in range(3):
            both = [arrived[pl.ds(h * 64 + r * 4 + g, SUB, stride=8), :] for r in range(2)]
            tiles.append(swap_blocks(both[0] + both[1], width))
        halves.append(jnp.concatenate(tiles, axis=0))
    own_currents = jnp.where(position == 0, halves[0], halves[1])
    twin_currents = jnp.where(position == 0, halves[1], halves[0])
    currents = [own_currents, twin_currents]

    cond[...] = jnp.zeros_like(cond)
    odd = parity()
    rims = ((own_pair, twin_pair, odd == 1), (own_next, twin_next, odd == 0))

    def rim_rows(reach):
        for own, twin, is_low in rims:
            for i in range(reach):
                row = jnp.where(is_low, HALO - reach + i, i)
                yield own, twin, row, jnp.where(is_low, SUB - reach + i, 2 * SUB + i)

    for side, mid in enumerate((own_conductance, twin_conductance)):
        for way in range(4):
            cond[side, way, SUB : 2 * SUB] = mid[way]
    for own, twin, row, place in rim_rows(HALO):
        for side, rim in enumerate((own, twin)):
            for way in range(4):
                cond[side, way, pl.ds(place, 1)] = rim[row, size + way : size + way + 1]
    pot[...] = jnp.zeros_like(pot)
    eye = row_index(size, size) == lane_index(size, size)

    def solve_row(side, matrix, row):
        product = matrix * rhs_ref[side, pl.ds(row, 1)]
        column = jnp.sum(product, axis=1, keepdims=True)
        line = jnp.sum(jnp.where(eye, column, 0.0), axis=0, keepdims=True)
        pot[side, pl.ds(base + row, 1)] = line

    lane = lane_index(span)
    for sweep in range(ITERS_I):
        reach = ITERS_I - 1 - sweep
        sides = (0, 1) if reach else (0,)
        if sweep == 0:
            rhs = currents
        else:
            mid = [pot[side, base : base + span] for side in range(2)]
            west = [pltpu.roll(mid[side], 1, 1) for side in range(2)]
            east = [pltpu.roll(mid[side], LANES - 1, 1) for side in range(2)]
            rhs = []
            for side in sides:
                is_right = position == (1 - side)
                west_edge = jnp.where(is_right, west[1 - side], 0.0)
                east_edge = jnp.where(is_right, 0.0, east[1 - side])
                coupled = currents[side] + cond[side, 0] * pot[side, base - 1 : base - 1 + span]
                coupled = coupled + cond[side, 1] * pot[side, base + 1 : base + 1 + span]
                coupled = coupled + cond[side, 2] * jnp.where(lane == 0, west_edge, west[side])
                coupled = coupled + cond[side, 3] * jnp.where(lane == LANES - 1, east_edge, east[side])
                rhs.append(coupled)
        for side in sides:
            rhs_ref[side] = rhs[side]
        for own, twin, row, place in rim_rows(reach):
            for side, rim in enumerate((own, twin)):
                solve_row(side, rim[row, :size], place)
        for side in sides:
            for e in range(SUB):
                solve_row(side, (own_blocks, twin_blocks)[side][e], SUB + e)
    result = pot[0, base + SUB : base + 2 * SUB]
    out_ref[...] = result
    for d in range(send_ref.shape[0] // rows):
        send_ref[d * rows : (d + 1) * rows] = result


def gather_kernel(width, columns, direct, table_ref, nodes_ref, out_ref):
    first_column = lax.axis_index("shell") * width
    if direct:
        table = table_ref[...]
    else:
        half = lax.shift_right_logical(first_column, 7)
        strip = table_ref[:, pl.ds(half, 1), :, :]
        strip = strip.reshape(strip.shape[0] * SUB, LANES)
        pick = lane_index(width) == row_index(width) + (first_column & (LANES - 1))
        table = lax.dot_general(
            jnp.where(pick, 1.0, 0.0),
            strip,
            (((1,), (1,)), ((), ())),
            precision=lax.Precision.HIGHEST,
            preferred_element_type=jnp.float32,
        )
    lines = [jnp.broadcast_to(table[c : c + 1, :], (SUB, LANES)) for c in range(width)]
    for r in range(nodes_ref.shape[0] // SUB):
        rows = slice(r * SUB, (r + 1) * SUB)
        row, column = node_row_column(nodes_ref[rows], columns)
        column = column - first_column
        value = jnp.zeros((SUB, LANES), jnp.float32)
        for c in range(width):
            value = jnp.where(column == c, jnp.take_along_axis(lines[c], row, axis=1), value)
        out_ref[rows] = value


def ring(axis, step, periodic):
    count = lax.axis_size(axis)
    pairs = [(i, i + step) for i in range(count)]
    if periodic:
        return [(i, j % count) for i, j in pairs]
    return [(i, j) for i, j in pairs if 0 <= j < count]


def pairs(first, periodic):
    count = lax.axis_size("shell")
    assert count % 2 == 0
    out = []
    for i in range(first, count, 2):
        if i + 1 < count or periodic:
            j = (i + 1) % count
            out += [(i, j), (j, i)]
    return out


def exchange_halos(after, pair, edge):
    return (
        lax.ppermute(after, "shell", pairs(1, True)),
        lax.ppermute(pair, "shell", pairs(0, True)),
        lax.ppermute(edge, "radial", [(0, 1), (1, 0)]),
    )


def padded_2(block, sides, width):
    for axis, dim in sides:
        low = lax.ppermute(
            lax.slice_in_dim(block, block.shape[dim] - width, None, axis=dim), axis, ring(axis, 1, False)
        )
        high = lax.ppermute(lax.slice_in_dim(block, 0, width, axis=dim), axis, ring(axis, -1, False))
        block = jnp.concatenate([low, block, high], axis=dim)
    return block


def general_solve(partial, conductance, blocks, rows_total, width):
    row_partials = lax.all_to_all(
        partial.reshape(rows_total, width), "shell", split_axis=0, concat_axis=1, tiled=True
    )
    currents = lax.psum_scatter(row_partials, "radial", scatter_dimension=1, tiled=True)

    def apply_blocks(vector):
        return jnp.einsum("rij,rj->ri", blocks, vector, precision=lax.Precision.HIGHEST)

    potential = apply_blocks(currents)
    for _ in range(ITERS_I - 1):
        panel = padded_2(potential, (("shell", 0), ("radial", 1)), 1)
        coupled = currents + conductance[0] * panel[:-2, 1:-1]
        coupled = coupled + conductance[1] * panel[2:, 1:-1]
        coupled = coupled + conductance[2] * panel[1:-1, :-2]
        coupled = coupled + conductance[3] * panel[1:-1, 2:]
        potential = apply_blocks(coupled)
    full_rows = lax.all_gather(potential, "radial", axis=1, tiled=True)
    strip = lax.all_to_all(full_rows, "shell", split_axis=1, concat_axis=0, tiled=True)
    return potential, strip.T


def body(state, footpoints, conductance, inverse_blocks):
    fields, layers, lons, lats = state.shape
    shells, radials = lax.axis_size("shell"), lax.axis_size("radial")
    assert (fields, lons, lats, radials) == (8, SUB, LANES, 2)
    cells = layers * SUB
    own_rows, half = conductance.shape[1:]
    assert half == LANES
    rows_total, columns = own_rows * shells, half * radials
    width = columns // shells
    x = state.reshape(fields, cells, lats)
    nodes = footpoints.reshape(cells, lats)
    blocks = inverse_blocks[:, 0]
    fast = own_rows == SUB and width * SUB == LANES

    halo_shapes = [shape_of(8, 2, layers, lats), shape_of(8, 2, layers, lats), shape_of(8, 2 * SUB, lats)]
    stage_scratch = [
        pltpu.VMEM((8, cells + 4 * SUB, lats), jnp.float32),
        pltpu.VMEM((8, (SUB + 4) * layers, lats), jnp.float32),
        pltpu.VMEM((8, cells, lats), jnp.float32),
    ]
    packed = call(functools.partial(pack_kernel, layers), halo_shapes, "pack")(x)
    halos = exchange_halos(*packed)

    if fast:
        rim_shape = shape_of(HALO, half + SUB, half)
        rim_pair, rim_next = call(
            rim_kernel, [rim_shape, rim_shape], "rim", in_specs=[IN_VMEM, IN_VMEM, UNREAD]
        )(blocks, conductance, packed[2])
        rims = [
            lax.ppermute(rim_pair, "shell", pairs(0, False)),
            lax.ppermute(rim_next, "shell", pairs(1, False)),
        ]

    send_shape = shape_of(shells * radials * 4, LANES) if fast else shape_of(width, LANES)
    sums = call(
        functools.partial(current_kernel, layers, width, columns, fast),
        send_shape,
        "currents",
        flops=CURRENTS,
        scratch=[pltpu.VMEM((max(16, width) + 2 * SUB, LANES), jnp.float32)],
    )(x, *halos, nodes)

    section_one, *packed = call(
        functools.partial(first_stage_kernel, layers),
        [shape_of(fields, cells, lats)] + halo_shapes,
        "first_stage",
        flops=DEAR,
        scratch=stage_scratch,
        in_specs=[IN_VMEM] * 4 + [UNREAD],
    )(x, *halos, sums)
    second_halos = exchange_halos(*packed)
    after = sums

    if fast:
        rims = call(
            relay_kernel,
            [rim_shape] * 2,
            "relay",
            flops=RELAY,
            in_specs=[UNREAD] * 3,
            out_specs=[UNREAD] * 2,
            input_output_aliases={0: 0, 1: 1},
        )(*rims, sums)
        twin = [(0, 1), (1, 0)]
        twin_parts = [lax.ppermute(v, "radial", twin) for v in (blocks, conductance, *rims)]
        arrived = lax.all_to_all(sums, ("shell", "radial"), split_axis=0, concat_axis=0, tiled=True)
        potential, spread = call(
            functools.partial(sweep_kernel, width),
            [shape_of(own_rows, half), shape_of(shells * radials * own_rows, half)],
            "sweeps",
            scratch=[
                pltpu.VMEM((2, 5 * SUB, half), jnp.float32),
                pltpu.VMEM((2, 3 * SUB, half), jnp.float32),
                pltpu.VMEM((2, 4, 3 * SUB, half), jnp.float32),
            ],
            flops=DEAR,
            in_specs=[IN_VMEM] * 9 + [UNREAD],
        )(arrived, blocks, conductance, *rims, *twin_parts, packed[2])
        after = spread
        table = lax.all_to_all(spread, ("shell", "radial"), split_axis=0, concat_axis=0, tiled=True)
        table = table.reshape(shells, radials, own_rows, half)
    else:
        potential, table = general_solve(sums, conductance, blocks, rows_total, width)

    state_next = call(
        functools.partial(second_stage_kernel, layers),
        shape_of(fields, cells, lats),
        "second_stage",
        flops=DEAR,
        scratch=stage_scratch,
        in_specs=[IN_VMEM] * 5 + [UNREAD],
    )(section_one, *second_halos, x, after)

    footpoint_potential = call(
        functools.partial(gather_kernel, width, columns, not fast), shape_of(cells, lats), "gather"
    )(table, nodes)
    return (
        state_next.reshape(state.shape),
        potential,
        footpoint_potential.reshape(footpoints.shape),
    )


def solution(mesh):
    return jax.shard_map(
        body,
        mesh=mesh,
        in_specs=(
            P(None, "radial", "shell", None),
            P("radial", "shell", None),
            P(None, "shell", "radial"),
            P("shell", "radial", None, None),
        ),
        out_specs=(
            P(None, "radial", "shell", None),
            P("shell", "radial"),
            P("radial", "shell", None),
        ),
        check_vma=False,
    )
```

```python
import functools
import jax
import jax.numpy as jnp
from jax import lax
from jax.experimental import pallas as pl
from jax.experimental.pallas import tpu as pltpu
from jax.sharding import PartitionSpec as P

ITERS_I = 4
HALO = ITERS_I - 1
GAMMA = 5.0 / 3.0
TIME_STEP = 0.02
CELL_AREA = 0.125
TINY = 1e-37
LANES = 128
SPLIT = 2
UNROLL = (4, 4, 8)
SUB = 8
PARTS = 3
SUM_PARTS, MXU_EVERY = 2, 2
VMEM_LIMIT = 6 * 1024 * 1024
CHEAP, CURRENTS, RELAY, DEAR = 1_000, 2_000_000_000, 1_000, 10_000_000_000
IN_HBM = pl.BlockSpec(memory_space=pltpu.HBM)
IN_VMEM = pl.BlockSpec(memory_space=pltpu.VMEM)
UNREAD = pl.BlockSpec(memory_space=pl.ANY)


def call(kernel, out_shape, name, flops=CHEAP, nbytes=1_000, scratch=(), **specs):
    return pl.pallas_call(
        kernel,
        out_shape=out_shape,
        **specs,
        scratch_shapes=list(scratch),
        compiler_params=pltpu.CompilerParams(vmem_limit_bytes=VMEM_LIMIT),
        cost_estimate=pl.CostEstimate(flops=flops, bytes_accessed=nbytes, transcendentals=0),
        name=name,
    )


def shape_of(*dims):
    return jax.ShapeDtypeStruct(dims, jnp.float32)


def lane_index(rows, width=LANES):
    return lax.broadcasted_iota(jnp.int32, (rows, width), 1)


def row_index(rows, width=LANES):
    return lax.broadcasted_iota(jnp.int32, (rows, width), 0)


class Fields:
    def __init__(self, refs):
        self.refs, self.count = refs, refs[0].shape[0]

    def __getitem__(self, index):
        k, *rest = index if isinstance(index, tuple) else (index,)
        return self.refs[k // self.count][(k % self.count, *rest)]

    def __setitem__(self, index, value):
        k, *rest = index
        self.refs[k // self.count][(k % self.count, *rest)] = value


def minmod(a, b):
    return jnp.maximum(jnp.minimum(a, jnp.maximum(b, 0.0)), jnp.minimum(b, 0.0))


def reciprocal(value):
    guess = pl.reciprocal(value, approx=True)
    return guess * (2.0 - value * guess)


def flux_and_speed(u, d):
    density, m, b, energy = u[0], u[1:4], u[4:7], u[7]
    inverse = reciprocal(density)
    v = [component * inverse for component in m]
    field_sq = b[0] * b[0] + b[1] * b[1] + b[2] * b[2]
    twice_kinetic = m[0] * v[0] + m[1] * v[1] + m[2] * v[2]
    pressure = (GAMMA - 1.0) * (energy - 0.5 * (twice_kinetic + field_sq))
    total = pressure + 0.5 * field_sq
    alignment = v[0] * b[0] + v[1] * b[1] + v[2] * b[2]
    vn, bn = v[d], b[d]
    momentum = [m[j] * vn - b[j] * bn for j in range(3)]
    momentum[d] = momentum[d] + total
    induction = [None if j == d else vn * b[j] - bn * v[j] for j in range(3)]
    flux = [m[d]] + momentum + induction + [(energy + total) * vn - bn * alignment]
    squared = (GAMMA * jnp.abs(pressure) + field_sq) * inverse
    speed = jnp.abs(vn) + squared * lax.rsqrt(jnp.maximum(squared, TINY))
    return flux, speed


def face_flux(left, right, d):
    left_flux, left_speed = flux_and_speed(left, d)
    right_flux, right_speed = flux_and_speed(right, d)
    speed = jnp.maximum(left_speed, right_speed)
    out = []
    for k in range(8):
        jump = speed * (right[k] - left[k])
        if left_flux[k] is None:
            out.append(-jump)
        else:
            out.append(left_flux[k] + right_flux[k] - jump)
    return out, left_flux


def march(load, cells, d, emit, unroll):
    before, here, after = load(-2), load(-1), load(0)
    half = [0.5 * minmod(after[k] - here[k], here[k] - before[k]) for k in range(8)]
    left = [here[k] + half[k] for k in range(8)]
    jump = [after[k] - here[k] for k in range(8)]

    def face(f, here, left, jump):
        ahead = load(f + 1)
        next_jump = [ahead[k] - here[k] for k in range(8)]
        half = [0.5 * minmod(next_jump[k], jump[k]) for k in range(8)]
        right = [here[k] - half[k] for k in range(8)]
        flux, _ = face_flux(left, right, d)
        return ahead, [here[k] + half[k] for k in range(8)], next_jump, flux

    here, left, jump, flux = face(0, after, left, jump)

    def step(f, carry):
        here, left, jump, flux = carry
        here, left, jump, new = face(f, here, left, jump)
        emit(f - 1, [new[k] - flux[k] for k in range(8)])
        return here, left, jump, new

    lax.fori_loop(1, cells + 1, step, (here, left, jump, flux), unroll=unroll)


def parity():
    return lax.axis_index("shell") & 1


def pack_halos(source, next_ref, pair_ref, edge_ref, layers, position):
    odd = parity()
    to_pair, to_next = jnp.where(odd == 1, 0, SUB - 2), jnp.where(odd == 1, SUB - 2, 0)
    for k in range(8):
        for j in range(2):
            pair_ref[k, j] = source[k, pl.ds(to_pair + j, layers, stride=SUB), :]
            next_ref[k, j] = source[k, pl.ds(to_next + j, layers, stride=SUB), :]
    first = jnp.where(position == 0, (layers - 2) * SUB, 0)
    first = pl.multiple_of(first, SUB)
    for k in range(8):
        edge_ref[k] = source[k, pl.ds(first, 2 * SUB), :]


def tendency_into(x_ref, next_ref, pair_ref, edge_ref, xr, xl, div, layers, position, last, finish):
    cells = layers * SUB
    from_below = parity() == 1
    for k in range(8):
        xr[k, 2 * SUB : 2 * SUB + cells] = x_ref[k]
        first, final = x_ref[k, 0:SUB], x_ref[k, cells - SUB : cells]
        for j in range(2):
            rows = slice(j * SUB, (j + 1) * SUB)
            xr[k, j * SUB : (j + 1) * SUB] = jnp.where(position == 0, first, edge_ref[k, rows])
            xr[k, cells + (2 + j) * SUB : cells + (3 + j) * SUB] = jnp.where(
                position == last, final, edge_ref[k, rows]
            )
            pair, after = pair_ref[k, j], next_ref[k, j]
            xl[k, j * layers : (j + 1) * layers] = jnp.where(from_below, pair, after)
            xl[k, (SUB + 2 + j) * layers : (SUB + 3 + j) * layers] = jnp.where(from_below, after, pair)
        for j in range(SUB):
            xl[k, (2 + j) * layers : (3 + j) * layers] = x_ref[k, pl.ds(j, layers, stride=SUB), :]

    def load_radial(c):
        start = (c + 2) * SUB
        if not isinstance(start, int):
            start = pl.multiple_of(start, SUB)
        return [xr[k, pl.ds(start, SUB), :] for k in range(8)]

    def emit_radial(c, values):
        start = pl.multiple_of(c * SUB, SUB)
        for k in range(8):
            div[k, pl.ds(start, SUB), :] = values[k]

    march(load_radial, layers, 0, emit_radial, UNROLL[0])

    def load_lon(c):
        start = (c + 2) * layers
        if not isinstance(start, int):
            start = pl.multiple_of(start, SUB)
        return [xl[k, pl.ds(start, layers), :] for k in range(8)]

    def emit_lon(c, values):
        for k in range(8):
            rows = pl.ds(c, layers, stride=SUB)
            div[k, rows, :] = div[k, rows, :] + values[k]

    march(load_lon, SUB, 1, emit_lon, UNROLL[1])

    lane = lane_index(SUB)
    at_first, at_last = lane == 0, lane == LANES - 1

    def layer(r, carry):
        rows = pl.ds(pl.multiple_of(r * SUB, SUB), SUB)
        x = [x_ref[k, rows, :] for k in range(8)]
        left, right = [], []
        for k in range(8):
            jump = jnp.where(at_last, 0.0, pltpu.roll(x[k], LANES - 1, 1) - x[k])
            half = 0.5 * minmod(jump, pltpu.roll(jump, 1, 1))
            left.append(x[k] + half)
            down = x[k] - half
            right.append(jnp.where(at_last, down, pltpu.roll(down, LANES - 1, 1)))
        flux, left_flux = face_flux(left, right, 2)
        total = []
        for k in range(8):
            edge = 0.0 if left_flux[k] is None else 2.0 * left_flux[k]
            total.append(
                div[k, rows, :] + flux[k] - jnp.where(at_first, edge, pltpu.roll(flux[k], 1, 1))
            )
        finish(rows, x, total)
        return carry

    lax.fori_loop(0, layers, layer, 0, unroll=UNROLL[2])


def pack_kernel(layers, x_ref, next_ref, pair_ref, edge_ref):
    pack_halos(x_ref, next_ref, pair_ref, edge_ref, layers, lax.axis_index("radial"))


def relay_kernel(*refs):
    pass


def first_stage_kernel(layers, x_ref, after, pair, edge, _, *refs):
    out_ref, (next_ref, pair_ref, edge_ref, xr, xl, div) = Fields(refs[:-6]), refs[-6:]
    position, last = lax.axis_index("radial"), lax.axis_size("radial") - 1

    def finish(rows, x, total):
        for k in range(8):
            out_ref[k, rows, :] = x[k] - 0.5 * TIME_STEP * total[k]

    tendency_into(x_ref, after, pair, edge, xr, xl, div, layers, position, last, finish)
    pack_halos(out_ref, next_ref, pair_ref, edge_ref, layers, position)


def second_stage_kernel(layers, after, pair, edge, state_ref, _, *refs):
    x_ref, (out_ref, xr, xl, div) = Fields(refs[:-4]), refs[-4:]
    position, last = lax.axis_index("radial"), lax.axis_size("radial") - 1

    def finish(rows, x, total):
        for k in range(8):
            out_ref[k, rows, :] = 0.5 * state_ref[k, rows, :] + 0.5 * (x[k] - 0.5 * TIME_STEP * total[k])

    tendency_into(x_ref, after, pair, edge, xr, xl, div, layers, position, last, finish)


def log2_of(value):
    assert value & (value - 1) == 0
    return value.bit_length() - 1


def node_row_column(nodes, columns):
    return lax.shift_right_logical(nodes, log2_of(columns)), nodes & (columns - 1)


def split(value, count):
    parts = []
    for _ in range(count):
        part = value.astype(jnp.bfloat16).astype(jnp.float32)
        parts.append(part)
        value = value - part
    return parts


def lat_pair(value):
    lane = lane_index(value.shape[0])
    above = jnp.where(lane == LANES - 1, value, pltpu.roll(value, LANES - 1, 1))
    below = jnp.where(lane == 0, value, pltpu.roll(value, 1, 1))
    return 0.5 * (above - below)


def aligned_current(b, radial, lon):
    first = lon(2) - lat_pair(b[1])
    second = lat_pair(b[0]) - radial(2)
    third = radial(1) - lon(0)
    aligned = first * b[0] + second * b[1] + third * b[2]
    field_sq = b[0] * b[0] + b[1] * b[1] + b[2] * b[2]
    return CELL_AREA * aligned * lax.rsqrt(1.0 + field_sq)


class Scatter:
    def __init__(self, width, columns):
        self.width, self.columns = width, columns
        self.first_column = lax.axis_index("shell") * width
        self.groups = max(16, width)
        self.group_rows = row_index(self.groups)
        self.slot_rows = row_index(LANES)
        self.total = jnp.zeros((PARTS * self.groups, LANES), jnp.float32)

    def add(self, values, nodes, lines):
        row, column = node_row_column(nodes, self.columns)
        slot = row * self.width + (column - self.first_column)
        group, place = lax.shift_right_logical(slot, 7), slot & (LANES - 1)
        parts = split(values, PARTS)
        lefts, rights = [], []
        for l in lines:
            here = self.group_rows == group[l : l + 1, :]
            lefts.append(
                jnp.concatenate([jnp.where(here, part[l : l + 1, :], 0.0) for part in parts], axis=0)
            )
            rights.append(jnp.where(self.slot_rows == place[l : l + 1, :], 1.0, 0.0))
        left = jnp.concatenate(lefts, axis=1).astype(jnp.bfloat16)
        right = jnp.concatenate(rights, axis=1).astype(jnp.bfloat16)
        self.total = self.total + lax.dot_general(
            left, right, (((1,), (1,)), ((), ())), preferred_element_type=jnp.float32
        )

    def sums(self):
        sums = self.total[: self.groups]
        for part in range(1, PARTS):
            sums = sums + self.total[part * self.groups : (part + 1) * self.groups]
        return sums


def inner_current_kernel(layers, width, columns, x_ref, edge, nodes_ref, _, out_ref):
    position, last = lax.axis_index("radial"), lax.axis_size("radial") - 1
    scatter = Scatter(width, columns)
    rows = lambda r: slice(r * SUB, (r + 1) * SUB)
    for r in range(layers):
        b = [x_ref[4 + k, rows(r)] for k in range(3)]

        def radial(k):
            if r == 0:
                below = jnp.where(position == 0, b[k], edge[4 + k, rows(1)])
            else:
                below = x_ref[4 + k, rows(r - 1)]
            if r == layers - 1:
                above = jnp.where(position == last, b[k], edge[4 + k, rows(0)])
            else:
                above = x_ref[4 + k, rows(r + 1)]
            return 0.5 * (above - below)

        def lon(k):
            return 0.5 * (pltpu.roll(b[k], SUB - 1, 0) - pltpu.roll(b[k], 1, 0))

        scatter.add(aligned_current(b, radial, lon), nodes_ref[rows(r)], range(1, SUB - 1))
    out_ref[...] = scatter.sums()


def outer_current_kernel(
    layers, width, columns, window, x_ref, after, pair, edge, nodes_ref, inner_ref, _, out_ref, held
):
    position, last = lax.axis_index("radial"), lax.axis_size("radial") - 1
    from_below = parity() == 1
    scatter = Scatter(width, columns)
    layer = row_index(layers)
    for l in (0, SUB - 1):
        line = lambda k, l: x_ref[4 + k, pl.ds(l, layers, stride=SUB), :]
        b = [line(k, l) for k in range(3)]

        def radial(k):
            first = jnp.where(position == 0, b[k][:1], edge[4 + k, SUB + l : SUB + l + 1])
            final = jnp.where(position == last, b[k][layers - 1 :], edge[4 + k, l : l + 1])
            below = jnp.where(layer == 0, first, pltpu.roll(b[k], 1, 0))
            above = jnp.where(layer == layers - 1, final, pltpu.roll(b[k], layers - 1, 0))
            return 0.5 * (above - below)

        def lon(k):
            if l == 0:
                return 0.5 * (line(k, 1) - jnp.where(from_below, pair[4 + k, 1], after[4 + k, 1]))
            return 0.5 * (jnp.where(from_below, after[4 + k, 0], pair[4 + k, 0]) - line(k, l - 1))

        values = aligned_current(b, radial, lon)
        nodes = nodes_ref[pl.ds(l, layers, stride=SUB), :]
        for r in range(0, layers, SUB):
            scatter.add(values[r : r + SUB], nodes[r : r + SUB], range(SUB))
    sums = inner_ref[...] + scatter.sums()
    groups = scatter.groups
    if not window:
        out_ref[...] = sums[: out_ref.shape[0]]
        return
    held[...] = jnp.zeros_like(held)
    held[SUB : SUB + groups] = sums
    out_ref[...] = jnp.zeros_like(out_ref)
    for twin in range(2):
        for j in range(3):
            out_ref[pl.ds(twin * 4 + j, groups, stride=8), :] = held[SUB - 1 + j : SUB - 1 + j + groups]


def rim_kernel(blocks_ref, conductance_ref, _, pair_ref, next_ref):
    size = blocks_ref.shape[1]
    high = blocks_ref.shape[0] - HALO
    odd = parity()
    for ref, first in ((pair_ref, jnp.where(odd == 1, 0, high)), (next_ref, jnp.where(odd == 1, high, 0))):
        for e in range(HALO):
            ref[e, :size] = blocks_ref[first + e]
            ref[e, size:] = jnp.zeros((SUB, size), jnp.float32)
            for way in range(4):
                ref[e, size + way : size + way + 1] = conductance_ref[way, pl.ds(first + e, 1)]


def swap_blocks(tile, piece):
    sub = row_index(SUB)
    block = lax.shift_right_logical(lane_index(SUB), log2_of(piece))
    for bit in (1, 2, 4):
        up, across = (sub & bit) != 0, (block & bit) != 0
        from_below = pltpu.roll(pltpu.roll(tile, SUB - bit, 0), bit * piece, 1)
        from_above = pltpu.roll(pltpu.roll(tile, bit, 0), LANES - bit * piece, 1)
        tile = jnp.where(up == across, tile, jnp.where(up, from_above, from_below))
    return tile


def sweep_kernel(
    width,
    arrived,
    own_blocks,
    own_conductance,
    own_pair,
    own_next,
    twin_blocks,
    twin_conductance,
    twin_pair,
    twin_next,
    _,
    out_ref,
    send_ref,
    pot,
    rhs_ref,
    cond,
):
    position = lax.axis_index("radial")
    size = LANES
    span = 3 * SUB
    base = SUB
    halves = []
    for h in range(2):
        tiles = []
        for g in range(3):
            both = [arrived[pl.ds(h * 64 + r * 4 + g, SUB, stride=8), :] for r in range(2)]
            tiles.append(swap_blocks(both[0] + both[1], width))
        halves.append(jnp.concatenate(tiles, axis=0))
    own_currents = jnp.where(position == 0, halves[0], halves[1])
    twin_currents = jnp.where(position == 0, halves[1], halves[0])
    currents = [own_currents, twin_currents]

    cond[...] = jnp.zeros_like(cond)
    odd = parity()
    rims = ((own_pair, twin_pair, odd == 1), (own_next, twin_next, odd == 0))

    def rim_rows(side, reach):
        for own, twin, is_low in rims:
            for i in range(reach):
                row = jnp.where(is_low, HALO - reach + i, i)
                yield (own, twin)[side], row, jnp.where(is_low, SUB - reach + i, 2 * SUB + i)

    for side, mid in enumerate((own_conductance, twin_conductance)):
        for way in range(4):
            cond[side, way, SUB : 2 * SUB] = mid[way]
    for side in range(2):
        for rim, row, place in rim_rows(side, HALO - side):
            for way in range(4):
                cond[side, way, pl.ds(place, 1)] = rim[row, size + way : size + way + 1]
    pot[...] = jnp.zeros_like(pot)
    eye = row_index(size, size) == lane_index(size, size)
    ones = jnp.ones((SUM_PARTS * size, size), jnp.bfloat16)
    turn = [0]

    def solve_row(side, matrix, row):
        product = matrix * rhs_ref[side, pl.ds(row, 1)]
        turn[0] += 1
        if turn[0] % MXU_EVERY == 0:
            parts = jnp.concatenate(split(product, SUM_PARTS), axis=1).astype(jnp.bfloat16)
            column = jnp.dot(parts, ones, preferred_element_type=jnp.float32)
        else:
            column = jnp.sum(product, axis=1, keepdims=True)
        line = jnp.sum(jnp.where(eye, column, 0.0), axis=0, keepdims=True)
        pot[side, pl.ds(base + row, 1)] = line

    lane = lane_index(span)
    for sweep in range(ITERS_I):
        reach = ITERS_I - 1 - sweep
        sides = (0, 1) if reach else (0,)
        if sweep == 0:
            rhs = currents
        else:
            mid = [pot[side, base : base + span] for side in range(2)]
            west = [pltpu.roll(mid[side], 1, 1) for side in range(2)]
            east = [pltpu.roll(mid[side], LANES - 1, 1) for side in range(2)]
            rhs = []
            for side in sides:
                is_right = position == (1 - side)
                west_edge = jnp.where(is_right, west[1 - side], 0.0)
                east_edge = jnp.where(is_right, 0.0, east[1 - side])
                coupled = currents[side] + cond[side, 0] * pot[side, base - 1 : base - 1 + span]
                coupled = coupled + cond[side, 1] * pot[side, base + 1 : base + 1 + span]
                coupled = coupled + cond[side, 2] * jnp.where(lane == 0, west_edge, west[side])
                coupled = coupled + cond[side, 3] * jnp.where(lane == LANES - 1, east_edge, east[side])
                rhs.append(coupled)
        for side in sides:
            rhs_ref[side] = rhs[side]
        for side in sides:
            for rim, row, place in rim_rows(side, reach - side):
                solve_row(side, rim[row, :size], place)
        for side in sides:
            for e in range(SUB):
                solve_row(side, (own_blocks, twin_blocks)[side][e], SUB + e)
    result = pot[0, base + SUB : base + 2 * SUB]
    out_ref[...] = result
    packed = swap_blocks(result, width)
    send_ref[...] = jnp.zeros_like(send_ref)
    for twin in range(2):
        send_ref[pl.ds(position * 2 * SUB + twin, SUB, stride=2), :] = packed


def gather_kernel(width, columns, direct, table_ref, nodes_ref, out_ref):
    first_column = lax.axis_index("shell") * width
    if direct:
        table = table_ref[...]
    else:
        half = lax.shift_right_logical(first_column, 7)
        table = table_ref[pl.ds(half, table_ref.shape[0] // 2, stride=2), :]
    lines = [jnp.broadcast_to(table[c : c + 1, :], (SUB, LANES)) for c in range(table.shape[0])]
    for r in range(nodes_ref.shape[0] // SUB):
        rows = slice(r * SUB, (r + 1) * SUB)
        row, column = node_row_column(nodes_ref[rows], columns)
        slot = row * width + (column - first_column)
        group, place = lax.shift_right_logical(slot, 7), slot & (LANES - 1)
        value = jnp.zeros((SUB, LANES), jnp.float32)
        for c, line in enumerate(lines):
            value = jnp.where(group == c, jnp.take_along_axis(line, place, axis=1), value)
        out_ref[rows] = value


def ring(axis, step, periodic):
    count = lax.axis_size(axis)
    pairs = [(i, i + step) for i in range(count)]
    if periodic:
        return [(i, j % count) for i, j in pairs]
    return [(i, j) for i, j in pairs if 0 <= j < count]


def pairs(first, periodic):
    count = lax.axis_size("shell")
    assert count % 2 == 0
    out = []
    for i in range(first, count, 2):
        if i + 1 < count or periodic:
            j = (i + 1) % count
            out += [(i, j), (j, i)]
    return out


def exchange_halos(after, pair, edge):
    return (
        lax.ppermute(after, "shell", pairs(1, True)),
        lax.ppermute(pair, "shell", pairs(0, True)),
        lax.ppermute(edge, "radial", [(0, 1), (1, 0)]),
    )


def padded_2(block, sides, width):
    for axis, dim in sides:
        low = lax.ppermute(
            lax.slice_in_dim(block, block.shape[dim] - width, None, axis=dim), axis, ring(axis, 1, False)
        )
        high = lax.ppermute(lax.slice_in_dim(block, 0, width, axis=dim), axis, ring(axis, -1, False))
        block = jnp.concatenate([low, block, high], axis=dim)
    return block


def general_solve(partial, conductance, blocks, rows_total, width):
    row_partials = lax.all_to_all(
        partial.reshape(rows_total, width), "shell", split_axis=0, concat_axis=1, tiled=True
    )
    currents = lax.psum_scatter(row_partials, "radial", scatter_dimension=1, tiled=True)

    def apply_blocks(vector):
        return jnp.einsum("rij,rj->ri", blocks, vector, precision=lax.Precision.HIGHEST)

    potential = apply_blocks(currents)
    for _ in range(ITERS_I - 1):
        panel = padded_2(potential, (("shell", 0), ("radial", 1)), 1)
        coupled = currents + conductance[0] * panel[:-2, 1:-1]
        coupled = coupled + conductance[1] * panel[2:, 1:-1]
        coupled = coupled + conductance[2] * panel[1:-1, :-2]
        coupled = coupled + conductance[3] * panel[1:-1, 2:]
        potential = apply_blocks(coupled)
    full_rows = lax.all_gather(potential, "radial", axis=1, tiled=True)
    strip = lax.all_to_all(full_rows, "shell", split_axis=1, concat_axis=0, tiled=True)
    return potential, strip.reshape(width, LANES)


def body(state, footpoints, conductance, inverse_blocks):
    fields, layers, lons, lats = state.shape
    shells, radials = lax.axis_size("shell"), lax.axis_size("radial")
    assert (fields, lons, lats, radials) == (8, SUB, LANES, 2)
    cells = layers * SUB
    own_rows, half = conductance.shape[1:]
    assert half == LANES
    rows_total, columns = own_rows * shells, half * radials
    width = columns // shells
    x = state.reshape(fields, cells, lats)
    nodes = footpoints.reshape(cells, lats)
    blocks = inverse_blocks[:, 0]
    fast = own_rows == SUB and width * SUB == LANES

    halo_shapes = [shape_of(8, 2, layers, lats), shape_of(8, 2, layers, lats), shape_of(8, 2 * SUB, lats)]
    stage_scratch = [
        pltpu.VMEM((8, cells + 4 * SUB, lats), jnp.float32),
        pltpu.VMEM((8, (SUB + 4) * layers, lats), jnp.float32),
        pltpu.VMEM((8, cells, lats), jnp.float32),
    ]
    packed = call(functools.partial(pack_kernel, layers), halo_shapes, "pack")(x)
    halos = exchange_halos(*packed)

    if fast:
        rim_shape = shape_of(HALO, half + SUB, half)
        rim_pair, rim_next = call(
            rim_kernel,
            [rim_shape, rim_shape],
            "rim",
            in_specs=[IN_VMEM, IN_VMEM, UNREAD],
        )(blocks, conductance, packed[2])
        rims = [
            lax.ppermute(rim_pair, "shell", pairs(0, False)),
            lax.ppermute(rim_next, "shell", pairs(1, False)),
        ]

    send_shape = shape_of(shells * radials * 4, LANES) if fast else shape_of(width, LANES)
    groups = max(16, width)
    inner = call(
        functools.partial(inner_current_kernel, layers, width, columns), shape_of(groups, LANES), "inner_currents",
        in_specs=[IN_VMEM] * 3 + [UNREAD],
    )(x, halos[2], nodes, blocks)
    sums = call(
        functools.partial(outer_current_kernel, layers, width, columns, fast),
        send_shape,
        "outer_currents",
        flops=CURRENTS,
        scratch=[pltpu.VMEM((groups + 2 * SUB, LANES), jnp.float32)],
        in_specs=[IN_VMEM] * 6 + [UNREAD],
    )(x, *halos, nodes, inner, blocks)

    *section_one, after, pair, edge = call(
        functools.partial(first_stage_kernel, layers),
        [shape_of(fields // SPLIT, cells, lats)] * SPLIT + halo_shapes,
        "first_stage",
        flops=DEAR,
        scratch=stage_scratch,
        in_specs=[IN_VMEM] * 4 + [UNREAD],
    )(x, *halos, sums)
    second_halos = exchange_halos(after, pair, edge)
    later = sums

    if fast:
        rims = call(
            relay_kernel,
            [rim_shape] * 2,
            "relay",
            flops=RELAY,
            in_specs=[UNREAD] * 3,
            out_specs=[UNREAD] * 2,
            input_output_aliases={0: 0, 1: 1},
        )(*rims, sums)
        twin = [(0, 1), (1, 0)]
        twin_parts = [lax.ppermute(v, "radial", twin) for v in (blocks, conductance, *rims)]
        arrived = lax.all_to_all(sums, ("shell", "radial"), split_axis=0, concat_axis=0, tiled=True)
        potential, spread = call(
            functools.partial(sweep_kernel, width),
            [shape_of(own_rows, half), shape_of(shells * radials, half)],
            "sweeps",
            scratch=[
                pltpu.VMEM((2, 5 * SUB, half), jnp.float32),
                pltpu.VMEM((2, 3 * SUB, half), jnp.float32),
                pltpu.VMEM((2, 4, 3 * SUB, half), jnp.float32),
            ],
            flops=DEAR,
            in_specs=[IN_VMEM] * 9 + [UNREAD],
        )(arrived, blocks, conductance, *rims, *twin_parts, edge)
        later = spread
        table = lax.all_to_all(spread, ("shell", "radial"), split_axis=0, concat_axis=0, tiled=True)
    else:
        potential, table = general_solve(sums, conductance, blocks, rows_total, width)

    state_next = call(
        functools.partial(second_stage_kernel, layers),
        shape_of(fields, cells, lats),
        "second_stage",
        flops=DEAR,
        scratch=stage_scratch,
        in_specs=[IN_VMEM] * 4 + [UNREAD] + [IN_VMEM] * SPLIT,
    )(*second_halos, x, later, *section_one)

    footpoint_potential = call(
        functools.partial(gather_kernel, width, columns, not fast), shape_of(cells, lats), "gather"
    )(table, nodes)
    return (
        state_next.reshape(state.shape),
        potential,
        footpoint_potential.reshape(footpoints.shape),
    )


def solution(mesh):
    return jax.shard_map(
        body,
        mesh=mesh,
        in_specs=(
            P(None, "radial", "shell", None),
            P("radial", "shell", None),
            P(None, "shell", "radial"),
            P("shell", "radial", None, None),
        ),
        out_specs=(
            P(None, "radial", "shell", None),
            P("shell", "radial"),
            P("radial", "shell", None),
        ),
        check_vma=False,
    )
```

```python
import functools
import jax
import jax.numpy as jnp
from jax import lax
from jax.experimental import pallas as pl
from jax.experimental.pallas import tpu as pltpu
from jax.sharding import PartitionSpec as P

ITERS_I = 4
HALO = ITERS_I - 1
GAMMA = 5.0 / 3.0
TIME_STEP = 0.02
CELL_AREA = 0.125
TINY = 1e-37
LANES = 128
SPLIT = 2
UNROLL = (8, 8, 8)
SUB = 8
PARTS = 3
SUM_PARTS, MXU_EVERY = 2, 3
VMEM_LIMIT = 6 * 1024 * 1024
CHEAP, CURRENTS, RELAY, DEAR = 1_000, 2_000_000_000, 1_000, 10_000_000_000
IN_HBM = pl.BlockSpec(memory_space=pltpu.HBM)
IN_VMEM = pl.BlockSpec(memory_space=pltpu.VMEM)
UNREAD = pl.BlockSpec(memory_space=pl.ANY)


def call(kernel, out_shape, name, flops=CHEAP, nbytes=1_000, scratch=(), **specs):
    return pl.pallas_call(
        kernel,
        out_shape=out_shape,
        **specs,
        scratch_shapes=list(scratch),
        compiler_params=pltpu.CompilerParams(vmem_limit_bytes=VMEM_LIMIT),
        cost_estimate=pl.CostEstimate(flops=flops, bytes_accessed=nbytes, transcendentals=0),
        name=name,
    )


def shape_of(*dims):
    return jax.ShapeDtypeStruct(dims, jnp.float32)


def lane_index(rows, width=LANES):
    return lax.broadcasted_iota(jnp.int32, (rows, width), 1)


def row_index(rows, width=LANES):
    return lax.broadcasted_iota(jnp.int32, (rows, width), 0)


class Fields:
    def __init__(self, refs):
        self.refs, self.count = refs, refs[0].shape[0]

    def __getitem__(self, index):
        k, *rest = index if isinstance(index, tuple) else (index,)
        return self.refs[k // self.count][(k % self.count, *rest)]

    def __setitem__(self, index, value):
        k, *rest = index
        self.refs[k // self.count][(k % self.count, *rest)] = value


def minmod(a, b):
    return jnp.maximum(jnp.minimum(a, jnp.maximum(b, 0.0)), jnp.minimum(b, 0.0))


def reciprocal(value):
    guess = pl.reciprocal(value, approx=True)
    return guess * (2.0 - value * guess)


def flux_and_speed(u, d):
    density, m, b, energy = u[0], u[1:4], u[4:7], u[7]
    inverse = reciprocal(density)
    v = [component * inverse for component in m]
    field_sq = b[0] * b[0] + b[1] * b[1] + b[2] * b[2]
    twice_kinetic = m[0] * v[0] + m[1] * v[1] + m[2] * v[2]
    pressure = (GAMMA - 1.0) * (energy - 0.5 * (twice_kinetic + field_sq))
    total = pressure + 0.5 * field_sq
    alignment = v[0] * b[0] + v[1] * b[1] + v[2] * b[2]
    vn, bn = v[d], b[d]
    momentum = [m[j] * vn - b[j] * bn for j in range(3)]
    momentum[d] = momentum[d] + total
    induction = [None if j == d else vn * b[j] - bn * v[j] for j in range(3)]
    flux = [m[d]] + momentum + induction + [(energy + total) * vn - bn * alignment]
    squared = (GAMMA * jnp.abs(pressure) + field_sq) * inverse
    speed = jnp.abs(vn) + squared * lax.rsqrt(jnp.maximum(squared, TINY))
    return flux, speed


def face_flux(left, right, d):
    left_flux, left_speed = flux_and_speed(left, d)
    right_flux, right_speed = flux_and_speed(right, d)
    speed = jnp.maximum(left_speed, right_speed)
    out = []
    for k in range(8):
        jump = speed * (right[k] - left[k])
        if left_flux[k] is None:
            out.append(-jump)
        else:
            out.append(left_flux[k] + right_flux[k] - jump)
    return out, left_flux


def march(load, cells, d, emit, unroll):
    before, here, after = load(-2), load(-1), load(0)
    half = [0.5 * minmod(after[k] - here[k], here[k] - before[k]) for k in range(8)]
    left = [here[k] + half[k] for k in range(8)]
    jump = [after[k] - here[k] for k in range(8)]

    def face(f, here, left, jump):
        ahead = load(f + 1)
        next_jump = [ahead[k] - here[k] for k in range(8)]
        half = [0.5 * minmod(next_jump[k], jump[k]) for k in range(8)]
        right = [here[k] - half[k] for k in range(8)]
        flux, _ = face_flux(left, right, d)
        return ahead, [here[k] + half[k] for k in range(8)], next_jump, flux

    here, left, jump, flux = face(0, after, left, jump)

    def step(f, carry):
        here, left, jump, flux = carry
        here, left, jump, new = face(f, here, left, jump)
        emit(f - 1, [new[k] - flux[k] for k in range(8)])
        return here, left, jump, new

    lax.fori_loop(1, cells + 1, step, (here, left, jump, flux), unroll=unroll)


def parity():
    return lax.axis_index("shell") & 1


def pack_halos(source, next_ref, pair_ref, edge_ref, layers, position):
    odd = parity()
    to_pair, to_next = jnp.where(odd == 1, 0, SUB - 2), jnp.where(odd == 1, SUB - 2, 0)
    for k in range(8):
        for j in range(2):
            pair_ref[k, j] = source[k, pl.ds(to_pair + j, layers, stride=SUB), :]
            next_ref[k, j] = source[k, pl.ds(to_next + j, layers, stride=SUB), :]
    first = jnp.where(position == 0, (layers - 2) * SUB, 0)
    first = pl.multiple_of(first, SUB)
    for k in range(8):
        edge_ref[k] = source[k, pl.ds(first, 2 * SUB), :]


def tendency_into(x_ref, next_ref, pair_ref, edge_ref, xr, xl, div, lon_div, layers, position, last, finish):
    cells = layers * SUB
    from_below = parity() == 1
    for k in range(8):
        xr[k, 2 * SUB : 2 * SUB + cells] = x_ref[k]
        first, final = x_ref[k, 0:SUB], x_ref[k, cells - SUB : cells]
        for j in range(2):
            rows = slice(j * SUB, (j + 1) * SUB)
            xr[k, j * SUB : (j + 1) * SUB] = jnp.where(position == 0, first, edge_ref[k, rows])
            xr[k, cells + (2 + j) * SUB : cells + (3 + j) * SUB] = jnp.where(
                position == last, final, edge_ref[k, rows]
            )
            pair, after = pair_ref[k, j], next_ref[k, j]
            xl[k, j * layers : (j + 1) * layers] = jnp.where(from_below, pair, after)
            xl[k, (SUB + 2 + j) * layers : (SUB + 3 + j) * layers] = jnp.where(from_below, after, pair)
        for j in range(SUB):
            xl[k, (2 + j) * layers : (3 + j) * layers] = x_ref[k, pl.ds(j, layers, stride=SUB), :]

    def load_radial(c):
        start = (c + 2) * SUB
        if not isinstance(start, int):
            start = pl.multiple_of(start, SUB)
        return [xr[k, pl.ds(start, SUB), :] for k in range(8)]

    def emit_radial(c, values):
        start = pl.multiple_of(c * SUB, SUB)
        for k in range(8):
            div[k, pl.ds(start, SUB), :] = values[k]

    march(load_radial, layers, 0, emit_radial, UNROLL[0])

    def load_lon(c):
        start = (c + 2) * layers
        if not isinstance(start, int):
            start = pl.multiple_of(start, SUB)
        return [xl[k, pl.ds(start, layers), :] for k in range(8)]

    def emit_lon(c, values):
        start = pl.multiple_of(c * layers, SUB)
        for k in range(8):
            lon_div[k, pl.ds(start, layers), :] = values[k]

    march(load_lon, SUB, 1, emit_lon, UNROLL[1])

    lane = lane_index(SUB)
    at_first, at_last = lane == 0, lane == LANES - 1
    half_inside = jnp.where(at_first | at_last, 0.0, 0.5)

    def layer(r, carry):
        rows = pl.ds(pl.multiple_of(r * SUB, SUB), SUB)
        x = [x_ref[k, rows, :] for k in range(8)]
        left, right = [], []
        for k in range(8):
            jump = pltpu.roll(x[k], LANES - 1, 1) - x[k]
            half = half_inside * minmod(jump, pltpu.roll(jump, 1, 1))
            left.append(x[k] + half)
            down = x[k] - half
            right.append(jnp.where(at_last, down, pltpu.roll(down, LANES - 1, 1)))
        flux, left_flux = face_flux(left, right, 2)
        total = []
        for k in range(8):
            edge = 0.0 if left_flux[k] is None else 2.0 * left_flux[k]
            aside = div[k, rows, :] + lon_div[k, pl.ds(r, SUB, stride=layers), :]
            total.append(
                aside + flux[k] - jnp.where(at_first, edge, pltpu.roll(flux[k], 1, 1))
            )
        finish(rows, x, total)
        return carry

    lax.fori_loop(0, layers, layer, 0, unroll=UNROLL[2])


def pack_kernel(layers, x_ref, next_ref, pair_ref, edge_ref):
    pack_halos(x_ref, next_ref, pair_ref, edge_ref, layers, lax.axis_index("radial"))


def relay_kernel(*refs):
    pass


def first_stage_kernel(layers, x_ref, after, pair, edge, _, *refs):
    out_ref, (next_ref, pair_ref, edge_ref, xr, xl, div, lon_div) = Fields(refs[:-7]), refs[-7:]
    position, last = lax.axis_index("radial"), lax.axis_size("radial") - 1

    def finish(rows, x, total):
        for k in range(8):
            out_ref[k, rows, :] = x[k] - 0.5 * TIME_STEP * total[k]

    tendency_into(x_ref, after, pair, edge, xr, xl, div, lon_div, layers, position, last, finish)
    pack_halos(out_ref, next_ref, pair_ref, edge_ref, layers, position)


def second_stage_kernel(layers, after, pair, edge, state_ref, _, *refs):
    x_ref, (out_ref, xr, xl, div, lon_div) = Fields(refs[:-5]), refs[-5:]
    position, last = lax.axis_index("radial"), lax.axis_size("radial") - 1

    def finish(rows, x, total):
        for k in range(8):
            out_ref[k, rows, :] = 0.5 * state_ref[k, rows, :] + 0.5 * (x[k] - 0.5 * TIME_STEP * total[k])

    tendency_into(x_ref, after, pair, edge, xr, xl, div, lon_div, layers, position, last, finish)


def log2_of(value):
    assert value & (value - 1) == 0
    return value.bit_length() - 1


def node_row_column(nodes, columns):
    return lax.shift_right_logical(nodes, log2_of(columns)), nodes & (columns - 1)


def split(value, count):
    parts = []
    for _ in range(count):
        part = value.astype(jnp.bfloat16).astype(jnp.float32)
        parts.append(part)
        value = value - part
    return parts


def lat_pair(value):
    lane = lane_index(value.shape[0])
    above = jnp.where(lane == LANES - 1, value, pltpu.roll(value, LANES - 1, 1))
    below = jnp.where(lane == 0, value, pltpu.roll(value, 1, 1))
    return 0.5 * (above - below)


def aligned_current(b, radial, lon):
    first = lon(2) - lat_pair(b[1])
    second = lat_pair(b[0]) - radial(2)
    third = radial(1) - lon(0)
    aligned = first * b[0] + second * b[1] + third * b[2]
    field_sq = b[0] * b[0] + b[1] * b[1] + b[2] * b[2]
    return CELL_AREA * aligned * lax.rsqrt(1.0 + field_sq)


class Scatter:
    def __init__(self, width, columns):
        self.width, self.columns = width, columns
        self.first_column = lax.axis_index("shell") * width
        self.groups = max(16, width)
        self.group_rows = row_index(self.groups)
        self.slot_rows = row_index(LANES)
        self.total = jnp.zeros((PARTS * self.groups, LANES), jnp.float32)

    def add(self, values, nodes, lines):
        row, column = node_row_column(nodes, self.columns)
        slot = row * self.width + (column - self.first_column)
        group, place = lax.shift_right_logical(slot, 7), slot & (LANES - 1)
        parts = split(values, PARTS)
        lefts, rights = [], []
        for l in lines:
            here = self.group_rows == group[l : l + 1, :]
            lefts.append(
                jnp.concatenate([jnp.where(here, part[l : l + 1, :], 0.0) for part in parts], axis=0)
            )
            rights.append(jnp.where(self.slot_rows == place[l : l + 1, :], 1.0, 0.0))
        left = jnp.concatenate(lefts, axis=1).astype(jnp.bfloat16)
        right = jnp.concatenate(rights, axis=1).astype(jnp.bfloat16)
        self.total = self.total + lax.dot_general(
            left, right, (((1,), (1,)), ((), ())), preferred_element_type=jnp.float32
        )

    def sums(self):
        sums = self.total[: self.groups]
        for part in range(1, PARTS):
            sums = sums + self.total[part * self.groups : (part + 1) * self.groups]
        return sums


def inner_current_kernel(layers, width, columns, x_ref, edge, nodes_ref, _, out_ref):
    position, last = lax.axis_index("radial"), lax.axis_size("radial") - 1
    scatter = Scatter(width, columns)
    rows = lambda r: slice(r * SUB, (r + 1) * SUB)
    for r in range(layers):
        b = [x_ref[4 + k, rows(r)] for k in range(3)]

        def radial(k):
            if r == 0:
                below = jnp.where(position == 0, b[k], edge[4 + k, rows(1)])
            else:
                below = x_ref[4 + k, rows(r - 1)]
            if r == layers - 1:
                above = jnp.where(position == last, b[k], edge[4 + k, rows(0)])
            else:
                above = x_ref[4 + k, rows(r + 1)]
            return 0.5 * (above - below)

        def lon(k):
            return 0.5 * (pltpu.roll(b[k], SUB - 1, 0) - pltpu.roll(b[k], 1, 0))

        scatter.add(aligned_current(b, radial, lon), nodes_ref[rows(r)], range(1, SUB - 1))
    out_ref[...] = scatter.sums()


def outer_current_kernel(
    layers, width, columns, window, x_ref, after, pair, edge, nodes_ref, inner_ref, _, out_ref, held
):
    position, last = lax.axis_index("radial"), lax.axis_size("radial") - 1
    from_below = parity() == 1
    scatter = Scatter(width, columns)
    layer = row_index(layers)
    for l in (0, SUB - 1):
        line = lambda k, l: x_ref[4 + k, pl.ds(l, layers, stride=SUB), :]
        b = [line(k, l) for k in range(3)]

        def radial(k):
            first = jnp.where(position == 0, b[k][:1], edge[4 + k, SUB + l : SUB + l + 1])
            final = jnp.where(position == last, b[k][layers - 1 :], edge[4 + k, l : l + 1])
            below = jnp.where(layer == 0, first, pltpu.roll(b[k], 1, 0))
            above = jnp.where(layer == layers - 1, final, pltpu.roll(b[k], layers - 1, 0))
            return 0.5 * (above - below)

        def lon(k):
            if l == 0:
                return 0.5 * (line(k, 1) - jnp.where(from_below, pair[4 + k, 1], after[4 + k, 1]))
            return 0.5 * (jnp.where(from_below, after[4 + k, 0], pair[4 + k, 0]) - line(k, l - 1))

        values = aligned_current(b, radial, lon)
        nodes = nodes_ref[pl.ds(l, layers, stride=SUB), :]
        for r in range(0, layers, SUB):
            scatter.add(values[r : r + SUB], nodes[r : r + SUB], range(SUB))
    sums = inner_ref[...] + scatter.sums()
    groups = scatter.groups
    if not window:
        out_ref[...] = sums[: out_ref.shape[0]]
        return
    held[...] = jnp.zeros_like(held)
    held[SUB : SUB + groups] = sums
    out_ref[...] = jnp.zeros_like(out_ref)
    for twin in range(2):
        for j in range(3):
            out_ref[pl.ds(twin * 4 + j, groups, stride=8), :] = held[SUB - 1 + j : SUB - 1 + j + groups]


def rim_kernel(blocks_ref, conductance_ref, _, pair_ref, next_ref):
    size = blocks_ref.shape[1]
    high = blocks_ref.shape[0] - HALO
    odd = parity()
    for ref, first in ((pair_ref, jnp.where(odd == 1, 0, high)), (next_ref, jnp.where(odd == 1, high, 0))):
        for e in range(HALO):
            ref[e, :size] = blocks_ref[first + e]
            ref[e, size:] = jnp.zeros((SUB, size), jnp.float32)
            for way in range(4):
                ref[e, size + way : size + way + 1] = conductance_ref[way, pl.ds(first + e, 1)]


def swap_blocks(tile, piece):
    sub = row_index(SUB)
    block = lax.shift_right_logical(lane_index(SUB), log2_of(piece))
    for bit in (1, 2, 4):
        up, across = (sub & bit) != 0, (block & bit) != 0
        from_below = pltpu.roll(pltpu.roll(tile, SUB - bit, 0), bit * piece, 1)
        from_above = pltpu.roll(pltpu.roll(tile, bit, 0), LANES - bit * piece, 1)
        tile = jnp.where(up == across, tile, jnp.where(up, from_above, from_below))
    return tile


def sweep_kernel(
    width,
    arrived,
    own_blocks,
    own_conductance,
    own_pair,
    own_next,
    twin_blocks,
    twin_conductance,
    twin_pair,
    twin_next,
    _,
    out_ref,
    send_ref,
    pot,
    rhs_ref,
    cond,
):
    position = lax.axis_index("radial")
    size = LANES
    span = 3 * SUB
    base = SUB
    halves = []
    for h in range(2):
        tiles = []
        for g in range(3):
            both = [arrived[pl.ds(h * 64 + r * 4 + g, SUB, stride=8), :] for r in range(2)]
            tiles.append(swap_blocks(both[0] + both[1], width))
        halves.append(jnp.concatenate(tiles, axis=0))
    own_currents = jnp.where(position == 0, halves[0], halves[1])
    twin_currents = jnp.where(position == 0, halves[1], halves[0])
    currents = [own_currents, twin_currents]

    cond[...] = jnp.zeros_like(cond)
    odd = parity()
    rims = ((own_pair, twin_pair, odd == 1), (own_next, twin_next, odd == 0))

    def rim_rows(side, reach):
        for own, twin, is_low in rims:
            for i in range(reach):
                row = jnp.where(is_low, HALO - reach + i, i)
                yield (own, twin)[side], row, jnp.where(is_low, SUB - reach + i, 2 * SUB + i)

    for side, mid in enumerate((own_conductance, twin_conductance)):
        for way in range(4):
            cond[side, way, SUB : 2 * SUB] = mid[way]
    for side in range(2):
        for rim, row, place in rim_rows(side, HALO - side):
            for way in range(4):
                cond[side, way, pl.ds(place, 1)] = rim[row, size + way : size + way + 1]
    pot[...] = jnp.zeros_like(pot)
    eye = row_index(size, size) == lane_index(size, size)
    ones = jnp.ones((SUM_PARTS * size, size), jnp.bfloat16)
    turn = [0]

    def solve_row(side, matrix, row):
        product = matrix * rhs_ref[side, pl.ds(row, 1)]
        turn[0] += 1
        if turn[0] % MXU_EVERY == 0:
            parts = jnp.concatenate(split(product, SUM_PARTS), axis=1).astype(jnp.bfloat16)
            column = jnp.dot(parts, ones, preferred_element_type=jnp.float32)
        else:
            column = jnp.sum(product, axis=1, keepdims=True)
        line = jnp.sum(jnp.where(eye, column, 0.0), axis=0, keepdims=True)
        pot[side, pl.ds(base + row, 1)] = line

    lane = lane_index(span)
    for sweep in range(ITERS_I):
        reach = ITERS_I - 1 - sweep
        sides = (0, 1) if reach else (0,)
        if sweep == 0:
            rhs = currents
        else:
            mid = [pot[side, base : base + span] for side in range(2)]
            west = [pltpu.roll(mid[side], 1, 1) for side in range(2)]
            east = [pltpu.roll(mid[side], LANES - 1, 1) for side in range(2)]
            rhs = []
            for side in sides:
                is_right = position == (1 - side)
                west_edge = jnp.where(is_right, west[1 - side], 0.0)
                east_edge = jnp.where(is_right, 0.0, east[1 - side])
                coupled = currents[side] + cond[side, 0] * pot[side, base - 1 : base - 1 + span]
                coupled = coupled + cond[side, 1] * pot[side, base + 1 : base + 1 + span]
                coupled = coupled + cond[side, 2] * jnp.where(lane == 0, west_edge, west[side])
                coupled = coupled + cond[side, 3] * jnp.where(lane == LANES - 1, east_edge, east[side])
                rhs.append(coupled)
        for side in sides:
            rhs_ref[side] = rhs[side]
        for side in sides:
            for rim, row, place in rim_rows(side, reach - side):
                solve_row(side, rim[row, :size], place)
        for side in sides:
            for e in range(SUB):
                solve_row(side, (own_blocks, twin_blocks)[side][e], SUB + e)
    result = pot[0, base + SUB : base + 2 * SUB]
    out_ref[...] = result
    packed = swap_blocks(result, width)
    send_ref[...] = jnp.zeros_like(send_ref)
    for twin in range(2):
        send_ref[pl.ds(position * 2 * SUB + twin, SUB, stride=2), :] = packed


def gather_kernel(width, columns, direct, table_ref, nodes_ref, out_ref):
    first_column = lax.axis_index("shell") * width
    if direct:
        table = table_ref[...]
    else:
        half = lax.shift_right_logical(first_column, 7)
        table = table_ref[pl.ds(half, table_ref.shape[0] // 2, stride=2), :]
    lines = [jnp.broadcast_to(table[c : c + 1, :], (SUB, LANES)) for c in range(table.shape[0])]
    for r in range(nodes_ref.shape[0] // SUB):
        rows = slice(r * SUB, (r + 1) * SUB)
        row, column = node_row_column(nodes_ref[rows], columns)
        slot = row * width + (column - first_column)
        group, place = lax.shift_right_logical(slot, 7), slot & (LANES - 1)
        value = jnp.zeros((SUB, LANES), jnp.float32)
        for c, line in enumerate(lines):
            value = jnp.where(group == c, jnp.take_along_axis(line, place, axis=1), value)
        out_ref[rows] = value


def ring(axis, step, periodic):
    count = lax.axis_size(axis)
    pairs = [(i, i + step) for i in range(count)]
    if periodic:
        return [(i, j % count) for i, j in pairs]
    return [(i, j) for i, j in pairs if 0 <= j < count]


def pairs(first, periodic):
    count = lax.axis_size("shell")
    assert count % 2 == 0
    out = []
    for i in range(first, count, 2):
        if i + 1 < count or periodic:
            j = (i + 1) % count
            out += [(i, j), (j, i)]
    return out


def exchange_halos(after, pair, edge):
    return (
        lax.ppermute(after, "shell", pairs(1, True)),
        lax.ppermute(pair, "shell", pairs(0, True)),
        lax.ppermute(edge, "radial", [(0, 1), (1, 0)]),
    )


def padded_2(block, sides, width):
    for axis, dim in sides:
        low = lax.ppermute(
            lax.slice_in_dim(block, block.shape[dim] - width, None, axis=dim), axis, ring(axis, 1, False)
        )
        high = lax.ppermute(lax.slice_in_dim(block, 0, width, axis=dim), axis, ring(axis, -1, False))
        block = jnp.concatenate([low, block, high], axis=dim)
    return block


def general_solve(partial, conductance, blocks, rows_total, width):
    row_partials = lax.all_to_all(
        partial.reshape(rows_total, width), "shell", split_axis=0, concat_axis=1, tiled=True
    )
    currents = lax.psum_scatter(row_partials, "radial", scatter_dimension=1, tiled=True)

    def apply_blocks(vector):
        return jnp.einsum("rij,rj->ri", blocks, vector, precision=lax.Precision.HIGHEST)

    potential = apply_blocks(currents)
    for _ in range(ITERS_I - 1):
        panel = padded_2(potential, (("shell", 0), ("radial", 1)), 1)
        coupled = currents + conductance[0] * panel[:-2, 1:-1]
        coupled = coupled + conductance[1] * panel[2:, 1:-1]
        coupled = coupled + conductance[2] * panel[1:-1, :-2]
        coupled = coupled + conductance[3] * panel[1:-1, 2:]
        potential = apply_blocks(coupled)
    full_rows = lax.all_gather(potential, "radial", axis=1, tiled=True)
    strip = lax.all_to_all(full_rows, "shell", split_axis=1, concat_axis=0, tiled=True)
    return potential, strip.reshape(width, LANES)


def body(state, footpoints, conductance, inverse_blocks):
    fields, layers, lons, lats = state.shape
    shells, radials = lax.axis_size("shell"), lax.axis_size("radial")
    assert (fields, lons, lats, radials) == (8, SUB, LANES, 2)
    cells = layers * SUB
    own_rows, half = conductance.shape[1:]
    assert half == LANES
    rows_total, columns = own_rows * shells, half * radials
    width = columns // shells
    x = state.reshape(fields, cells, lats)
    nodes = footpoints.reshape(cells, lats)
    blocks = inverse_blocks[:, 0]
    fast = own_rows == SUB and width * SUB == LANES

    halo_shapes = [shape_of(8, 2, layers, lats), shape_of(8, 2, layers, lats), shape_of(8, 2 * SUB, lats)]
    stage_scratch = [
        pltpu.VMEM((8, cells + 4 * SUB, lats), jnp.float32),
        pltpu.VMEM((8, (SUB + 4) * layers, lats), jnp.float32),
        pltpu.VMEM((8, cells, lats), jnp.float32),
        pltpu.VMEM((8, cells, lats), jnp.float32),
    ]
    packed = call(functools.partial(pack_kernel, layers), halo_shapes, "pack")(x)
    halos = exchange_halos(*packed)

    if fast:
        rim_shape = shape_of(HALO, half + SUB, half)
        rim_pair, rim_next = call(
            rim_kernel,
            [rim_shape, rim_shape],
            "rim",
            in_specs=[IN_VMEM, IN_VMEM, UNREAD],
        )(blocks, conductance, packed[2])
        rims = [
            lax.ppermute(rim_pair, "shell", pairs(0, False)),
            lax.ppermute(rim_next, "shell", pairs(1, False)),
        ]

    send_shape = shape_of(shells * radials * 4, LANES) if fast else shape_of(width, LANES)
    groups = max(16, width)
    inner = call(
        functools.partial(inner_current_kernel, layers, width, columns), shape_of(groups, LANES), "inner_currents",
        in_specs=[IN_VMEM] * 3 + [UNREAD],
    )(x, halos[2], nodes, blocks)
    sums = call(
        functools.partial(outer_current_kernel, layers, width, columns, fast),
        send_shape,
        "outer_currents",
        flops=CURRENTS,
        scratch=[pltpu.VMEM((groups + 2 * SUB, LANES), jnp.float32)],
        in_specs=[IN_VMEM] * 6 + [UNREAD],
    )(x, *halos, nodes, inner, blocks)

    *section_one, after, pair, edge = call(
        functools.partial(first_stage_kernel, layers),
        [shape_of(fields // SPLIT, cells, lats)] * SPLIT + halo_shapes,
        "first_stage",
        flops=DEAR,
        scratch=stage_scratch,
        in_specs=[IN_VMEM] * 4 + [UNREAD],
    )(x, *halos, sums)
    second_halos = exchange_halos(after, pair, edge)
    later = sums

    if fast:
        rims = call(
            relay_kernel,
            [rim_shape] * 2,
            "relay",
            flops=RELAY,
            in_specs=[UNREAD] * 3,
            out_specs=[UNREAD] * 2,
            input_output_aliases={0: 0, 1: 1},
        )(*rims, sums)
        twin = [(0, 1), (1, 0)]
        twin_parts = [lax.ppermute(v, "radial", twin) for v in (blocks, conductance, *rims)]
        arrived = lax.all_to_all(sums, ("shell", "radial"), split_axis=0, concat_axis=0, tiled=True)
        potential, spread = call(
            functools.partial(sweep_kernel, width),
            [shape_of(own_rows, half), shape_of(shells * radials, half)],
            "sweeps",
            scratch=[
                pltpu.VMEM((2, 5 * SUB, half), jnp.float32),
                pltpu.VMEM((2, 3 * SUB, half), jnp.float32),
                pltpu.VMEM((2, 4, 3 * SUB, half), jnp.float32),
            ],
            flops=DEAR,
            in_specs=[IN_VMEM] * 9 + [UNREAD],
        )(arrived, blocks, conductance, *rims, *twin_parts, edge)
        later = spread
        table = lax.all_to_all(spread, ("shell", "radial"), split_axis=0, concat_axis=0, tiled=True)
    else:
        potential, table = general_solve(sums, conductance, blocks, rows_total, width)

    state_next = call(
        functools.partial(second_stage_kernel, layers),
        shape_of(fields, cells, lats),
        "second_stage",
        flops=DEAR,
        scratch=stage_scratch,
        in_specs=[IN_VMEM] * 4 + [UNREAD] + [IN_VMEM] * SPLIT,
    )(*second_halos, x, later, *section_one)

    footpoint_potential = call(
        functools.partial(gather_kernel, width, columns, not fast), shape_of(cells, lats), "gather"
    )(table, nodes)
    return (
        state_next.reshape(state.shape),
        potential,
        footpoint_potential.reshape(footpoints.shape),
    )


def solution(mesh):
    return jax.shard_map(
        body,
        mesh=mesh,
        in_specs=(
            P(None, "radial", "shell", None),
            P("radial", "shell", None),
            P(None, "shell", "radial"),
            P("shell", "radial", None, None),
        ),
        out_specs=(
            P(None, "radial", "shell", None),
            P("shell", "radial"),
            P("radial", "shell", None),
        ),
        check_vma=False,
    )
```

```python
import functools
import jax
import jax.numpy as jnp
from jax import lax
from jax.experimental import pallas as pl
from jax.experimental.pallas import tpu as pltpu
from jax.sharding import PartitionSpec as P

ITERS_I = 4
HALO = ITERS_I - 1
GAMMA = 5.0 / 3.0
TIME_STEP = 0.02
CELL_AREA = 0.125
TINY = 1e-37
LANES = 128
SPLIT = 2
UNROLL = (16, 8, 8)
SUB = 8
PARTS = 3
SUM_PARTS, MXU_EVERY = 2, 3
VMEM_LIMIT = 6 * 1024 * 1024
CHEAP, CURRENTS, RELAY, DEAR = 1_000, 2_000_000_000, 1_000, 10_000_000_000
IN_HBM = pl.BlockSpec(memory_space=pltpu.HBM)
IN_VMEM = pl.BlockSpec(memory_space=pltpu.VMEM)
UNREAD = pl.BlockSpec(memory_space=pl.ANY)


def call(kernel, out_shape, name, flops=CHEAP, nbytes=1_000, scratch=(), **specs):
    return pl.pallas_call(
        kernel,
        out_shape=out_shape,
        **specs,
        scratch_shapes=list(scratch),
        compiler_params=pltpu.CompilerParams(vmem_limit_bytes=VMEM_LIMIT),
        cost_estimate=pl.CostEstimate(flops=flops, bytes_accessed=nbytes, transcendentals=0),
        name=name,
    )


def shape_of(*dims):
    return jax.ShapeDtypeStruct(dims, jnp.float32)


def lane_index(rows, width=LANES):
    return lax.broadcasted_iota(jnp.int32, (rows, width), 1)


def row_index(rows, width=LANES):
    return lax.broadcasted_iota(jnp.int32, (rows, width), 0)


class Fields:
    def __init__(self, refs):
        self.refs, self.count = refs, refs[0].shape[0]

    def __getitem__(self, index):
        k, *rest = index if isinstance(index, tuple) else (index,)
        return self.refs[k // self.count][(k % self.count, *rest)]

    def __setitem__(self, index, value):
        k, *rest = index
        self.refs[k // self.count][(k % self.count, *rest)] = value


def minmod(a, b):
    return jnp.maximum(jnp.minimum(a, jnp.maximum(b, 0.0)), jnp.minimum(b, 0.0))


def reciprocal(value):
    guess = pl.reciprocal(value, approx=True)
    return guess * (2.0 - value * guess)


def flux_and_speed(u, d):
    density, m, b, energy = u[0], u[1:4], u[4:7], u[7]
    inverse = reciprocal(density)
    v = [component * inverse for component in m]
    field_sq = b[0] * b[0] + b[1] * b[1] + b[2] * b[2]
    twice_kinetic = m[0] * v[0] + m[1] * v[1] + m[2] * v[2]
    pressure = (GAMMA - 1.0) * (energy - 0.5 * (twice_kinetic + field_sq))
    total = pressure + 0.5 * field_sq
    alignment = v[0] * b[0] + v[1] * b[1] + v[2] * b[2]
    vn, bn = v[d], b[d]
    momentum = [m[j] * vn - b[j] * bn for j in range(3)]
    momentum[d] = momentum[d] + total
    induction = [None if j == d else vn * b[j] - bn * v[j] for j in range(3)]
    flux = [m[d]] + momentum + induction + [(energy + total) * vn - bn * alignment]
    squared = (GAMMA * jnp.abs(pressure) + field_sq) * inverse
    speed = jnp.abs(vn) + squared * lax.rsqrt(jnp.maximum(squared, TINY))
    return flux, speed


def face_flux(left, right, d):
    left_flux, left_speed = flux_and_speed(left, d)
    right_flux, right_speed = flux_and_speed(right, d)
    speed = jnp.maximum(left_speed, right_speed)
    out = []
    for k in range(8):
        jump = speed * (right[k] - left[k])
        if left_flux[k] is None:
            out.append(-jump)
        else:
            out.append(left_flux[k] + right_flux[k] - jump)
    return out, left_flux


def march(load, cells, d, emit, unroll):
    before, here, after = load(-2), load(-1), load(0)
    half = [0.5 * minmod(after[k] - here[k], here[k] - before[k]) for k in range(8)]
    left = [here[k] + half[k] for k in range(8)]
    jump = [after[k] - here[k] for k in range(8)]

    def face(f, here, left, jump):
        ahead = load(f + 1)
        next_jump = [ahead[k] - here[k] for k in range(8)]
        half = [0.5 * minmod(next_jump[k], jump[k]) for k in range(8)]
        right = [here[k] - half[k] for k in range(8)]
        flux, _ = face_flux(left, right, d)
        return ahead, [here[k] + half[k] for k in range(8)], next_jump, flux

    here, left, jump, flux = face(0, after, left, jump)

    def step(f, carry):
        here, left, jump, flux = carry
        here, left, jump, new = face(f, here, left, jump)
        emit(f - 1, [new[k] - flux[k] for k in range(8)])
        return here, left, jump, new

    lax.fori_loop(1, cells + 1, step, (here, left, jump, flux), unroll=unroll)


def parity():
    return lax.axis_index("shell") & 1


def pack_halos(source, next_ref, pair_ref, edge_ref, layers, position):
    odd = parity()
    to_pair, to_next = jnp.where(odd == 1, 0, SUB - 2), jnp.where(odd == 1, SUB - 2, 0)
    for k in range(8):
        for j in range(2):
            pair_ref[k, j] = source[k, pl.ds(to_pair + j, layers, stride=SUB), :]
            next_ref[k, j] = source[k, pl.ds(to_next + j, layers, stride=SUB), :]
    first = jnp.where(position == 0, (layers - 2) * SUB, 0)
    first = pl.multiple_of(first, SUB)
    for k in range(8):
        edge_ref[k] = source[k, pl.ds(first, 2 * SUB), :]


def tendency_into(x_ref, next_ref, pair_ref, edge_ref, xr, xl, div, lon_div, layers, position, last, finish):
    cells = layers * SUB
    from_below = parity() == 1
    for k in range(8):
        xr[k, 2 * SUB : 2 * SUB + cells] = x_ref[k]
        first, final = x_ref[k, 0:SUB], x_ref[k, cells - SUB : cells]
        for j in range(2):
            rows = slice(j * SUB, (j + 1) * SUB)
            xr[k, j * SUB : (j + 1) * SUB] = jnp.where(position == 0, first, edge_ref[k, rows])
            xr[k, cells + (2 + j) * SUB : cells + (3 + j) * SUB] = jnp.where(
                position == last, final, edge_ref[k, rows]
            )
            pair, after = pair_ref[k, j], next_ref[k, j]
            xl[k, j * layers : (j + 1) * layers] = jnp.where(from_below, pair, after)
            xl[k, (SUB + 2 + j) * layers : (SUB + 3 + j) * layers] = jnp.where(from_below, after, pair)
        for j in range(SUB):
            xl[k, (2 + j) * layers : (3 + j) * layers] = x_ref[k, pl.ds(j, layers, stride=SUB), :]

    def load_radial(c):
        start = (c + 2) * SUB
        if not isinstance(start, int):
            start = pl.multiple_of(start, SUB)
        return [xr[k, pl.ds(start, SUB), :] for k in range(8)]

    def emit_radial(c, values):
        start = pl.multiple_of(c * SUB, SUB)
        for k in range(8):
            div[k, pl.ds(start, SUB), :] = values[k]

    march(load_radial, layers, 0, emit_radial, UNROLL[0])

    def load_lon(c):
        start = (c + 2) * layers
        if not isinstance(start, int):
            start = pl.multiple_of(start, SUB)
        return [xl[k, pl.ds(start, layers), :] for k in range(8)]

    def emit_lon(c, values):
        start = pl.multiple_of(c * layers, SUB)
        for k in range(8):
            lon_div[k, pl.ds(start, layers), :] = values[k]

    march(load_lon, SUB, 1, emit_lon, UNROLL[1])

    lane = lane_index(SUB)
    at_first, at_last = lane == 0, lane == LANES - 1
    half_inside = jnp.where(at_first | at_last, 0.0, 0.5)

    def layer(r, carry):
        rows = pl.ds(pl.multiple_of(r * SUB, SUB), SUB)
        x = [x_ref[k, rows, :] for k in range(8)]
        left, right = [], []
        for k in range(8):
            jump = pltpu.roll(x[k], LANES - 1, 1) - x[k]
            half = half_inside * minmod(jump, pltpu.roll(jump, 1, 1))
            left.append(x[k] + half)
            down = x[k] - half
            right.append(jnp.where(at_last, down, pltpu.roll(down, LANES - 1, 1)))
        flux, left_flux = face_flux(left, right, 2)
        total = []
        for k in range(8):
            edge = 0.0 if left_flux[k] is None else 2.0 * left_flux[k]
            aside = div[k, rows, :] + lon_div[k, pl.ds(r, SUB, stride=layers), :]
            total.append(
                aside + flux[k] - jnp.where(at_first, edge, pltpu.roll(flux[k], 1, 1))
            )
        finish(rows, x, total)
        return carry

    lax.fori_loop(0, layers, layer, 0, unroll=UNROLL[2])


def pack_kernel(layers, x_ref, next_ref, pair_ref, edge_ref):
    pack_halos(x_ref, next_ref, pair_ref, edge_ref, layers, lax.axis_index("radial"))


def relay_kernel(*refs):
    pass


def first_stage_kernel(layers, x_ref, after, pair, edge, _, *refs):
    out_ref, (next_ref, pair_ref, edge_ref, xr, xl, div, lon_div) = Fields(refs[:-7]), refs[-7:]
    position, last = lax.axis_index("radial"), lax.axis_size("radial") - 1

    def finish(rows, x, total):
        for k in range(8):
            out_ref[k, rows, :] = x[k] - 0.5 * TIME_STEP * total[k]

    tendency_into(x_ref, after, pair, edge, xr, xl, div, lon_div, layers, position, last, finish)
    pack_halos(out_ref, next_ref, pair_ref, edge_ref, layers, position)


def second_stage_kernel(layers, after, pair, edge, state_ref, _, *refs):
    x_ref, (out_ref, xr, xl, div, lon_div) = Fields(refs[:-5]), refs[-5:]
    position, last = lax.axis_index("radial"), lax.axis_size("radial") - 1

    def finish(rows, x, total):
        for k in range(8):
            out_ref[k, rows, :] = 0.5 * state_ref[k, rows, :] + 0.5 * (x[k] - 0.5 * TIME_STEP * total[k])

    tendency_into(x_ref, after, pair, edge, xr, xl, div, lon_div, layers, position, last, finish)


def log2_of(value):
    assert value & (value - 1) == 0
    return value.bit_length() - 1


def node_row_column(nodes, columns):
    return lax.shift_right_logical(nodes, log2_of(columns)), nodes & (columns - 1)


def split(value, count):
    parts = []
    for _ in range(count):
        part = value.astype(jnp.bfloat16).astype(jnp.float32)
        parts.append(part)
        value = value - part
    return parts


def lat_pair(value):
    lane = lane_index(value.shape[0])
    above = jnp.where(lane == LANES - 1, value, pltpu.roll(value, LANES - 1, 1))
    below = jnp.where(lane == 0, value, pltpu.roll(value, 1, 1))
    return 0.5 * (above - below)


def aligned_current(b, radial, lon):
    first = lon(2) - lat_pair(b[1])
    second = lat_pair(b[0]) - radial(2)
    third = radial(1) - lon(0)
    aligned = first * b[0] + second * b[1] + third * b[2]
    field_sq = b[0] * b[0] + b[1] * b[1] + b[2] * b[2]
    return CELL_AREA * aligned * lax.rsqrt(1.0 + field_sq)


class Scatter:
    def __init__(self, width, columns):
        self.width, self.columns = width, columns
        self.first_column = lax.axis_index("shell") * width
        self.groups = max(16, width)
        self.group_rows = row_index(self.groups)
        self.slot_rows = row_index(LANES)
        self.total = jnp.zeros((PARTS * self.groups, LANES), jnp.float32)

    def add(self, values, nodes, lines):
        row, column = node_row_column(nodes, self.columns)
        slot = row * self.width + (column - self.first_column)
        group, place = lax.shift_right_logical(slot, 7), slot & (LANES - 1)
        parts = split(values, PARTS)
        lefts, rights = [], []
        for l in lines:
            here = self.group_rows == group[l : l + 1, :]
            lefts.append(
                jnp.concatenate([jnp.where(here, part[l : l + 1, :], 0.0) for part in parts], axis=0)
            )
            rights.append(jnp.where(self.slot_rows == place[l : l + 1, :], 1.0, 0.0))
        left = jnp.concatenate(lefts, axis=1).astype(jnp.bfloat16)
        right = jnp.concatenate(rights, axis=1).astype(jnp.bfloat16)
        self.total = self.total + lax.dot_general(
            left, right, (((1,), (1,)), ((), ())), preferred_element_type=jnp.float32
        )

    def sums(self):
        sums = self.total[: self.groups]
        for part in range(1, PARTS):
            sums = sums + self.total[part * self.groups : (part + 1) * self.groups]
        return sums


def inner_current_kernel(layers, width, columns, x_ref, edge, nodes_ref, _, out_ref):
    position, last = lax.axis_index("radial"), lax.axis_size("radial") - 1
    scatter = Scatter(width, columns)
    rows = lambda r: slice(r * SUB, (r + 1) * SUB)
    for r in range(layers):
        b = [x_ref[4 + k, rows(r)] for k in range(3)]

        def radial(k):
            if r == 0:
                below = jnp.where(position == 0, b[k], edge[4 + k, rows(1)])
            else:
                below = x_ref[4 + k, rows(r - 1)]
            if r == layers - 1:
                above = jnp.where(position == last, b[k], edge[4 + k, rows(0)])
            else:
                above = x_ref[4 + k, rows(r + 1)]
            return 0.5 * (above - below)

        def lon(k):
            return 0.5 * (pltpu.roll(b[k], SUB - 1, 0) - pltpu.roll(b[k], 1, 0))

        scatter.add(aligned_current(b, radial, lon), nodes_ref[rows(r)], range(1, SUB - 1))
    out_ref[...] = scatter.sums()


def outer_current_kernel(
    layers, width, columns, window, x_ref, after, pair, edge, nodes_ref, inner_ref, _, out_ref, held
):
    position, last = lax.axis_index("radial"), lax.axis_size("radial") - 1
    from_below = parity() == 1
    scatter = Scatter(width, columns)
    layer = row_index(layers)
    for l in (0, SUB - 1):
        line = lambda k, l: x_ref[4 + k, pl.ds(l, layers, stride=SUB), :]
        b = [line(k, l) for k in range(3)]

        def radial(k):
            first = jnp.where(position == 0, b[k][:1], edge[4 + k, SUB + l : SUB + l + 1])
            final = jnp.where(position == last, b[k][layers - 1 :], edge[4 + k, l : l + 1])
            below = jnp.where(layer == 0, first, pltpu.roll(b[k], 1, 0))
            above = jnp.where(layer == layers - 1, final, pltpu.roll(b[k], layers - 1, 0))
            return 0.5 * (above - below)

        def lon(k):
            if l == 0:
                return 0.5 * (line(k, 1) - jnp.where(from_below, pair[4 + k, 1], after[4 + k, 1]))
            return 0.5 * (jnp.where(from_below, after[4 + k, 0], pair[4 + k, 0]) - line(k, l - 1))

        values = aligned_current(b, radial, lon)
        nodes = nodes_ref[pl.ds(l, layers, stride=SUB), :]
        for r in range(0, layers, SUB):
            scatter.add(values[r : r + SUB], nodes[r : r + SUB], range(SUB))
    sums = inner_ref[...] + scatter.sums()
    groups = scatter.groups
    if not window:
        out_ref[...] = sums[: out_ref.shape[0]]
        return
    held[...] = jnp.zeros_like(held)
    held[SUB : SUB + groups] = sums
    out_ref[...] = jnp.zeros_like(out_ref)
    for twin in range(2):
        for j in range(3):
            out_ref[pl.ds(twin * 4 + j, groups, stride=8), :] = held[SUB - 1 + j : SUB - 1 + j + groups]


def rim_kernel(blocks_ref, conductance_ref, _, pair_ref, next_ref):
    size = blocks_ref.shape[1]
    high = blocks_ref.shape[0] - HALO
    odd = parity()
    for ref, first in ((pair_ref, jnp.where(odd == 1, 0, high)), (next_ref, jnp.where(odd == 1, high, 0))):
        for e in range(HALO):
            ref[e, :size] = blocks_ref[first + e]
            ref[e, size:] = jnp.zeros((SUB, size), jnp.float32)
            for way in range(4):
                ref[e, size + way : size + way + 1] = conductance_ref[way, pl.ds(first + e, 1)]


def swap_blocks(tile, piece):
    sub = row_index(SUB)
    block = lax.shift_right_logical(lane_index(SUB), log2_of(piece))
    for bit in (1, 2, 4):
        up, across = (sub & bit) != 0, (block & bit) != 0
        from_below = pltpu.roll(pltpu.roll(tile, SUB - bit, 0), bit * piece, 1)
        from_above = pltpu.roll(pltpu.roll(tile, bit, 0), LANES - bit * piece, 1)
        tile = jnp.where(up == across, tile, jnp.where(up, from_above, from_below))
    return tile


def sweep_kernel(
    width,
    arrived,
    own_blocks,
    own_conductance,
    own_pair,
    own_next,
    twin_blocks,
    twin_conductance,
    twin_pair,
    twin_next,
    _,
    out_ref,
    send_ref,
    pot,
    rhs_ref,
    cond,
):
    position = lax.axis_index("radial")
    size = LANES
    span = 3 * SUB
    base = SUB
    halves = []
    for h in range(2):
        tiles = []
        for g in range(3):
            both = [arrived[pl.ds(h * 64 + r * 4 + g, SUB, stride=8), :] for r in range(2)]
            tiles.append(swap_blocks(both[0] + both[1], width))
        halves.append(jnp.concatenate(tiles, axis=0))
    own_currents = jnp.where(position == 0, halves[0], halves[1])
    twin_currents = jnp.where(position == 0, halves[1], halves[0])
    currents = [own_currents, twin_currents]

    cond[...] = jnp.zeros_like(cond)
    odd = parity()
    rims = ((own_pair, twin_pair, odd == 1), (own_next, twin_next, odd == 0))

    def rim_rows(side, reach):
        for own, twin, is_low in rims:
            for i in range(reach):
                row = jnp.where(is_low, HALO - reach + i, i)
                yield (own, twin)[side], row, jnp.where(is_low, SUB - reach + i, 2 * SUB + i)

    for side, mid in enumerate((own_conductance, twin_conductance)):
        for way in range(4):
            cond[side, way, SUB : 2 * SUB] = mid[way]
    for side in range(2):
        for rim, row, place in rim_rows(side, HALO - side):
            for way in range(4):
                cond[side, way, pl.ds(place, 1)] = rim[row, size + way : size + way + 1]
    pot[...] = jnp.zeros_like(pot)
    eye = row_index(size, size) == lane_index(size, size)
    ones = jnp.ones((SUM_PARTS * size, size), jnp.bfloat16)
    turn = [0]

    def solve_row(side, matrix, row):
        product = matrix * rhs_ref[side, pl.ds(row, 1)]
        turn[0] += 1
        if turn[0] % MXU_EVERY == 0:
            parts = jnp.concatenate(split(product, SUM_PARTS), axis=1).astype(jnp.bfloat16)
            column = jnp.dot(parts, ones, preferred_element_type=jnp.float32)
        else:
            column = jnp.sum(product, axis=1, keepdims=True)
        line = jnp.sum(jnp.where(eye, column, 0.0), axis=0, keepdims=True)
        pot[side, pl.ds(base + row, 1)] = line

    lane = lane_index(span)
    for sweep in range(ITERS_I):
        reach = ITERS_I - 1 - sweep
        sides = (0, 1) if reach else (0,)
        if sweep == 0:
            rhs = currents
        else:
            mid = [pot[side, base : base + span] for side in range(2)]
            west = [pltpu.roll(mid[side], 1, 1) for side in range(2)]
            east = [pltpu.roll(mid[side], LANES - 1, 1) for side in range(2)]
            rhs = []
            for side in sides:
                is_right = position == (1 - side)
                west_edge = jnp.where(is_right, west[1 - side], 0.0)
                east_edge = jnp.where(is_right, 0.0, east[1 - side])
                coupled = currents[side] + cond[side, 0] * pot[side, base - 1 : base - 1 + span]
                coupled = coupled + cond[side, 1] * pot[side, base + 1 : base + 1 + span]
                coupled = coupled + cond[side, 2] * jnp.where(lane == 0, west_edge, west[side])
                coupled = coupled + cond[side, 3] * jnp.where(lane == LANES - 1, east_edge, east[side])
                rhs.append(coupled)
        for side in sides:
            rhs_ref[side] = rhs[side]
        for side in sides:
            for rim, row, place in rim_rows(side, reach - side):
                solve_row(side, rim[row, :size], place)
        for side in sides:
            for e in range(SUB):
                solve_row(side, (own_blocks, twin_blocks)[side][e], SUB + e)
    result = pot[0, base + SUB : base + 2 * SUB]
    out_ref[...] = result
    packed = swap_blocks(result, width)
    send_ref[...] = jnp.zeros_like(send_ref)
    for twin in range(2):
        send_ref[pl.ds(position * 2 * SUB + twin, SUB, stride=2), :] = packed


def gather_kernel(width, columns, direct, table_ref, nodes_ref, out_ref):
    first_column = lax.axis_index("shell") * width
    if direct:
        table = table_ref[...]
    else:
        half = lax.shift_right_logical(first_column, 7)
        table = table_ref[pl.ds(half, table_ref.shape[0] // 2, stride=2), :]
    lines = [jnp.broadcast_to(table[c : c + 1, :], (SUB, LANES)) for c in range(table.shape[0])]
    for r in range(nodes_ref.shape[0] // SUB):
        rows = slice(r * SUB, (r + 1) * SUB)
        row, column = node_row_column(nodes_ref[rows], columns)
        slot = row * width + (column - first_column)
        group, place = lax.shift_right_logical(slot, 7), slot & (LANES - 1)
        value = jnp.zeros((SUB, LANES), jnp.float32)
        for c, line in enumerate(lines):
            value = jnp.where(group == c, jnp.take_along_axis(line, place, axis=1), value)
        out_ref[rows] = value


def ring(axis, step, periodic):
    count = lax.axis_size(axis)
    pairs = [(i, i + step) for i in range(count)]
    if periodic:
        return [(i, j % count) for i, j in pairs]
    return [(i, j) for i, j in pairs if 0 <= j < count]


def pairs(first, periodic):
    count = lax.axis_size("shell")
    assert count % 2 == 0
    out = []
    for i in range(first, count, 2):
        if i + 1 < count or periodic:
            j = (i + 1) % count
            out += [(i, j), (j, i)]
    return out


def exchange_halos(after, pair, edge):
    return (
        lax.ppermute(after, "shell", pairs(1, True)),
        lax.ppermute(pair, "shell", pairs(0, True)),
        lax.ppermute(edge, "radial", [(0, 1), (1, 0)]),
    )


def padded_2(block, sides, width):
    for axis, dim in sides:
        low = lax.ppermute(
            lax.slice_in_dim(block, block.shape[dim] - width, None, axis=dim), axis, ring(axis, 1, False)
        )
        high = lax.ppermute(lax.slice_in_dim(block, 0, width, axis=dim), axis, ring(axis, -1, False))
        block = jnp.concatenate([low, block, high], axis=dim)
    return block


def general_solve(partial, conductance, blocks, rows_total, width):
    row_partials = lax.all_to_all(
        partial.reshape(rows_total, width), "shell", split_axis=0, concat_axis=1, tiled=True
    )
    currents = lax.psum_scatter(row_partials, "radial", scatter_dimension=1, tiled=True)

    def apply_blocks(vector):
        return jnp.einsum("rij,rj->ri", blocks, vector, precision=lax.Precision.HIGHEST)

    potential = apply_blocks(currents)
    for _ in range(ITERS_I - 1):
        panel = padded_2(potential, (("shell", 0), ("radial", 1)), 1)
        coupled = currents + conductance[0] * panel[:-2, 1:-1]
        coupled = coupled + conductance[1] * panel[2:, 1:-1]
        coupled = coupled + conductance[2] * panel[1:-1, :-2]
        coupled = coupled + conductance[3] * panel[1:-1, 2:]
        potential = apply_blocks(coupled)
    full_rows = lax.all_gather(potential, "radial", axis=1, tiled=True)
    strip = lax.all_to_all(full_rows, "shell", split_axis=1, concat_axis=0, tiled=True)
    return potential, strip.reshape(width, LANES)


def body(state, footpoints, conductance, inverse_blocks):
    fields, layers, lons, lats = state.shape
    shells, radials = lax.axis_size("shell"), lax.axis_size("radial")
    assert (fields, lons, lats, radials) == (8, SUB, LANES, 2)
    cells = layers * SUB
    own_rows, half = conductance.shape[1:]
    assert half == LANES
    rows_total, columns = own_rows * shells, half * radials
    width = columns // shells
    x = state.reshape(fields, cells, lats)
    nodes = footpoints.reshape(cells, lats)
    blocks = inverse_blocks[:, 0]
    fast = own_rows == SUB and width * SUB == LANES

    halo_shapes = [shape_of(8, 2, layers, lats), shape_of(8, 2, layers, lats), shape_of(8, 2 * SUB, lats)]
    stage_scratch = [
        pltpu.VMEM((8, cells + 4 * SUB, lats), jnp.float32),
        pltpu.VMEM((8, (SUB + 4) * layers, lats), jnp.float32),
        pltpu.VMEM((8, cells, lats), jnp.float32),
        pltpu.VMEM((8, cells, lats), jnp.float32),
    ]
    packed = call(functools.partial(pack_kernel, layers), halo_shapes, "pack")(x)
    halos = exchange_halos(*packed)

    if fast:
        rim_shape = shape_of(HALO, half + SUB, half)
        rim_pair, rim_next = call(
            rim_kernel,
            [rim_shape, rim_shape],
            "rim",
            in_specs=[IN_VMEM, IN_VMEM, UNREAD],
        )(blocks, conductance, packed[2])
        rims = [
            lax.ppermute(rim_pair, "shell", pairs(0, False)),
            lax.ppermute(rim_next, "shell", pairs(1, False)),
        ]

    send_shape = shape_of(shells * radials * 4, LANES) if fast else shape_of(width, LANES)
    groups = max(16, width)
    inner = call(
        functools.partial(inner_current_kernel, layers, width, columns), shape_of(groups, LANES), "inner_currents",
        in_specs=[IN_VMEM] * 3 + [UNREAD],
    )(x, halos[2], nodes, blocks)
    sums = call(
        functools.partial(outer_current_kernel, layers, width, columns, fast),
        send_shape,
        "outer_currents",
        flops=CURRENTS,
        scratch=[pltpu.VMEM((groups + 2 * SUB, LANES), jnp.float32)],
        in_specs=[IN_VMEM] * 6 + [UNREAD],
    )(x, *halos, nodes, inner, blocks)

    *section_one, after, pair, edge = call(
        functools.partial(first_stage_kernel, layers),
        [shape_of(fields // SPLIT, cells, lats)] * SPLIT + halo_shapes,
        "first_stage",
        flops=DEAR,
        scratch=stage_scratch,
        in_specs=[IN_VMEM] * 4 + [UNREAD],
    )(x, *halos, sums)
    second_halos = exchange_halos(after, pair, edge)
    later = sums

    if fast:
        rims = call(
            relay_kernel,
            [rim_shape] * 2,
            "relay",
            flops=RELAY,
            in_specs=[UNREAD] * 3,
            out_specs=[UNREAD] * 2,
            input_output_aliases={0: 0, 1: 1},
        )(*rims, sums)
        twin = [(0, 1), (1, 0)]
        twin_parts = [lax.ppermute(v, "radial", twin) for v in (blocks, conductance, *rims)]
        arrived = lax.all_to_all(sums, ("shell", "radial"), split_axis=0, concat_axis=0, tiled=True)
        potential, spread = call(
            functools.partial(sweep_kernel, width),
            [shape_of(own_rows, half), shape_of(shells * radials, half)],
            "sweeps",
            scratch=[
                pltpu.VMEM((2, 5 * SUB, half), jnp.float32),
                pltpu.VMEM((2, 3 * SUB, half), jnp.float32),
                pltpu.VMEM((2, 4, 3 * SUB, half), jnp.float32),
            ],
            flops=DEAR,
            in_specs=[IN_VMEM] * 9 + [UNREAD],
        )(arrived, blocks, conductance, *rims, *twin_parts, edge)
        later = spread
        table = lax.all_to_all(spread, ("shell", "radial"), split_axis=0, concat_axis=0, tiled=True)
    else:
        potential, table = general_solve(sums, conductance, blocks, rows_total, width)

    state_next = call(
        functools.partial(second_stage_kernel, layers),
        shape_of(fields, cells, lats),
        "second_stage",
        flops=DEAR,
        scratch=stage_scratch,
        in_specs=[IN_VMEM] * 4 + [UNREAD] + [IN_VMEM] * SPLIT,
    )(*second_halos, x, later, *section_one)

    footpoint_potential = call(
        functools.partial(gather_kernel, width, columns, not fast), shape_of(cells, lats), "gather"
    )(table, nodes)
    return (
        state_next.reshape(state.shape),
        potential,
        footpoint_potential.reshape(footpoints.shape),
    )


def solution(mesh):
    return jax.shard_map(
        body,
        mesh=mesh,
        in_specs=(
            P(None, "radial", "shell", None),
            P("radial", "shell", None),
            P(None, "shell", "radial"),
            P("shell", "radial", None, None),
        ),
        out_specs=(
            P(None, "radial", "shell", None),
            P("shell", "radial"),
            P("radial", "shell", None),
        ),
        check_vma=False,
    )
```

```python
import functools
import jax
import jax.numpy as jnp
from jax import lax
from jax.experimental import pallas as pl
from jax.experimental.pallas import tpu as pltpu
from jax.sharding import PartitionSpec as P

ITERS_I = 4
HALO = ITERS_I - 1
GAMMA = 5.0 / 3.0
TIME_STEP = 0.02
CELL_AREA = 0.125
TINY = 1e-37
LANES = 128
SPLIT = 2
UNROLL = (16, 8, 8)
SUB = 8
PARTS = 3
SUM_PARTS, MXU_EVERY = 3, 4
VMEM_LIMIT = 6 * 1024 * 1024
CHEAP, CURRENTS, RELAY, DEAR = 1_000, 2_000_000_000, 1_000, 10_000_000_000
IN_HBM = pl.BlockSpec(memory_space=pltpu.HBM)
IN_VMEM = pl.BlockSpec(memory_space=pltpu.VMEM)
UNREAD = pl.BlockSpec(memory_space=pl.ANY)


def call(kernel, out_shape, name, flops=CHEAP, nbytes=1_000, scratch=(), **specs):
    return pl.pallas_call(
        kernel,
        out_shape=out_shape,
        **specs,
        scratch_shapes=list(scratch),
        compiler_params=pltpu.CompilerParams(vmem_limit_bytes=VMEM_LIMIT),
        cost_estimate=pl.CostEstimate(flops=flops, bytes_accessed=nbytes, transcendentals=0),
        name=name,
    )


def shape_of(*dims):
    return jax.ShapeDtypeStruct(dims, jnp.float32)


def lane_index(rows, width=LANES):
    return lax.broadcasted_iota(jnp.int32, (rows, width), 1)


def row_index(rows, width=LANES):
    return lax.broadcasted_iota(jnp.int32, (rows, width), 0)


class Fields:
    def __init__(self, refs):
        self.refs, self.count = refs, refs[0].shape[0]

    def __getitem__(self, index):
        k, *rest = index if isinstance(index, tuple) else (index,)
        return self.refs[k // self.count][(k % self.count, *rest)]

    def __setitem__(self, index, value):
        k, *rest = index
        self.refs[k // self.count][(k % self.count, *rest)] = value


def minmod(a, b):
    return jnp.maximum(jnp.minimum(a, jnp.maximum(b, 0.0)), jnp.minimum(b, 0.0))


def reciprocal(value):
    guess = pl.reciprocal(value, approx=True)
    return guess * (2.0 - value * guess)


def flux_and_speed(u, d):
    density, m, b, energy = u[0], u[1:4], u[4:7], u[7]
    inverse = reciprocal(density)
    v = [component * inverse for component in m]
    field_sq = b[0] * b[0] + b[1] * b[1] + b[2] * b[2]
    twice_kinetic = m[0] * v[0] + m[1] * v[1] + m[2] * v[2]
    pressure = (GAMMA - 1.0) * (energy - 0.5 * (twice_kinetic + field_sq))
    total = pressure + 0.5 * field_sq
    alignment = v[0] * b[0] + v[1] * b[1] + v[2] * b[2]
    vn, bn = v[d], b[d]
    momentum = [m[j] * vn - b[j] * bn for j in range(3)]
    momentum[d] = momentum[d] + total
    induction = [None if j == d else vn * b[j] - bn * v[j] for j in range(3)]
    flux = [m[d]] + momentum + induction + [(energy + total) * vn - bn * alignment]
    squared = (GAMMA * jnp.abs(pressure) + field_sq) * inverse
    speed = jnp.abs(vn) + squared * lax.rsqrt(jnp.maximum(squared, TINY))
    return flux, speed


def face_flux(left, right, d):
    left_flux, left_speed = flux_and_speed(left, d)
    right_flux, right_speed = flux_and_speed(right, d)
    speed = jnp.maximum(left_speed, right_speed)
    out = []
    for k in range(8):
        jump = speed * (right[k] - left[k])
        if left_flux[k] is None:
            out.append(-jump)
        else:
            out.append(left_flux[k] + right_flux[k] - jump)
    return out, left_flux


def march(load, cells, d, emit, unroll):
    before, here, after = load(-2), load(-1), load(0)
    half = [0.5 * minmod(after[k] - here[k], here[k] - before[k]) for k in range(8)]
    left = [here[k] + half[k] for k in range(8)]
    jump = [after[k] - here[k] for k in range(8)]

    def face(f, here, left, jump):
        ahead = load(f + 1)
        next_jump = [ahead[k] - here[k] for k in range(8)]
        half = [0.5 * minmod(next_jump[k], jump[k]) for k in range(8)]
        right = [here[k] - half[k] for k in range(8)]
        flux, _ = face_flux(left, right, d)
        return ahead, [here[k] + half[k] for k in range(8)], next_jump, flux

    here, left, jump, flux = face(0, after, left, jump)

    def step(f, carry):
        here, left, jump, flux = carry
        here, left, jump, new = face(f, here, left, jump)
        emit(f - 1, [new[k] - flux[k] for k in range(8)])
        return here, left, jump, new

    lax.fori_loop(1, cells + 1, step, (here, left, jump, flux), unroll=unroll)


def parity():
    return lax.axis_index("shell") & 1


def pack_halos(source, next_ref, pair_ref, edge_ref, layers, position):
    odd = parity()
    to_pair, to_next = jnp.where(odd == 1, 0, SUB - 2), jnp.where(odd == 1, SUB - 2, 0)
    for k in range(8):
        for j in range(2):
            pair_ref[k, j] = source[k, pl.ds(to_pair + j, layers, stride=SUB), :]
            next_ref[k, j] = source[k, pl.ds(to_next + j, layers, stride=SUB), :]
    first = jnp.where(position == 0, (layers - 2) * SUB, 0)
    first = pl.multiple_of(first, SUB)
    for k in range(8):
        edge_ref[k] = source[k, pl.ds(first, 2 * SUB), :]


def tendency_into(x_ref, next_ref, pair_ref, edge_ref, xr, xl, div, lon_div, layers, position, last, finish):
    cells = layers * SUB
    from_below = parity() == 1
    for k in range(8):
        xr[k, 2 * SUB : 2 * SUB + cells] = x_ref[k]
        first, final = x_ref[k, 0:SUB], x_ref[k, cells - SUB : cells]
        for j in range(2):
            rows = slice(j * SUB, (j + 1) * SUB)
            xr[k, j * SUB : (j + 1) * SUB] = jnp.where(position == 0, first, edge_ref[k, rows])
            xr[k, cells + (2 + j) * SUB : cells + (3 + j) * SUB] = jnp.where(
                position == last, final, edge_ref[k, rows]
            )
            pair, after = pair_ref[k, j], next_ref[k, j]
            xl[k, j * layers : (j + 1) * layers] = jnp.where(from_below, pair, after)
            xl[k, (SUB + 2 + j) * layers : (SUB + 3 + j) * layers] = jnp.where(from_below, after, pair)
        for j in range(SUB):
            xl[k, (2 + j) * layers : (3 + j) * layers] = x_ref[k, pl.ds(j, layers, stride=SUB), :]

    def load_radial(c):
        start = (c + 2) * SUB
        if not isinstance(start, int):
            start = pl.multiple_of(start, SUB)
        return [xr[k, pl.ds(start, SUB), :] for k in range(8)]

    def emit_radial(c, values):
        start = pl.multiple_of(c * SUB, SUB)
        for k in range(8):
            div[k, pl.ds(start, SUB), :] = values[k]

    march(load_radial, layers, 0, emit_radial, UNROLL[0])

    def load_lon(c):
        start = (c + 2) * layers
        if not isinstance(start, int):
            start = pl.multiple_of(start, SUB)
        return [xl[k, pl.ds(start, layers), :] for k in range(8)]

    def emit_lon(c, values):
        start = pl.multiple_of(c * layers, SUB)
        for k in range(8):
            lon_div[k, pl.ds(start, layers), :] = values[k]

    march(load_lon, SUB, 1, emit_lon, UNROLL[1])

    lane = lane_index(SUB)
    at_first, at_last = lane == 0, lane == LANES - 1
    half_inside = jnp.where(at_first | at_last, 0.0, 0.5)

    def layer(r, carry):
        rows = pl.ds(pl.multiple_of(r * SUB, SUB), SUB)
        x = [x_ref[k, rows, :] for k in range(8)]
        left, right = [], []
        for k in range(8):
            jump = pltpu.roll(x[k], LANES - 1, 1) - x[k]
            half = half_inside * minmod(jump, pltpu.roll(jump, 1, 1))
            left.append(x[k] + half)
            down = x[k] - half
            right.append(jnp.where(at_last, down, pltpu.roll(down, LANES - 1, 1)))
        flux, left_flux = face_flux(left, right, 2)
        total = []
        for k in range(8):
            edge = 0.0 if left_flux[k] is None else 2.0 * left_flux[k]
            aside = div[k, rows, :] + lon_div[k, pl.ds(r, SUB, stride=layers), :]
            total.append(
                aside + flux[k] - jnp.where(at_first, edge, pltpu.roll(flux[k], 1, 1))
            )
        finish(rows, x, total)
        return carry

    lax.fori_loop(0, layers, layer, 0, unroll=UNROLL[2])


def pack_kernel(layers, x_ref, next_ref, pair_ref, edge_ref):
    pack_halos(x_ref, next_ref, pair_ref, edge_ref, layers, lax.axis_index("radial"))


def relay_kernel(*refs):
    pass


def first_stage_kernel(layers, x_ref, after, pair, edge, _, *refs):
    out_ref, (next_ref, pair_ref, edge_ref, xr, xl, div, lon_div) = Fields(refs[:-7]), refs[-7:]
    position, last = lax.axis_index("radial"), lax.axis_size("radial") - 1

    def finish(rows, x, total):
        for k in range(8):
            out_ref[k, rows, :] = x[k] - 0.5 * TIME_STEP * total[k]

    tendency_into(x_ref, after, pair, edge, xr, xl, div, lon_div, layers, position, last, finish)
    pack_halos(out_ref, next_ref, pair_ref, edge_ref, layers, position)


def second_stage_kernel(layers, after, pair, edge, state_ref, _, *refs):
    x_ref, (out_ref, xr, xl, div, lon_div) = Fields(refs[:-5]), refs[-5:]
    position, last = lax.axis_index("radial"), lax.axis_size("radial") - 1

    def finish(rows, x, total):
        for k in range(8):
            out_ref[k, rows, :] = 0.5 * state_ref[k, rows, :] + 0.5 * (x[k] - 0.5 * TIME_STEP * total[k])

    tendency_into(x_ref, after, pair, edge, xr, xl, div, lon_div, layers, position, last, finish)


def log2_of(value):
    assert value & (value - 1) == 0
    return value.bit_length() - 1


def node_row_column(nodes, columns):
    return lax.shift_right_logical(nodes, log2_of(columns)), nodes & (columns - 1)


def split(value, count):
    parts = []
    for _ in range(count):
        part = value.astype(jnp.bfloat16).astype(jnp.float32)
        parts.append(part)
        value = value - part
    return parts


def lat_pair(value):
    lane = lane_index(value.shape[0])
    above = jnp.where(lane == LANES - 1, value, pltpu.roll(value, LANES - 1, 1))
    below = jnp.where(lane == 0, value, pltpu.roll(value, 1, 1))
    return 0.5 * (above - below)


def aligned_current(b, radial, lon):
    first = lon(2) - lat_pair(b[1])
    second = lat_pair(b[0]) - radial(2)
    third = radial(1) - lon(0)
    aligned = first * b[0] + second * b[1] + third * b[2]
    field_sq = b[0] * b[0] + b[1] * b[1] + b[2] * b[2]
    return CELL_AREA * aligned * lax.rsqrt(1.0 + field_sq)


class Scatter:
    def __init__(self, width, columns):
        self.width, self.columns = width, columns
        self.first_column = lax.axis_index("shell") * width
        self.groups = max(16, width)
        self.group_rows = row_index(self.groups)
        self.slot_rows = row_index(LANES)
        self.total = jnp.zeros((PARTS * self.groups, LANES), jnp.float32)

    def add(self, values, nodes, lines):
        row, column = node_row_column(nodes, self.columns)
        slot = row * self.width + (column - self.first_column)
        group, place = lax.shift_right_logical(slot, 7), slot & (LANES - 1)
        parts = split(values, PARTS)
        lefts, rights = [], []
        for l in lines:
            here = self.group_rows == group[l : l + 1, :]
            lefts.append(
                jnp.concatenate([jnp.where(here, part[l : l + 1, :], 0.0) for part in parts], axis=0)
            )
            rights.append(jnp.where(self.slot_rows == place[l : l + 1, :], 1.0, 0.0))
        left = jnp.concatenate(lefts, axis=1).astype(jnp.bfloat16)
        right = jnp.concatenate(rights, axis=1).astype(jnp.bfloat16)
        self.total = self.total + lax.dot_general(
            left, right, (((1,), (1,)), ((), ())), preferred_element_type=jnp.float32
        )

    def sums(self):
        sums = self.total[: self.groups]
        for part in range(1, PARTS):
            sums = sums + self.total[part * self.groups : (part + 1) * self.groups]
        return sums


def inner_current_kernel(layers, width, columns, x_ref, edge, nodes_ref, _, out_ref):
    position, last = lax.axis_index("radial"), lax.axis_size("radial") - 1
    scatter = Scatter(width, columns)
    rows = lambda r: slice(r * SUB, (r + 1) * SUB)
    for r in range(layers):
        b = [x_ref[4 + k, rows(r)] for k in range(3)]

        def radial(k):
            if r == 0:
                below = jnp.where(position == 0, b[k], edge[4 + k, rows(1)])
            else:
                below = x_ref[4 + k, rows(r - 1)]
            if r == layers - 1:
                above = jnp.where(position == last, b[k], edge[4 + k, rows(0)])
            else:
                above = x_ref[4 + k, rows(r + 1)]
            return 0.5 * (above - below)

        def lon(k):
            return 0.5 * (pltpu.roll(b[k], SUB - 1, 0) - pltpu.roll(b[k], 1, 0))

        scatter.add(aligned_current(b, radial, lon), nodes_ref[rows(r)], range(1, SUB - 1))
    out_ref[...] = scatter.sums()


def outer_current_kernel(
    layers, width, columns, window, x_ref, after, pair, edge, nodes_ref, inner_ref, _, out_ref, held
):
    position, last = lax.axis_index("radial"), lax.axis_size("radial") - 1
    from_below = parity() == 1
    scatter = Scatter(width, columns)
    layer = row_index(layers)
    for l in (0, SUB - 1):
        line = lambda k, l: x_ref[4 + k, pl.ds(l, layers, stride=SUB), :]
        b = [line(k, l) for k in range(3)]

        def radial(k):
            first = jnp.where(position == 0, b[k][:1], edge[4 + k, SUB + l : SUB + l + 1])
            final = jnp.where(position == last, b[k][layers - 1 :], edge[4 + k, l : l + 1])
            below = jnp.where(layer == 0, first, pltpu.roll(b[k], 1, 0))
            above = jnp.where(layer == layers - 1, final, pltpu.roll(b[k], layers - 1, 0))
            return 0.5 * (above - below)

        def lon(k):
            if l == 0:
                return 0.5 * (line(k, 1) - jnp.where(from_below, pair[4 + k, 1], after[4 + k, 1]))
            return 0.5 * (jnp.where(from_below, after[4 + k, 0], pair[4 + k, 0]) - line(k, l - 1))

        values = aligned_current(b, radial, lon)
        nodes = nodes_ref[pl.ds(l, layers, stride=SUB), :]
        for r in range(0, layers, SUB):
            scatter.add(values[r : r + SUB], nodes[r : r + SUB], range(SUB))
    sums = inner_ref[...] + scatter.sums()
    groups = scatter.groups
    if not window:
        out_ref[...] = sums[: out_ref.shape[0]]
        return
    held[...] = jnp.zeros_like(held)
    held[SUB : SUB + groups] = sums
    out_ref[...] = jnp.zeros_like(out_ref)
    for twin in range(2):
        for j in range(3):
            out_ref[pl.ds(twin * 4 + j, groups, stride=8), :] = held[SUB - 1 + j : SUB - 1 + j + groups]


def rim_kernel(blocks_ref, conductance_ref, _, pair_ref, next_ref):
    size = blocks_ref.shape[1]
    high = blocks_ref.shape[0] - HALO
    odd = parity()
    for ref, first in ((pair_ref, jnp.where(odd == 1, 0, high)), (next_ref, jnp.where(odd == 1, high, 0))):
        for e in range(HALO):
            ref[e, :size] = blocks_ref[first + e]
            ref[e, size:] = jnp.zeros((SUB, size), jnp.float32)
            for way in range(4):
                ref[e, size + way : size + way + 1] = conductance_ref[way, pl.ds(first + e, 1)]


def swap_blocks(tile, piece):
    sub = row_index(SUB)
    block = lax.shift_right_logical(lane_index(SUB), log2_of(piece))
    for bit in (1, 2, 4):
        up, across = (sub & bit) != 0, (block & bit) != 0
        from_below = pltpu.roll(pltpu.roll(tile, SUB - bit, 0), bit * piece, 1)
        from_above = pltpu.roll(pltpu.roll(tile, bit, 0), LANES - bit * piece, 1)
        tile = jnp.where(up == across, tile, jnp.where(up, from_above, from_below))
    return tile


def sweep_kernel(
    width,
    arrived,
    own_blocks,
    own_conductance,
    own_pair,
    own_next,
    twin_blocks,
    twin_conductance,
    twin_pair,
    twin_next,
    _,
    out_ref,
    send_ref,
    pot,
    rhs_ref,
    cond,
):
    position = lax.axis_index("radial")
    size = LANES
    span = 3 * SUB
    base = SUB
    halves = []
    for h in range(2):
        tiles = []
        for g in range(3):
            both = [arrived[pl.ds(h * 64 + r * 4 + g, SUB, stride=8), :] for r in range(2)]
            tiles.append(swap_blocks(both[0] + both[1], width))
        halves.append(jnp.concatenate(tiles, axis=0))
    own_currents = jnp.where(position == 0, halves[0], halves[1])
    twin_currents = jnp.where(position == 0, halves[1], halves[0])
    currents = [own_currents, twin_currents]

    cond[...] = jnp.zeros_like(cond)
    odd = parity()
    rims = ((own_pair, twin_pair, odd == 1), (own_next, twin_next, odd == 0))

    def rim_rows(side, reach):
        for own, twin, is_low in rims:
            for i in range(reach):
                row = jnp.where(is_low, HALO - reach + i, i)
                yield (own, twin)[side], row, jnp.where(is_low, SUB - reach + i, 2 * SUB + i)

    for side, mid in enumerate((own_conductance, twin_conductance)):
        for way in range(4):
            cond[side, way, SUB : 2 * SUB] = mid[way]
    for side in range(2):
        for rim, row, place in rim_rows(side, HALO - side):
            for way in range(4):
                cond[side, way, pl.ds(place, 1)] = rim[row, size + way : size + way + 1]
    pot[...] = jnp.zeros_like(pot)
    eye = row_index(size, size) == lane_index(size, size)
    ones = jnp.ones((SUM_PARTS * size, size), jnp.bfloat16)
    turn = [0]

    def solve_row(side, matrix, row):
        product = matrix * rhs_ref[side, pl.ds(row, 1)]
        turn[0] += 1
        if turn[0] % MXU_EVERY == 0:
            parts = jnp.concatenate(split(product, SUM_PARTS), axis=1).astype(jnp.bfloat16)
            column = jnp.dot(parts, ones, preferred_element_type=jnp.float32)
        else:
            column = jnp.sum(product, axis=1, keepdims=True)
        line = jnp.sum(jnp.where(eye, column, 0.0), axis=0, keepdims=True)
        pot[side, pl.ds(base + row, 1)] = line

    lane = lane_index(span)
    for sweep in range(ITERS_I):
        reach = ITERS_I - 1 - sweep
        sides = (0, 1) if reach else (0,)
        if sweep == 0:
            rhs = currents
        else:
            mid = [pot[side, base : base + span] for side in range(2)]
            west = [pltpu.roll(mid[side], 1, 1) for side in range(2)]
            east = [pltpu.roll(mid[side], LANES - 1, 1) for side in range(2)]
            rhs = []
            for side in sides:
                is_right = position == (1 - side)
                west_edge = jnp.where(is_right, west[1 - side], 0.0)
                east_edge = jnp.where(is_right, 0.0, east[1 - side])
                coupled = currents[side] + cond[side, 0] * pot[side, base - 1 : base - 1 + span]
                coupled = coupled + cond[side, 1] * pot[side, base + 1 : base + 1 + span]
                coupled = coupled + cond[side, 2] * jnp.where(lane == 0, west_edge, west[side])
                coupled = coupled + cond[side, 3] * jnp.where(lane == LANES - 1, east_edge, east[side])
                rhs.append(coupled)
        for side in sides:
            rhs_ref[side] = rhs[side]
        for side in sides:
            for rim, row, place in rim_rows(side, reach - side):
                solve_row(side, rim[row, :size], place)
        for side in sides:
            for e in range(SUB):
                solve_row(side, (own_blocks, twin_blocks)[side][e], SUB + e)
    result = pot[0, base + SUB : base + 2 * SUB]
    out_ref[...] = result
    packed = swap_blocks(result, width)
    send_ref[...] = jnp.zeros_like(send_ref)
    for twin in range(2):
        send_ref[pl.ds(position * 2 * SUB + twin, SUB, stride=2), :] = packed


def gather_kernel(width, columns, direct, table_ref, nodes_ref, out_ref):
    first_column = lax.axis_index("shell") * width
    if direct:
        table = table_ref[...]
    else:
        half = lax.shift_right_logical(first_column, 7)
        table = table_ref[pl.ds(half, table_ref.shape[0] // 2, stride=2), :]
    lines = [jnp.broadcast_to(table[c : c + 1, :], (SUB, LANES)) for c in range(table.shape[0])]
    for r in range(nodes_ref.shape[0] // SUB):
        rows = slice(r * SUB, (r + 1) * SUB)
        row, column = node_row_column(nodes_ref[rows], columns)
        slot = row * width + (column - first_column)
        group, place = lax.shift_right_logical(slot, 7), slot & (LANES - 1)
        value = jnp.zeros((SUB, LANES), jnp.float32)
        for c, line in enumerate(lines):
            value = jnp.where(group == c, jnp.take_along_axis(line, place, axis=1), value)
        out_ref[rows] = value


def ring(axis, step, periodic):
    count = lax.axis_size(axis)
    pairs = [(i, i + step) for i in range(count)]
    if periodic:
        return [(i, j % count) for i, j in pairs]
    return [(i, j) for i, j in pairs if 0 <= j < count]


def pairs(first, periodic):
    count = lax.axis_size("shell")
    assert count % 2 == 0
    out = []
    for i in range(first, count, 2):
        if i + 1 < count or periodic:
            j = (i + 1) % count
            out += [(i, j), (j, i)]
    return out


def exchange_halos(after, pair, edge):
    return (
        lax.ppermute(after, "shell", pairs(1, True)),
        lax.ppermute(pair, "shell", pairs(0, True)),
        lax.ppermute(edge, "radial", [(0, 1), (1, 0)]),
    )


def padded_2(block, sides, width):
    for axis, dim in sides:
        low = lax.ppermute(
            lax.slice_in_dim(block, block.shape[dim] - width, None, axis=dim), axis, ring(axis, 1, False)
        )
        high = lax.ppermute(lax.slice_in_dim(block, 0, width, axis=dim), axis, ring(axis, -1, False))
        block = jnp.concatenate([low, block, high], axis=dim)
    return block


def general_solve(partial, conductance, blocks, rows_total, width):
    row_partials = lax.all_to_all(
        partial.reshape(rows_total, width), "shell", split_axis=0, concat_axis=1, tiled=True
    )
    currents = lax.psum_scatter(row_partials, "radial", scatter_dimension=1, tiled=True)

    def apply_blocks(vector):
        return jnp.einsum("rij,rj->ri", blocks, vector, precision=lax.Precision.HIGHEST)

    potential = apply_blocks(currents)
    for _ in range(ITERS_I - 1):
        panel = padded_2(potential, (("shell", 0), ("radial", 1)), 1)
        coupled = currents + conductance[0] * panel[:-2, 1:-1]
        coupled = coupled + conductance[1] * panel[2:, 1:-1]
        coupled = coupled + conductance[2] * panel[1:-1, :-2]
        coupled = coupled + conductance[3] * panel[1:-1, 2:]
        potential = apply_blocks(coupled)
    full_rows = lax.all_gather(potential, "radial", axis=1, tiled=True)
    strip = lax.all_to_all(full_rows, "shell", split_axis=1, concat_axis=0, tiled=True)
    return potential, strip.reshape(width, LANES)


def body(state, footpoints, conductance, inverse_blocks):
    fields, layers, lons, lats = state.shape
    shells, radials = lax.axis_size("shell"), lax.axis_size("radial")
    assert (fields, lons, lats, radials) == (8, SUB, LANES, 2)
    cells = layers * SUB
    own_rows, half = conductance.shape[1:]
    assert half == LANES
    rows_total, columns = own_rows * shells, half * radials
    width = columns // shells
    x = state.reshape(fields, cells, lats)
    nodes = footpoints.reshape(cells, lats)
    blocks = inverse_blocks[:, 0]
    fast = own_rows == SUB and width * SUB == LANES

    halo_shapes = [shape_of(8, 2, layers, lats), shape_of(8, 2, layers, lats), shape_of(8, 2 * SUB, lats)]
    stage_scratch = [
        pltpu.VMEM((8, cells + 4 * SUB, lats), jnp.float32),
        pltpu.VMEM((8, (SUB + 4) * layers, lats), jnp.float32),
        pltpu.VMEM((8, cells, lats), jnp.float32),
        pltpu.VMEM((8, cells, lats), jnp.float32),
    ]
    packed = call(functools.partial(pack_kernel, layers), halo_shapes, "pack")(x)
    halos = exchange_halos(*packed)

    if fast:
        rim_shape = shape_of(HALO, half + SUB, half)
        rim_pair, rim_next = call(
            rim_kernel,
            [rim_shape, rim_shape],
            "rim",
            in_specs=[IN_VMEM, IN_VMEM, UNREAD],
        )(blocks, conductance, packed[2])
        rims = [
            lax.ppermute(rim_pair, "shell", pairs(0, False)),
            lax.ppermute(rim_next, "shell", pairs(1, False)),
        ]

    send_shape = shape_of(shells * radials * 4, LANES) if fast else shape_of(width, LANES)
    groups = max(16, width)
    inner = call(
        functools.partial(inner_current_kernel, layers, width, columns), shape_of(groups, LANES), "inner_currents",
        in_specs=[IN_VMEM] * 3 + [UNREAD],
    )(x, halos[2], nodes, blocks)
    sums = call(
        functools.partial(outer_current_kernel, layers, width, columns, fast),
        send_shape,
        "outer_currents",
        flops=CURRENTS,
        scratch=[pltpu.VMEM((groups + 2 * SUB, LANES), jnp.float32)],
        in_specs=[IN_VMEM] * 6 + [UNREAD],
    )(x, *halos, nodes, inner, blocks)

    *section_one, after, pair, edge = call(
        functools.partial(first_stage_kernel, layers),
        [shape_of(fields // SPLIT, cells, lats)] * SPLIT + halo_shapes,
        "first_stage",
        flops=DEAR,
        scratch=stage_scratch,
        in_specs=[IN_VMEM] * 4 + [UNREAD],
    )(x, *halos, sums)
    second_halos = exchange_halos(after, pair, edge)
    later = sums

    if fast:
        rims = call(
            relay_kernel,
            [rim_shape] * 2,
            "relay",
            flops=RELAY,
            in_specs=[UNREAD] * 3,
            out_specs=[UNREAD] * 2,
            input_output_aliases={0: 0, 1: 1},
        )(*rims, sums)
        twin = [(0, 1), (1, 0)]
        twin_parts = [lax.ppermute(v, "radial", twin) for v in (blocks, conductance, *rims)]
        arrived = lax.all_to_all(sums, ("shell", "radial"), split_axis=0, concat_axis=0, tiled=True)
        potential, spread = call(
            functools.partial(sweep_kernel, width),
            [shape_of(own_rows, half), shape_of(shells * radials, half)],
            "sweeps",
            scratch=[
                pltpu.VMEM((2, 5 * SUB, half), jnp.float32),
                pltpu.VMEM((2, 3 * SUB, half), jnp.float32),
                pltpu.VMEM((2, 4, 3 * SUB, half), jnp.float32),
            ],
            flops=DEAR,
            in_specs=[IN_VMEM] * 9 + [UNREAD],
        )(arrived, blocks, conductance, *rims, *twin_parts, edge)
        later = spread
        table = lax.all_to_all(spread, ("shell", "radial"), split_axis=0, concat_axis=0, tiled=True)
    else:
        potential, table = general_solve(sums, conductance, blocks, rows_total, width)

    state_next = call(
        functools.partial(second_stage_kernel, layers),
        shape_of(fields, cells, lats),
        "second_stage",
        flops=DEAR,
        scratch=stage_scratch,
        in_specs=[IN_VMEM] * 4 + [UNREAD] + [IN_VMEM] * SPLIT,
    )(*second_halos, x, later, *section_one)

    footpoint_potential = call(
        functools.partial(gather_kernel, width, columns, not fast), shape_of(cells, lats), "gather"
    )(table, nodes)
    return (
        state_next.reshape(state.shape),
        potential,
        footpoint_potential.reshape(footpoints.shape),
    )


def solution(mesh):
    return jax.shard_map(
        body,
        mesh=mesh,
        in_specs=(
            P(None, "radial", "shell", None),
            P("radial", "shell", None),
            P(None, "shell", "radial"),
            P("shell", "radial", None, None),
        ),
        out_specs=(
            P(None, "radial", "shell", None),
            P("shell", "radial"),
            P("radial", "shell", None),
        ),
        check_vma=False,
    )
```
